128 devices in a mesh: dp: 16 (over y_hi, z, core), ctx: 8 (over y_lo, x).
Axes of the slice: x: 4, y: 4 (y_hi: 2, y_lo: 2; y = y_hi * 2 + y_lo), z: 4, core: 2. Of those that a mesh axis runs over, the one named last changes fastest.
Arguments:
- token_ids: int32 [16, 1024], P('dp', 'ctx'), may hold values from 0 to 511
- embedding: bfloat16 [512, 4096], replicated, may hold values from -6 to 6
- short_filter: float32 [3, 3, 4096], replicated, may hold values from -3 to 3
- long_filter: bfloat16 [1024, 4096], P('dp', 'ctx'), may hold values from -1.3 to 1.3
- cotangent: bfloat16 [16, 1024, 4096], P('dp', 'ctx'), may hold values from -1.5 to 1.5
Outputs:
- mixed: bfloat16 [16, 1024, 4096], P('dp', 'ctx')
- grad_embedding: float32 [512, 4096], P('dp', 'ctx')
- grad_filter: float32 [1024, 4096], P('dp', 'ctx')
The draws below stay inside these ranges and needn't reach their ends.
All inputs are finite; a program needn't handle non-finite values.
Results may differ from the reference program's by a relative error of at most 0.02.
Values may be sent and summed in bfloat16 or wider, within the bound.
A program may use at most 128 MiB of HBM per device.

```python
import math
import jax
import jax.numpy as jnp
from jax import lax

D = 4096
VOCAB = 512
TAPS = 3
SEQLEN = 1024
SEQS = 16


def draw_long_filter(key, part):
    key = jax.random.fold_in(key, 7)
    rate_key, tap_key = jax.random.split(key)
    rates = jnp.exp(jax.random.uniform(rate_key, (D,), jnp.float32, math.log(0.3 / SEQLEN), math.log(1.0 / 20.0)))
    position = jnp.arange(SEQLEN, dtype=jnp.float32)
    envelope = jnp.exp(-position[:, None] * rates[None, :])
    spread = jnp.sqrt(jnp.maximum(2.0 * rates, 1.0 / SEQLEN))
    taps = jax.random.truncated_normal(tap_key, -4.0, 4.0, (SEQLEN, D), jnp.float32)
    return (taps * envelope * spread[None, :]).astype(jnp.bfloat16)


def with_ends(values, rng, low, high):
    place = [jax.random.randint(jax.random.fold_in(rng, axis), (), 0, length) for axis, length in enumerate(values.shape)]
    longest = values.shape.index(max(values.shape))
    neighbour = place[:longest] + [(place[longest] + 1) % values.shape[longest]] + place[longest + 1:]
    return values.at[tuple(place)].set(low).at[tuple(neighbour)].set(high)


def block_levels(rng, shape, cuts, low, top_value):
    loudness = 1.0
    for dim, parts in cuts:
        steps = jax.random.uniform(jax.random.fold_in(jax.random.fold_in(rng, 6), dim), (parts,), jnp.float32, low / len(cuts), top_value / len(cuts))
        loudness = loudness * jnp.repeat(jnp.exp(steps), shape[dim] // parts).reshape((-1,) + (1,) * (len(shape) - 1 - dim))
    return loudness


def normal_values(stream_key, shape, scale, bound, cuts=(), kind=jnp.bfloat16):
    values = jax.random.normal(stream_key, shape, jnp.float32) * scale
    if len(cuts) > 0:
        values = block_levels(stream_key, shape, cuts, -0.22, 0.18) * values
    return jnp.clip(values, min=-bound, max=bound).astype(kind)


def setup_inputs(seed: int = 0) -> dict:
    keys = jax.random.split(jax.random.key(seed), 6)
    token_ids = with_ends(jax.random.randint(keys[0], (SEQS, SEQLEN), 0, VOCAB), jax.random.fold_in(keys[0], 1), 0, VOCAB - 1).astype(jnp.int32)
    embedding = normal_values(keys[1], (VOCAB, D), 1.0, 6.0)
    short_filter = normal_values(keys[2], (3, TAPS, D), 0.5, 3.0, (), jnp.float32)
    long_filter = draw_long_filter(jax.random.fold_in(keys[5], 71), 0)
    cotangent = normal_values(keys[4], (SEQS, SEQLEN, D), 0.25, 1.5, ((0, 16), (1, 8)))
    return {"token_ids": token_ids, "embedding": embedding, "short_filter": short_filter, "long_filter": long_filter, "cotangent": cotangent}


highest = lax.Precision.HIGHEST

def delayed(field, steps):
    front = jnp.zeros_like(field[:steps])
    return jnp.concatenate([front, field[:-steps]], 0)

def advanced(field, steps):
    back = jnp.zeros_like(field[:steps])
    return jnp.concatenate([field[steps:], back], 0)

def split_length(total):
    first = math.isqrt(total)
    while total % first:
        first = first - 1
    return (first, total // first)

def square_table(count):
    index = jnp.arange(count, dtype=jnp.int32)
    angle = (index[:, None] * index[None, :] % count).astype(jnp.float32) * (2.0 * math.pi / count)
    return (jnp.cos(angle).astype(jnp.bfloat16), jnp.sin(angle).astype(jnp.bfloat16))

def make_tables(total):
    first, second = split_length(total)
    cos_p, sin_p = square_table(first)
    cos_q, sin_q = square_table(second)
    rows_idx = jnp.arange(first, dtype=jnp.int32)
    cols_idx = jnp.arange(second, dtype=jnp.int32)
    angle = (rows_idx[:, None] * cols_idx[None, :] % total).astype(jnp.float32) * (2.0 * math.pi / total)
    return (cos_p, sin_p, cos_q, sin_q, jnp.cos(angle)[:, :, None], jnp.sin(angle)[:, :, None])

def dot_full(table, field):
    return jnp.dot(table.astype(jnp.float32), field.astype(jnp.float32), precision=highest)

def mix(table, field, form):
    return jnp.einsum(form, table.astype(jnp.float32), field.astype(jnp.float32), precision=highest)

def forward_dft(signal, tables):
    cos_p, sin_p, cos_q, sin_q, tw_cos, tw_sin = tables
    first = cos_p.shape[0]
    second = cos_q.shape[0]
    width = signal.shape[1]
    flat = signal.reshape(first, second * width)
    a_re = dot_full(cos_p, flat).reshape(first, second, width)
    a_im = -dot_full(sin_p, flat).reshape(first, second, width)
    b_re = (a_re * tw_cos + a_im * tw_sin).astype(jnp.bfloat16)
    b_im = (a_im * tw_cos - a_re * tw_sin).astype(jnp.bfloat16)
    form = 'kn,anc->akc'
    x_re = mix(cos_q, b_re, form) + mix(sin_q, b_im, form)
    x_im = mix(cos_q, b_im, form) - mix(sin_q, b_re, form)
    return (x_re, x_im)

def inverse_dft(x_re, x_im, tables):
    cos_p, sin_p, cos_q, sin_q, tw_cos, tw_sin = tables
    first, second, width = x_re.shape
    form = 'nk,akc->anc'
    b_re = mix(cos_q, x_re, form) - mix(sin_q, x_im, form)
    b_im = mix(cos_q, x_im, form) + mix(sin_q, x_re, form)
    c_re = (b_re * tw_cos - b_im * tw_sin).astype(jnp.bfloat16).reshape(first, second * width)
    c_im = (b_im * tw_cos + b_re * tw_sin).astype(jnp.bfloat16).reshape(first, second * width)
    result = dot_full(cos_p, c_re) - dot_full(sin_p, c_im)
    return result.reshape(first * second, width) / (first * second)

def padded_dft(field, tables):
    grown = jnp.concatenate([field, jnp.zeros_like(field)], 0)
    return forward_dft(grown, tables)

def reference(token_ids, embedding, short_filter, long_filter, cotangent):
    length = token_ids.shape[1]
    tables = make_tables(2 * length)
    h_re, h_im = padded_dft(long_filter, tables)

    def one_sequence(pair):
        ids_row, grad_out = pair
        x_rows = embedding[ids_row].astype(jnp.float32)
        once = delayed(x_rows, 1)
        twice = delayed(x_rows, 2)
        branches = [short_filter[r, 0] * x_rows + short_filter[r, 1] * once + short_filter[r, 2] * twice for r in range(3)]
        u_q, u_k, u_v = branches
        z_rows = (u_k * u_v).astype(jnp.bfloat16)
        z_re, z_im = padded_dft(z_rows, tables)
        p_re = (z_re * h_re - z_im * h_im).astype(jnp.bfloat16)
        p_im = (z_re * h_im + z_im * h_re).astype(jnp.bfloat16)
        conv = inverse_dft(p_re, p_im, tables)[:length].astype(jnp.bfloat16)
        mixed = (u_q * conv.astype(jnp.float32)).astype(jnp.bfloat16)
        grad_f = grad_out.astype(jnp.float32)
        g_conv = (grad_f * u_q).astype(jnp.bfloat16)
        g_q = grad_f * conv.astype(jnp.float32)
        g_re, g_im = padded_dft(g_conv, tables)
        q_re = (g_re * h_re + g_im * h_im).astype(jnp.bfloat16)
        q_im = (g_im * h_re - g_re * h_im).astype(jnp.bfloat16)
        g_z = inverse_dft(q_re, q_im, tables)[:length].astype(jnp.bfloat16)
        f_re = (g_re * z_re + g_im * z_im).astype(jnp.bfloat16)
        f_im = (g_im * z_re - g_re * z_im).astype(jnp.bfloat16)
        g_filter = inverse_dft(f_re, f_im, tables)[:length]
        g_k = g_z.astype(jnp.float32) * u_v
        g_v = g_z.astype(jnp.float32) * u_k
        g_x = jnp.zeros_like(x_rows)
        for r, g_r in enumerate((g_q, g_k, g_v)):
            g_x = g_x + short_filter[r, 0] * g_r + short_filter[r, 1] * advanced(g_r, 1) + short_filter[r, 2] * advanced(g_r, 2)
        g_x = g_x.astype(jnp.bfloat16)
        table = jax.ops.segment_sum(g_x.astype(jnp.float32), ids_row, num_segments=VOCAB)
        return (mixed, table, g_filter)
    mixed, tables_out, filters = lax.map(one_sequence, (token_ids, cotangent))
    return (mixed, lax.optimization_barrier(jnp.sum(tables_out, axis=0)), lax.optimization_barrier(jnp.sum(filters, axis=0)))
```

```python
import math

import jax
import jax.numpy as jnp
import numpy as np
from jax import lax
from jax.sharding import PartitionSpec as P

BF = jnp.bfloat16
F32 = jnp.float32


def tables(length):
    sub = length // 4
    k = np.arange(sub)[None, :, None]
    t = 4 * np.arange(sub)[None, None, :] + np.arange(4)[:, None, None]
    angle = 2.0 * math.pi * (((4 * k + 1) * t) % (4 * length)) / (4 * length)
    fwd = np.concatenate([np.cos(angle), -np.sin(angle)], 1)
    inv = fwd.transpose(0, 2, 1) / length
    return jnp.asarray(fwd, BF), jnp.asarray(inv, BF)


def forward(field, table):
    half = table.shape[1] // 2
    p = jnp.einsum("jkn,jnc->jkc", table, field, preferred_element_type=F32)
    re, im = p[:, :half], p[:, half:]
    a_re, a_im, b_re, b_im = re[0] + re[2], im[0] + im[2], re[0] - re[2], im[0] - im[2]
    c_re, c_im, d_re, d_im = re[1] + re[3], im[1] + im[3], re[1] - re[3], im[1] - im[3]
    return (
        jnp.stack([a_re + c_re, b_re + d_im, a_re - c_re, b_re - d_im]),
        jnp.stack([a_im + c_im, b_im - d_re, a_im - c_im, b_im + d_re]),
    )


def inverse(re, im, table):
    a_re, a_im, b_re, b_im = re[0] + re[2], im[0] + im[2], re[0] - re[2], im[0] - im[2]
    c_re, c_im, d_re, d_im = re[1] + re[3], im[1] + im[3], re[1] - re[3], im[1] - im[3]
    w_re = jnp.stack([a_re + c_re, b_re - d_im, a_re - c_re, b_re + d_im])
    w_im = jnp.stack([a_im + c_im, b_im + d_re, a_im - c_im, b_im - d_re])
    w = jnp.concatenate([w_re, w_im], 1).astype(BF)
    return jnp.einsum("jnk,jkc->jnc", table, w, preferred_element_type=F32)


def split4(rows):
    return rows.reshape(rows.shape[0] // 4, 4, rows.shape[1]).transpose(1, 0, 2)


def join4(parts):
    return parts.transpose(1, 0, 2).reshape(parts.shape[0] * parts.shape[1], parts.shape[2])


def body(token_ids, embedding, short_filter, long_filter, cotangent):
    vocab, width = embedding.shape
    ctx, dp = lax.axis_size("ctx"), lax.axis_size("dp")
    part = width // ctx
    length = token_ids.shape[1] * ctx
    mine = lax.axis_index("ctx") * part
    fwd, inv = tables(length)
    ids = lax.all_gather(token_ids[0], "ctx", axis=0, tiled=True)
    ids = ids.reshape(length // 4, 4).T
    emb = lax.dynamic_slice(embedding, (0, mine), (vocab, part))
    taps = lax.dynamic_slice(short_filter, (0, 0, mine), (3, 3, part))
    onehot = (ids[:, :, None] == jnp.arange(vocab, dtype=jnp.int32)).astype(BF)
    x = jnp.einsum("jnv,vc->jnc", onehot, emb, preferred_element_type=F32)

    cot = lax.all_to_all(split4(cotangent[0]), "ctx", split_axis=2, concat_axis=1, tiled=True).astype(F32)
    full = split4(lax.all_gather(long_filter, "dp", axis=0, tiled=True))

    late = jnp.concatenate([jnp.zeros_like(x[:, :1]), x[:, :-1]], 1)
    once = jnp.stack([late[3], x[0], x[1], x[2]])
    twice = jnp.stack([late[2], late[3], x[0], x[1]])
    u_q, u_k, u_v = [taps[r, 0] * x + taps[r, 1] * once + taps[r, 2] * twice for r in range(3)]
    z = (u_k * u_v).astype(BF)
    z_re, z_im = forward(z, fwd)
    h_re, h_im = forward(full, fwd)
    conv = inverse(z_re * h_re - z_im * h_im, z_re * h_im + z_im * h_re, inv).astype(BF).astype(F32)
    mixed = (u_q * conv).astype(BF)
    mixed = join4(lax.all_to_all(mixed, "ctx", split_axis=1, concat_axis=2, tiled=True))

    g_conv = (cot * u_q).astype(BF)
    g_q = cot * conv
    g_re, g_im = forward(g_conv, fwd)
    g_z = inverse(g_re * h_re + g_im * h_im, g_im * h_re - g_re * h_im, inv).astype(BF).astype(F32)
    term = inverse(g_re * z_re + g_im * z_im, g_im * z_re - g_re * z_im, inv).astype(BF)
    term = term.reshape(4, dp, length // 4 // dp, part).transpose(1, 0, 2, 3)
    term = lax.all_to_all(term, "dp", split_axis=0, concat_axis=0, tiled=True)
    grad_filter = join4(jnp.sum(term.astype(F32), 0))

    g_x = jnp.zeros_like(x)
    for r, g_r in enumerate((g_q, g_z * u_v, g_z * u_k)):
        early = jnp.concatenate([g_r[:, 1:], jnp.zeros_like(g_r[:, :1])], 1)
        once = jnp.stack([g_r[1], g_r[2], g_r[3], early[0]])
        twice = jnp.stack([g_r[2], g_r[3], early[0], early[1]])
        g_x = g_x + taps[r, 0] * g_r + taps[r, 1] * once + taps[r, 2] * twice
    g_x = g_x.astype(BF)
    table = jnp.einsum("jnv,jnc->vc", onehot, g_x, preferred_element_type=F32).astype(BF)
    table = lax.all_to_all(table.reshape(dp, vocab // dp, part), "dp", split_axis=0, concat_axis=0, tiled=True)
    grad_embedding = jnp.sum(table.astype(F32), 0)
    return (mixed[None], grad_embedding, grad_filter)


def solution(mesh):
    in_specs = (P("dp", "ctx"), P(), P(), P("dp", "ctx"), P("dp", "ctx", None))
    out_specs = (P("dp", "ctx", None), P("dp", "ctx"), P("dp", "ctx"))
    return jax.shard_map(body, mesh=mesh, in_specs=in_specs, out_specs=out_specs, check_vma=False)
```

```python
import functools
import math

import jax
import jax.numpy as jnp
import numpy as np
from jax import lax
from jax.experimental import pallas as pl
from jax.experimental.pallas import tpu as pltpu
from jax.sharding import PartitionSpec as P

BF = jnp.bfloat16
F32 = jnp.float32
MESH = pl.DeviceIdType.MESH
LANES = 128
KC = 16


def tables(length, block):
    sub = length // 4
    k = np.arange(sub)[None, :, None]
    t = 4 * np.arange(sub)[None, None, :] + np.arange(4)[:, None, None]
    angle = 2.0 * math.pi * (((4 * k + 1) * t) % (4 * length)) / (4 * length)
    fwd = np.concatenate([np.cos(angle), -np.sin(angle)], 1)
    inv = fwd.transpose(0, 2, 1) / length
    out = np.arange(block)
    perm = np.zeros((2, block, block))
    perm[0, out, 4 * (out % (block // 4)) + out // (block // 4)] = 1.0
    perm[1] = perm[0].T
    return jnp.asarray(fwd, BF), jnp.asarray(inv, BF), jnp.asarray(perm, BF)


def radix4(re, im, sign):
    a_re, a_im, b_re, b_im = re[0] + re[2], im[0] + im[2], re[0] - re[2], im[0] - im[2]
    c_re, c_im, d_re, d_im = re[1] + re[3], im[1] + im[3], re[1] - re[3], im[1] - im[3]
    if sign > 0:
        d_re, d_im = -d_re, -d_im
    return (
        [a_re + c_re, b_re + d_im, a_re - c_re, b_re - d_im],
        [a_im + c_im, b_im - d_re, a_im - c_im, b_im + d_re],
    )


def loop(count, step):
    def run(i, carry):
        step(i)
        return carry

    lax.fori_loop(0, count, run, 0)


def dot(a, b):
    return jnp.dot(a, b, preferred_element_type=F32)


def kernel(
    dims,
    ids_ref, perm, emb_hbm, taps_hbm, lf_hbm, cot_hbm, fwd_hbm, inv_hbm,
    mixed_hbm, ge_ref, gf_ref,
    ids_in, emb, taps, lf_in, cot_in, fwd, inv,
    x, uq, uk, uv, field, hfield, spec_h, spec_z, pbuf, wbuf, wf, conv, gq, gx,
    mixed_out, gf_out, gf_in, ge_acc, ge_out, ge_in,
    local_sem, ids_send, ids_recv, lf_send, lf_recv, cot_send, cot_recv,
    mix_send, mix_recv, gf_send, gf_recv, ge_send, ge_recv,
):
    dp_n, ctx_n, vocab, part, block = dims
    cw = part // 2
    sub = ctx_n * block // 4
    bs = block // 4
    pair_n = 2 * ctx_n
    per = dp_n // ctx_n
    lr = block // per
    vr = vocab // dp_n
    dp = lax.axis_index("dp")
    p_me = lax.axis_index("ctx")
    g = lax.div(dp, 2)
    c_me = lax.rem(dp, 2)
    pair_me = c_me * ctx_n + p_me
    first = pl.multiple_of(p_me * part + c_me * cw, cw)
    halves = [pl.ds(h * LANES, LANES) for h in range(cw // LANES)]

    def chunk(i, size):
        return pl.ds(pl.multiple_of(i * size, size), size)

    loads = [
        pltpu.make_async_copy(emb_hbm.at[:, pl.ds(first, cw)], emb, local_sem.at[0]),
        pltpu.make_async_copy(taps_hbm.at[:, :, pl.ds(first, cw)], taps, local_sem.at[1]),
        pltpu.make_async_copy(fwd_hbm, fwd, local_sem.at[2]),
        pltpu.make_async_copy(inv_hbm, inv, local_sem.at[3]),
    ]
    for load in loads:
        load.start()

    barrier = pltpu.get_barrier_semaphore()

    def greet_pair(i):
        to = lax.rem(pair_me + 1 + i, pair_n)
        device = (2 * g + lax.div(to, ctx_n), lax.rem(to, ctx_n))
        pl.semaphore_signal(barrier, inc=1, device_id=device, device_id_type=MESH)

    def greet_dp(i):
        device = (lax.rem(dp + 1 + i, dp_n), p_me)
        pl.semaphore_signal(barrier, inc=1, device_id=device, device_id_type=MESH)

    loop(pair_n - 1, greet_pair)
    loop(dp_n - 1, greet_dp)
    pl.semaphore_wait(barrier, pair_n + dp_n - 2)

    def ids_copy(to):
        return pltpu.make_async_remote_copy(
            src_ref=ids_ref, dst_ref=ids_in.at[pair_me], send_sem=ids_send.at[to], recv_sem=ids_recv.at[pair_me],
            device_id=(2 * g + lax.div(to, ctx_n), lax.rem(to, ctx_n)), device_id_type=MESH,
        )

    def lf_copy(to):
        return pltpu.make_async_remote_copy(
            src_ref=lf_hbm.at[:, chunk(lax.rem(to, 2), cw)], dst_ref=lf_in.at[dp],
            send_sem=lf_send.at[to], recv_sem=lf_recv.at[dp], device_id=(to, p_me), device_id_type=MESH,
        )

    def cot_columns(to):
        return cot_hbm.at[0, :, chunk(2 * lax.rem(to, ctx_n) + lax.div(to, ctx_n), cw)]

    def cot_copy(to):
        return pltpu.make_async_remote_copy(
            src_ref=cot_columns(to), dst_ref=cot_in.at[pair_me], send_sem=cot_send.at[to], recv_sem=cot_recv.at[pair_me],
            device_id=(2 * g + lax.div(to, ctx_n), lax.rem(to, ctx_n)), device_id_type=MESH,
        )

    def mix_copy(to):
        return pltpu.make_async_remote_copy(
            src_ref=mixed_out.at[to], dst_ref=mixed_hbm.at[0, :, pl.ds(first, cw)],
            send_sem=mix_send.at[to], recv_sem=mix_recv.at[pair_me],
            device_id=(2 * g + lax.div(to, ctx_n), lax.rem(to, ctx_n)), device_id_type=MESH,
        )

    def gf_copy(to):
        return pltpu.make_async_remote_copy(
            src_ref=gf_out.at[to], dst_ref=gf_in.at[dp], send_sem=gf_send.at[to], recv_sem=gf_recv.at[dp],
            device_id=(to, p_me), device_id_type=MESH,
        )

    def ge_copy(to):
        return pltpu.make_async_remote_copy(
            src_ref=ge_out.at[chunk(to, vr)], dst_ref=ge_in.at[dp], send_sem=ge_send.at[to], recv_sem=ge_recv.at[dp],
            device_id=(to, p_me), device_id_type=MESH,
        )

    def others(count, me, step):
        loop(count - 1, lambda i: step(lax.rem(me + 1 + i, count)))

    def arrived(slot, sem):
        pltpu.make_async_copy(slot, slot, sem).wait()

    pltpu.make_async_copy(ids_ref, ids_in.at[pair_me], ids_recv.at[pair_me]).start()
    pltpu.make_async_copy(lf_hbm.at[:, chunk(c_me, cw)], lf_in.at[dp], lf_recv.at[dp]).start()
    pltpu.make_async_copy(cot_columns(pair_me), cot_in.at[pair_me], cot_recv.at[pair_me]).start()
    others(pair_n, pair_me, lambda to: ids_copy(to).start())
    others(dp_n, dp, lambda to: lf_copy(to).start())
    others(pair_n, pair_me, lambda to: cot_copy(to).start())

    loads[0].wait()
    loads[1].wait()
    vocab_lane = lax.broadcasted_iota(jnp.int32, (block, LANES), 1).astype(F32)

    def embed(i):
        s, p = lax.div(i, ctx_n), lax.rem(i, ctx_n)
        arrived(ids_in.at[i], ids_recv.at[i])
        row = ids_in[i, 0:1, :].astype(F32)
        column = jnp.transpose(jnp.broadcast_to(row, (block, block)))
        onehot = jnp.concatenate(
            [(column == vocab_lane + float(q * LANES)).astype(F32).astype(BF) for q in range(vocab // LANES)], 1
        )
        rows = dot(onehot, emb[...])
        for j in range(4):
            x[s, j, chunk(p, bs), :] = rows[j * bs : (j + 1) * bs]

    loop(pair_n, embed)

    row16 = lax.broadcasted_iota(jnp.int32, (bs, LANES), 0)
    for h in halves:
        f = [[taps[r, i : i + 1, h] for i in range(3)] for r in range(3)]

        def short(s, h=h, f=f):
            def step(p, carry):
                rows = chunk(p, bs)
                xs = [x[s, j, rows, h] for j in range(4)]
                turned = [pltpu.roll(xs[2], 1, 0), pltpu.roll(xs[3], 1, 0)]
                late = [jnp.where(row16 == 0, carry[q], turned[q]) for q in range(2)]
                line = late + xs
                us = [
                    [f[r][0] * line[j + 2] + f[r][1] * line[j + 1] + f[r][2] * line[j] for j in range(4)]
                    for r in range(3)
                ]
                for j in range(4):
                    uq[s, j, rows, h] = us[0][j]
                    uk[s, j, rows, h] = us[1][j]
                    uv[s, j, rows, h] = us[2][j]
                    field[s, j, rows, h] = (us[1][j] * us[2][j]).astype(BF)
                return tuple(turned)

            zero = jnp.zeros((bs, LANES), F32)
            lax.fori_loop(0, ctx_n, step, (zero, zero))

        loop(2, short)

    loads[2].wait()

    def gather_taps(i):
        for q in range(per):
            arrived(lf_in.at[i * per + q], lf_recv.at[i * per + q])
        rows = jnp.concatenate([lf_in[i * per + q] for q in range(per)], 0)
        rows = dot(perm[0], rows).astype(BF)
        for j in range(4):
            hfield[j, chunk(i, bs), :] = rows[j * bs : (j + 1) * bs]

    loop(ctx_n, gather_taps)

    def filter_dft(j):
        pbuf[0, j] = dot(fwd[j], hfield[j])

    loop(4, filter_dft)

    def butterfly(s, i, h):
        re = [pbuf[s, j, chunk(i, KC), h] for j in range(4)]
        im = [pbuf[s, j, pl.ds(pl.multiple_of(sub + i * KC, KC), KC), h] for j in range(4)]
        return radix4(re, im, -1)

    def filter_mix(i):
        for h in halves:
            re, im = butterfly(0, i, h)
            for m in range(4):
                spec_h[m, 0, chunk(i, KC), h] = re[m]
                spec_h[m, 1, chunk(i, KC), h] = im[m]

    loop(sub // KC, filter_mix)

    def field_dft(i):
        s, j = lax.div(i, 4), lax.rem(i, 4)
        pbuf[s, j] = dot(fwd[j], field[s, j])

    def put(ref, i, h, re, im):
        re, im = radix4(re, im, 1)
        for j in range(4):
            ref[j, chunk(i, KC), h] = re[j].astype(BF)
            ref[j, pl.ds(pl.multiple_of(sub + i * KC, KC), KC), h] = im[j].astype(BF)

    loop(8, field_dft)
    loads[3].wait()

    for s in range(2):

        def conv_mix(i, s=s):
            for h in halves:
                re, im = butterfly(s, i, h)
                out_re, out_im = [], []
                for m in range(4):
                    spec_z[s, m, 0, chunk(i, KC), h] = re[m]
                    spec_z[s, m, 1, chunk(i, KC), h] = im[m]
                    h_re, h_im = spec_h[m, 0, chunk(i, KC), h], spec_h[m, 1, chunk(i, KC), h]
                    out_re.append(re[m] * h_re - im[m] * h_im)
                    out_im.append(re[m] * h_im + im[m] * h_re)
                put(wbuf.at[s], i, h, out_re, out_im)

        loop(sub // KC, conv_mix)

        def conv_idft(j, s=s):
            conv[s, j] = dot(inv[j], wbuf[s, j]).astype(BF).astype(F32)

        loop(4, conv_idft)

        def mix(i, s=s):
            p = lax.rem(p_me + 1 + i, ctx_n)
            rows = chunk(p, bs)
            out = jnp.concatenate([(uq[s, j, rows, :] * conv[s, j, rows, :]).astype(BF) for j in range(4)], 0)
            to = s * ctx_n + p
            mixed_out[to] = dot(perm[1], out).astype(BF)

            @pl.when(to != pair_me)
            def _():
                mix_copy(to).start()

            @pl.when(to == pair_me)
            def _():
                pltpu.make_async_copy(
                    mixed_out.at[to], mixed_hbm.at[0, :, pl.ds(first, cw)], mix_recv.at[pair_me]
                ).start()

        loop(ctx_n, mix)

    def take(i):
        s, p = lax.div(i, ctx_n), lax.rem(i, ctx_n)
        arrived(cot_in.at[i], cot_recv.at[i])
        out = dot(perm[0], cot_in[i])
        rows = chunk(p, bs)
        for j in range(4):
            piece = out[j * bs : (j + 1) * bs]
            field[s, j, rows, :] = (piece * uq[s, j, rows, :]).astype(BF)
            gq[s, j, rows, :] = piece * conv[s, j, rows, :]

    loop(pair_n, take)
    loop(8, field_dft)

    def back_mix(i):
        for h in halves:
            sum_re, sum_im = None, None
            for s in range(2):
                re, im = butterfly(s, i, h)
                out_re, out_im, f_re, f_im = [], [], [], []
                for m in range(4):
                    h_re, h_im = spec_h[m, 0, chunk(i, KC), h], spec_h[m, 1, chunk(i, KC), h]
                    z_re, z_im = spec_z[s, m, 0, chunk(i, KC), h], spec_z[s, m, 1, chunk(i, KC), h]
                    out_re.append(re[m] * h_re + im[m] * h_im)
                    out_im.append(im[m] * h_re - re[m] * h_im)
                    f_re.append(re[m] * z_re + im[m] * z_im)
                    f_im.append(im[m] * z_re - re[m] * z_im)
                put(wbuf.at[s], i, h, out_re, out_im)
                if s == 0:
                    sum_re, sum_im = f_re, f_im
                else:
                    sum_re = [a + b for a, b in zip(sum_re, f_re)]
                    sum_im = [a + b for a, b in zip(sum_im, f_im)]
            put(wf, i, h, sum_re, sum_im)

    loop(sub // KC, back_mix)

    def filter_idft(j):
        hfield[j] = dot(inv[j], wf[j]).astype(BF)

    loop(4, filter_idft)

    def filter_rows(i):
        rows = jnp.concatenate([hfield[j, chunk(i, bs), :] for j in range(4)], 0)
        rows = dot(perm[1], rows).astype(BF)
        for q in range(per):
            gf_out[i * per + q] = rows[q * lr : (q + 1) * lr]

    loop(ctx_n, filter_rows)
    others(dp_n, dp, lambda to: gf_copy(to).start())
    pltpu.make_async_copy(gf_out.at[dp], gf_in.at[dp], gf_recv.at[dp]).start()

    def gz_idft(i):
        s, j = lax.div(i, 4), lax.rem(i, 4)
        conv[s, j] = dot(inv[j], wbuf[s, j])

    loop(8, gz_idft)

    for h in halves:
        f = [[taps[r, i : i + 1, h] for i in range(3)] for r in range(3)]

        def grad(s, h=h, f=f):
            def step(i, carry):
                p = ctx_n - 1 - i
                rows = chunk(p, bs)
                lines = [[], [], []]
                for j in range(4):
                    gz = conv[s, j, rows, h].astype(BF).astype(F32)
                    gs = [gq[s, j, rows, h], gz * uv[s, j, rows, h], gz * uk[s, j, rows, h]]
                    for tap in range(3):
                        lines[tap].append(f[0][tap] * gs[0] + f[1][tap] * gs[1] + f[2][tap] * gs[2])
                turned = [pltpu.roll(v, bs - 1, 0) for v in (lines[1][0], lines[2][0], lines[2][1])]
                early = [jnp.where(row16 == bs - 1, carry[q], turned[q]) for q in range(3)]
                once = lines[1][1:] + [early[0]]
                twice = lines[2][2:] + [early[1], early[2]]
                for j in range(4):
                    gx[s, p, j, :, h] = (lines[0][j] + once[j] + twice[j]).astype(BF)
                return tuple(turned)

            zero = jnp.zeros((bs, LANES), F32)
            lax.fori_loop(0, ctx_n, step, (zero, zero, zero))

        loop(2, grad)

    vocab_row = lax.broadcasted_iota(jnp.int32, (vocab, 2 * block), 0).astype(F32)
    ge_acc[...] = jnp.zeros_like(ge_acc)

    def scatter(i):
        s, p = lax.div(2 * i, ctx_n), lax.rem(2 * i, ctx_n)
        row = jnp.concatenate([ids_in[2 * i, 0:1, :], ids_in[2 * i + 1, 0:1, :]], 1).astype(F32)
        onehot = (vocab_row == row).astype(F32).astype(BF)
        rows = jnp.concatenate([gx[s, p + q, j] for q in range(2) for j in range(4)], 0)
        ge_acc[...] += dot(onehot, rows)

    loop(ctx_n, scatter)
    ge_out[...] = ge_acc[...].astype(BF)
    others(dp_n, dp, lambda to: ge_copy(to).start())
    pltpu.make_async_copy(ge_out.at[chunk(dp, vr)], ge_in.at[dp], ge_recv.at[dp]).start()

    loop(dp_n, lambda i: arrived(gf_in.at[i], gf_recv.at[i]))
    for q in range(2):
        total = gf_in[q].astype(F32)
        for i in range(1, dp_n // 2):
            total = total + gf_in[2 * i + q].astype(F32)
        gf_ref[:, q * cw : (q + 1) * cw] = total
    loop(dp_n, lambda i: arrived(ge_in.at[i], ge_recv.at[i]))
    for q in range(2):
        total = ge_in[q].astype(F32)
        for i in range(1, dp_n // 2):
            total = total + ge_in[2 * i + q].astype(F32)
        ge_ref[:, q * cw : (q + 1) * cw] = total

    def mixed_arrived(i):
        s, p = lax.div(i, ctx_n), lax.rem(i, ctx_n)
        arrived(mixed_hbm.at[0, :, chunk(2 * p + s, cw)], mix_recv.at[i])

    loop(pair_n, mixed_arrived)

    def pair_sent(to):
        ids_copy(to).wait_send()
        cot_copy(to).wait_send()
        mix_copy(to).wait_send()

    def dp_sent(to):
        lf_copy(to).wait_send()
        gf_copy(to).wait_send()
        ge_copy(to).wait_send()

    others(pair_n, pair_me, pair_sent)
    others(dp_n, dp, dp_sent)


def body(token_ids, embedding, short_filter, long_filter, cotangent):
    vocab, width = embedding.shape
    dp_n, ctx_n = lax.axis_size("dp"), lax.axis_size("ctx")
    part = width // ctx_n
    block = token_ids.shape[1]
    length = block * ctx_n
    cw, sub, bs, pair_n = part // 2, length // 4, block // 4, 2 * ctx_n
    lr, vr = length // dp_n, vocab // dp_n
    fwd, inv, perm = tables(length, block)
    ids = jnp.broadcast_to(token_ids.reshape(bs, 4).T.reshape(1, block), (8, block))
    hbm = pl.BlockSpec(memory_space=pl.ANY)
    vmem = pl.BlockSpec(memory_space=pltpu.VMEM)
    dma = pltpu.SemaphoreType.DMA
    return pl.pallas_call(
        functools.partial(kernel, (dp_n, ctx_n, vocab, part, block)),
        out_shape=[
            jax.ShapeDtypeStruct((1, block, width), BF),
            jax.ShapeDtypeStruct((vr, part), F32),
            jax.ShapeDtypeStruct((lr, part), F32),
        ],
        in_specs=[vmem, vmem, hbm, hbm, hbm, hbm, hbm, hbm],
        out_specs=[hbm, vmem, vmem],
        scratch_shapes=[
            pltpu.VMEM((pair_n, 8, block), jnp.int32),
            pltpu.VMEM((vocab, cw), BF),
            pltpu.VMEM((3, 3, cw), F32),
            pltpu.VMEM((dp_n, lr, cw), BF),
            pltpu.VMEM((pair_n, block, cw), BF),
            pltpu.VMEM(fwd.shape, BF),
            pltpu.VMEM(inv.shape, BF),
            pltpu.VMEM((2, 4, sub, cw), F32),
            pltpu.VMEM((2, 4, sub, cw), F32),
            pltpu.VMEM((2, 4, sub, cw), F32),
            pltpu.VMEM((2, 4, sub, cw), F32),
            pltpu.VMEM((2, 4, sub, cw), BF),
            pltpu.VMEM((4, sub, cw), BF),
            pltpu.VMEM((4, 2, sub, cw), F32),
            pltpu.VMEM((2, 4, 2, sub, cw), F32),
            pltpu.VMEM((2, 4, 2 * sub, cw), F32),
            pltpu.VMEM((2, 4, 2 * sub, cw), BF),
            pltpu.VMEM((4, 2 * sub, cw), BF),
            pltpu.VMEM((2, 4, sub, cw), F32),
            pltpu.VMEM((2, 4, sub, cw), F32),
            pltpu.VMEM((2, ctx_n, 4, bs, cw), BF),
            pltpu.VMEM((pair_n, block, cw), BF),
            pltpu.VMEM((dp_n, lr, cw), BF),
            pltpu.VMEM((dp_n, lr, cw), BF),
            pltpu.VMEM((vocab, cw), F32),
            pltpu.VMEM((vocab, cw), BF),
            pltpu.VMEM((dp_n, vr, cw), BF),
            dma((4,)),
            dma((pair_n,)), dma((pair_n,)),
            dma((dp_n,)), dma((dp_n,)),
            dma((pair_n,)), dma((pair_n,)),
            dma((pair_n,)), dma((pair_n,)),
            dma((dp_n,)), dma((dp_n,)),
            dma((dp_n,)), dma((dp_n,)),
        ],
        compiler_params=pltpu.CompilerParams(
            collective_id=0, has_side_effects=True, vmem_limit_bytes=56 * 1024 * 1024
        ),
        name="hyena",
    )(ids, perm, embedding, short_filter, long_filter, cotangent, fwd, inv)


def solution(mesh):
    in_specs = (P("dp", "ctx"), P(), P(), P("dp", "ctx"), P("dp", "ctx", None))
    out_specs = (P("dp", "ctx", None), P("dp", "ctx"), P("dp", "ctx"))
    return jax.shard_map(body, mesh=mesh, in_specs=in_specs, out_specs=out_specs, check_vma=False)
```

```python
import functools
import math

import jax
import jax.numpy as jnp
import numpy as np
from jax import lax
from jax.experimental import pallas as pl
from jax.experimental.pallas import tpu as pltpu
from jax.sharding import PartitionSpec as P

BF = jnp.bfloat16
F32 = jnp.float32
MESH = pl.DeviceIdType.MESH
LANES = 128
KC = 16


def tables(length, block):
    sub = length // 4
    k = np.arange(sub)[None, :, None]
    t = 4 * np.arange(sub)[None, None, :] + np.arange(4)[:, None, None]
    angle = 2.0 * math.pi * (((4 * k + 1) * t) % (4 * length)) / (4 * length)
    fwd = np.concatenate([np.cos(angle), -np.sin(angle)], 1)
    inv = fwd.transpose(0, 2, 1) / length
    out = np.arange(block)
    perm = np.zeros((2, block, block))
    perm[0, out, 4 * (out % (block // 4)) + out // (block // 4)] = 1.0
    perm[1] = perm[0].T
    return jnp.asarray(fwd, BF), jnp.asarray(inv, BF), jnp.asarray(perm, BF)


def radix4(re, im, sign):
    a_re, a_im, b_re, b_im = re[0] + re[2], im[0] + im[2], re[0] - re[2], im[0] - im[2]
    c_re, c_im, d_re, d_im = re[1] + re[3], im[1] + im[3], re[1] - re[3], im[1] - im[3]
    if sign > 0:
        d_re, d_im = -d_re, -d_im
    return (
        [a_re + c_re, b_re + d_im, a_re - c_re, b_re - d_im],
        [a_im + c_im, b_im - d_re, a_im - c_im, b_im + d_re],
    )


def loop(count, step):
    def run(i, carry):
        step(i)
        return carry

    lax.fori_loop(0, count, run, 0)


def dot(a, b):
    return jnp.dot(a, b, preferred_element_type=F32)


def kernel(
    dims,
    ids_ref, perm, emb_hbm, taps_hbm, lf_hbm, cot_hbm, fwd_hbm, inv_hbm,
    mixed_hbm, ge_ref, gf_ref,
    ids_mine, ids_in, emb, taps, lf_in, cot_in, fwd, inv,
    x, uq, uk, uv, field, hfield, spec_h, spec_z, pbuf, wbuf, wf, conv, gq, gx,
    onehot, lookups, mixed_out, gf_out, gf_in, ge_out, ge_in,
    local_sem, ids_send, ids_recv, lf_send, lf_recv, cot_send, cot_recv,
    mix_send, mix_recv, gf_send, gf_recv, ge_send, ge_recv,
):
    dp_n, ctx_n, vocab, part, block = dims
    cw = part // 2
    sub = ctx_n * block // 4
    bs = block // 4
    pair_n = 2 * ctx_n
    per = dp_n // ctx_n
    lr = block // per
    vr = vocab // dp_n
    dp = lax.axis_index("dp")
    p_me = lax.axis_index("ctx")
    g = lax.div(dp, 2)
    c_me = lax.rem(dp, 2)
    pair_me = c_me * ctx_n + p_me
    first = pl.multiple_of(p_me * part + c_me * cw, cw)
    halves = [pl.ds(h * LANES, LANES) for h in range(cw // LANES)]

    def chunk(i, size):
        return pl.ds(pl.multiple_of(i * size, size), size)

    loads = [
        pltpu.make_async_copy(emb_hbm.at[:, pl.ds(first, cw)], emb, local_sem.at[0]),
        pltpu.make_async_copy(taps_hbm.at[:, :, pl.ds(first, cw)], taps, local_sem.at[1]),
        pltpu.make_async_copy(fwd_hbm, fwd, local_sem.at[2]),
        pltpu.make_async_copy(inv_hbm, inv, local_sem.at[3]),
    ]
    for load in loads:
        load.start()

    ids = jnp.broadcast_to(ids_ref[...].astype(F32), (8, block))
    high = jnp.where(ids >= 256.0, 1.0, 0.0)
    low = ids - 256.0 * high
    ids_mine[...] = dot(low.astype(BF), perm[1]) + 256.0 * dot(high.astype(BF), perm[1])

    barrier = pltpu.get_barrier_semaphore()

    def greet_pair(i):
        to = lax.rem(pair_me + 1 + i, pair_n)
        device = (2 * g + lax.div(to, ctx_n), lax.rem(to, ctx_n))
        pl.semaphore_signal(barrier, inc=1, device_id=device, device_id_type=MESH)

    def greet_dp(i):
        device = (lax.rem(dp + 1 + i, dp_n), p_me)
        pl.semaphore_signal(barrier, inc=1, device_id=device, device_id_type=MESH)

    loop(pair_n - 1, greet_pair)
    loop(dp_n - 1, greet_dp)
    pl.semaphore_wait(barrier, pair_n + dp_n - 2)

    def ids_copy(to):
        return pltpu.make_async_remote_copy(
            src_ref=ids_mine, dst_ref=ids_in.at[pair_me], send_sem=ids_send.at[to], recv_sem=ids_recv.at[pair_me],
            device_id=(2 * g + lax.div(to, ctx_n), lax.rem(to, ctx_n)), device_id_type=MESH,
        )

    def lf_copy(to):
        return pltpu.make_async_remote_copy(
            src_ref=lf_hbm.at[:, chunk(lax.rem(to, 2), cw)], dst_ref=lf_in.at[dp],
            send_sem=lf_send.at[to], recv_sem=lf_recv.at[dp], device_id=(to, p_me), device_id_type=MESH,
        )

    def cot_columns(to):
        return cot_hbm.at[0, :, chunk(2 * lax.rem(to, ctx_n) + lax.div(to, ctx_n), cw)]

    def cot_copy(to):
        return pltpu.make_async_remote_copy(
            src_ref=cot_columns(to), dst_ref=cot_in.at[pair_me], send_sem=cot_send.at[to], recv_sem=cot_recv.at[pair_me],
            device_id=(2 * g + lax.div(to, ctx_n), lax.rem(to, ctx_n)), device_id_type=MESH,
        )

    def mix_copy(to):
        return pltpu.make_async_remote_copy(
            src_ref=mixed_out.at[to], dst_ref=mixed_hbm.at[0, :, pl.ds(first, cw)],
            send_sem=mix_send.at[to], recv_sem=mix_recv.at[pair_me],
            device_id=(2 * g + lax.div(to, ctx_n), lax.rem(to, ctx_n)), device_id_type=MESH,
        )

    def gf_copy(to):
        return pltpu.make_async_remote_copy(
            src_ref=gf_out.at[to], dst_ref=gf_in.at[dp], send_sem=gf_send.at[to], recv_sem=gf_recv.at[dp],
            device_id=(to, p_me), device_id_type=MESH,
        )

    def ge_copy(to):
        return pltpu.make_async_remote_copy(
            src_ref=ge_out.at[chunk(to, vr)], dst_ref=ge_in.at[dp], send_sem=ge_send.at[to], recv_sem=ge_recv.at[dp],
            device_id=(to, p_me), device_id_type=MESH,
        )

    def others(count, me, step):
        loop(count - 1, lambda i: step(lax.rem(me + 1 + i, count)))

    def arrived(slot, sem):
        pltpu.make_async_copy(slot, slot, sem).wait()

    pltpu.make_async_copy(ids_mine, ids_in.at[pair_me], ids_recv.at[pair_me]).start()
    pltpu.make_async_copy(lf_hbm.at[:, chunk(c_me, cw)], lf_in.at[dp], lf_recv.at[dp]).start()
    pltpu.make_async_copy(cot_columns(pair_me), cot_in.at[pair_me], cot_recv.at[pair_me]).start()
    others(pair_n, pair_me, lambda to: ids_copy(to).start())
    others(dp_n, dp, lambda to: lf_copy(to).start())
    others(pair_n, pair_me, lambda to: cot_copy(to).start())

    loads[0].wait()
    loads[1].wait()
    vocab_lane = lax.broadcasted_iota(jnp.int32, (block, LANES), 1).astype(F32)

    def phase_lookup():
        def lookup(i):
            arrived(ids_in.at[i], ids_recv.at[i])
            column = jnp.transpose(jnp.broadcast_to(ids_in[i, 0:1, :], (block, block)))
            for q in range(vocab // LANES):
                onehot[chunk(i, block), q * LANES : (q + 1) * LANES] = (
                    (column == vocab_lane + float(q * LANES)).astype(F32).astype(BF)
                )

        loop(pair_n, lookup)

    def phase_embed():
        def embed(i):
            rows = dot(onehot[chunk(i, 4 * block), :], emb[...])
            for q in range(4):
                s, p = lax.div(4 * i + q, ctx_n), lax.rem(4 * i + q, ctx_n)
                for j in range(4):
                    x[s, j, chunk(p, bs), :] = rows[q * block + j * bs : q * block + (j + 1) * bs]

        loop(pair_n // 4, embed)

    phase_lookup()
    phase_embed()

    row16 = lax.broadcasted_iota(jnp.int32, (bs, LANES), 0)
    def phase_short():
        for h in halves:
            f = [[taps[r, i : i + 1, h] for i in range(3)] for r in range(3)]

            def short(s, h=h, f=f):
                def step(p, carry):
                    rows = chunk(p, bs)
                    xs = [x[s, j, rows, h] for j in range(4)]
                    turned = [pltpu.roll(xs[2], 1, 0), pltpu.roll(xs[3], 1, 0)]
                    late = [jnp.where(row16 == 0, carry[q], turned[q]) for q in range(2)]
                    line = late + xs
                    us = [
                        [f[r][0] * line[j + 2] + f[r][1] * line[j + 1] + f[r][2] * line[j] for j in range(4)]
                        for r in range(3)
                    ]
                    for j in range(4):
                        uq[s, j, rows, h] = us[0][j]
                        uk[s, j, rows, h] = us[1][j]
                        uv[s, j, rows, h] = us[2][j]
                        field[s, j, rows, h] = (us[1][j] * us[2][j]).astype(BF)
                    return tuple(turned)

                zero = jnp.zeros((bs, LANES), F32)
                lax.fori_loop(0, ctx_n, step, (zero, zero))

            loop(2, short)

    phase_short()

    loads[2].wait()

    def phase_taps():
        def gather_taps(i):
            for q in range(per):
                arrived(lf_in.at[i * per + q], lf_recv.at[i * per + q])
            rows = jnp.concatenate([lf_in[i * per + q] for q in range(per)], 0)
            rows = dot(perm[0], rows).astype(BF)
            for j in range(4):
                hfield[j, chunk(i, bs), :] = rows[j * bs : (j + 1) * bs]

        loop(ctx_n, gather_taps)

    phase_taps()

    def filter_dft(j):
        pbuf[0, j] = dot(fwd[j], hfield[j])

    def phase_filter_dft():
        loop(4, filter_dft)

    phase_filter_dft()

    def butterfly(s, i, h):
        re = [pbuf[s, j, chunk(i, KC), h] for j in range(4)]
        im = [pbuf[s, j, pl.ds(pl.multiple_of(sub + i * KC, KC), KC), h] for j in range(4)]
        return radix4(re, im, -1)

    def filter_mix(i):
        for h in halves:
            re, im = butterfly(0, i, h)
            for m in range(4):
                spec_h[m, 0, chunk(i, KC), h] = re[m]
                spec_h[m, 1, chunk(i, KC), h] = im[m]

    def phase_filter_mix():
        loop(sub // KC, filter_mix)

    phase_filter_mix()

    def field_dft(i):
        s, j = lax.div(i, 4), lax.rem(i, 4)
        pbuf[s, j] = dot(fwd[j], field[s, j])

    def put(ref, i, h, re, im):
        re, im = radix4(re, im, 1)
        for j in range(4):
            ref[j, chunk(i, KC), h] = re[j].astype(BF)
            ref[j, pl.ds(pl.multiple_of(sub + i * KC, KC), KC), h] = im[j].astype(BF)

    def phase_field_dft():
        loop(8, field_dft)

    phase_field_dft()
    loads[3].wait()

    for s in range(2):

        def conv_mix(i, s=s):
            for h in halves:
                re, im = butterfly(s, i, h)
                out_re, out_im = [], []
                for m in range(4):
                    spec_z[s, m, 0, chunk(i, KC), h] = re[m]
                    spec_z[s, m, 1, chunk(i, KC), h] = im[m]
                    h_re, h_im = spec_h[m, 0, chunk(i, KC), h], spec_h[m, 1, chunk(i, KC), h]
                    out_re.append(re[m] * h_re - im[m] * h_im)
                    out_im.append(re[m] * h_im + im[m] * h_re)
                put(wbuf.at[s], i, h, out_re, out_im)

        def phase_conv_mix():
            loop(sub // KC, conv_mix)

        phase_conv_mix()

        def conv_idft(j, s=s):
            conv[s, j] = dot(inv[j], wbuf[s, j]).astype(BF).astype(F32)

        def phase_conv_idft():
            loop(4, conv_idft)

        phase_conv_idft()

        def mix(i, s=s):
            p = lax.rem(p_me + 1 + i, ctx_n)
            rows = chunk(p, bs)
            out = jnp.concatenate([(uq[s, j, rows, :] * conv[s, j, rows, :]).astype(BF) for j in range(4)], 0)
            to = s * ctx_n + p
            mixed_out[to] = dot(perm[1], out).astype(BF)

            @pl.when(to != pair_me)
            def _():
                mix_copy(to).start()

            @pl.when(to == pair_me)
            def _():
                pltpu.make_async_copy(
                    mixed_out.at[to], mixed_hbm.at[0, :, pl.ds(first, cw)], mix_recv.at[pair_me]
                ).start()

        def phase_mix():
            loop(ctx_n, mix)

        phase_mix()

    vocab_row = lax.broadcasted_iota(jnp.int32, (vocab, block), 0).astype(F32)

    def phase_lookup_rows():
        def lookup(i):
            lookups[:, chunk(i, block)] = (vocab_row == ids_in[i, 0:1, :]).astype(F32).astype(BF)

        loop(pair_n, lookup)

    def take(i):
        s, p = lax.div(i, ctx_n), lax.rem(i, ctx_n)
        arrived(cot_in.at[i], cot_recv.at[i])
        out = dot(perm[0], cot_in[i])
        rows = chunk(p, bs)
        for j in range(4):
            piece = out[j * bs : (j + 1) * bs]
            field[s, j, rows, :] = (piece * uq[s, j, rows, :]).astype(BF)
            gq[s, j, rows, :] = piece * conv[s, j, rows, :]

    def phase_take():
        loop(pair_n, take)

    phase_lookup_rows()
    phase_take()
    phase_field_dft()

    def back_mix(i):
        for h in halves:
            sum_re, sum_im = None, None
            for s in range(2):
                re, im = butterfly(s, i, h)
                out_re, out_im, f_re, f_im = [], [], [], []
                for m in range(4):
                    h_re, h_im = spec_h[m, 0, chunk(i, KC), h], spec_h[m, 1, chunk(i, KC), h]
                    z_re, z_im = spec_z[s, m, 0, chunk(i, KC), h], spec_z[s, m, 1, chunk(i, KC), h]
                    out_re.append(re[m] * h_re + im[m] * h_im)
                    out_im.append(im[m] * h_re - re[m] * h_im)
                    f_re.append(re[m] * z_re + im[m] * z_im)
                    f_im.append(im[m] * z_re - re[m] * z_im)
                put(wbuf.at[s], i, h, out_re, out_im)
                if s == 0:
                    sum_re, sum_im = f_re, f_im
                else:
                    sum_re = [a + b for a, b in zip(sum_re, f_re)]
                    sum_im = [a + b for a, b in zip(sum_im, f_im)]
            put(wf, i, h, sum_re, sum_im)

    def phase_back_mix():
        loop(sub // KC, back_mix)

    phase_back_mix()

    def filter_idft(j):
        hfield[j] = dot(inv[j], wf[j]).astype(BF)

    def phase_filter_idft():
        loop(4, filter_idft)

    phase_filter_idft()

    def filter_rows(i):
        rows = jnp.concatenate([hfield[j, chunk(i, bs), :] for j in range(4)], 0)
        rows = dot(perm[1], rows).astype(BF)
        for q in range(per):
            gf_out[i * per + q] = rows[q * lr : (q + 1) * lr]

    def phase_filter_rows():
        loop(ctx_n, filter_rows)

    phase_filter_rows()
    others(dp_n, dp, lambda to: gf_copy(to).start())
    pltpu.make_async_copy(gf_out.at[dp], gf_in.at[dp], gf_recv.at[dp]).start()

    def gz_idft(i):
        s, j = lax.div(i, 4), lax.rem(i, 4)
        conv[s, j] = dot(inv[j], wbuf[s, j])

    def phase_gz_idft():
        loop(8, gz_idft)

    phase_gz_idft()

    def phase_grad():
        for h in halves:
            f = [[taps[r, i : i + 1, h] for i in range(3)] for r in range(3)]

            def grad(s, h=h, f=f):
                def step(i, carry):
                    p = ctx_n - 1 - i
                    rows = chunk(p, bs)
                    lines = [[], [], []]
                    for j in range(4):
                        gz = conv[s, j, rows, h].astype(BF).astype(F32)
                        gs = [gq[s, j, rows, h], gz * uv[s, j, rows, h], gz * uk[s, j, rows, h]]
                        for tap in range(3):
                            lines[tap].append(f[0][tap] * gs[0] + f[1][tap] * gs[1] + f[2][tap] * gs[2])
                    turned = [pltpu.roll(v, bs - 1, 0) for v in (lines[1][0], lines[2][0], lines[2][1])]
                    early = [jnp.where(row16 == bs - 1, carry[q], turned[q]) for q in range(3)]
                    once = lines[1][1:] + [early[0]]
                    twice = lines[2][2:] + [early[1], early[2]]
                    for j in range(4):
                        gx[s, p, j, :, h] = (lines[0][j] + once[j] + twice[j]).astype(BF)
                    return tuple(turned)

                zero = jnp.zeros((bs, LANES), F32)
                lax.fori_loop(0, ctx_n, step, (zero, zero, zero))

            loop(2, grad)

    phase_grad()

    def phase_scatter():
        ge_out[...] = dot(lookups[...], gx[...].reshape(pair_n * block, cw)).astype(BF)

    phase_scatter()
    others(dp_n, dp, lambda to: ge_copy(to).start())
    pltpu.make_async_copy(ge_out.at[chunk(dp, vr)], ge_in.at[dp], ge_recv.at[dp]).start()

    loop(dp_n, lambda i: arrived(gf_in.at[i], gf_recv.at[i]))
    for q in range(2):
        total = gf_in[q].astype(F32)
        for i in range(1, dp_n // 2):
            total = total + gf_in[2 * i + q].astype(F32)
        gf_ref[:, q * cw : (q + 1) * cw] = total
    loop(dp_n, lambda i: arrived(ge_in.at[i], ge_recv.at[i]))
    for q in range(2):
        total = ge_in[q].astype(F32)
        for i in range(1, dp_n // 2):
            total = total + ge_in[2 * i + q].astype(F32)
        ge_ref[:, q * cw : (q + 1) * cw] = total

    def mixed_arrived(i):
        s, p = lax.div(i, ctx_n), lax.rem(i, ctx_n)
        arrived(mixed_hbm.at[0, :, chunk(2 * p + s, cw)], mix_recv.at[i])

    loop(pair_n, mixed_arrived)

    def pair_sent(to):
        ids_copy(to).wait_send()
        cot_copy(to).wait_send()
        mix_copy(to).wait_send()

    def dp_sent(to):
        lf_copy(to).wait_send()
        gf_copy(to).wait_send()
        ge_copy(to).wait_send()

    others(pair_n, pair_me, pair_sent)
    others(dp_n, dp, dp_sent)


def collect(mixed_raw, ge_raw, gf_raw, mixed, ge, gf, sem):
    rows = mixed.shape[1] // 4
    moves = [(mixed_raw.at[:, pl.ds(i * rows, rows)], mixed.at[:, pl.ds(i * rows, rows)]) for i in range(4)]
    moves += [(ge_raw, ge), (gf_raw, gf)]
    moves = [pltpu.make_async_copy(a, b, sem.at[i]) for i, (a, b) in enumerate(moves)]
    for move in moves:
        move.start()
    for move in moves:
        move.wait()


def body(token_ids, embedding, short_filter, long_filter, cotangent):
    vocab, width = embedding.shape
    dp_n, ctx_n = lax.axis_size("dp"), lax.axis_size("ctx")
    part = width // ctx_n
    block = token_ids.shape[1]
    length = block * ctx_n
    cw, sub, bs, pair_n = part // 2, length // 4, block // 4, 2 * ctx_n
    lr, vr = length // dp_n, vocab // dp_n
    fwd, inv, perm = tables(length, block)
    hbm = pl.BlockSpec(memory_space=pl.ANY)
    vmem = pl.BlockSpec(memory_space=pltpu.VMEM)
    dma = pltpu.SemaphoreType.DMA
    results = pl.pallas_call(
        functools.partial(kernel, (dp_n, ctx_n, vocab, part, block)),
        out_shape=[
            jax.ShapeDtypeStruct((1, block, width), BF),
            jax.ShapeDtypeStruct((vr, part), F32),
            jax.ShapeDtypeStruct((lr, part), F32),
        ],
        in_specs=[vmem, vmem, hbm, hbm, hbm, hbm, hbm, hbm],
        out_specs=[hbm, vmem, vmem],
        scratch_shapes=[
            pltpu.VMEM((8, block), F32),
            pltpu.VMEM((pair_n, 8, block), F32),
            pltpu.VMEM((vocab, cw), BF),
            pltpu.VMEM((3, 3, cw), F32),
            pltpu.VMEM((dp_n, lr, cw), BF),
            pltpu.VMEM((pair_n, block, cw), BF),
            pltpu.VMEM(fwd.shape, BF),
            pltpu.VMEM(inv.shape, BF),
            pltpu.VMEM((2, 4, sub, cw), F32),
            pltpu.VMEM((2, 4, sub, cw), F32),
            pltpu.VMEM((2, 4, sub, cw), F32),
            pltpu.VMEM((2, 4, sub, cw), F32),
            pltpu.VMEM((2, 4, sub, cw), BF),
            pltpu.VMEM((4, sub, cw), BF),
            pltpu.VMEM((4, 2, sub, cw), F32),
            pltpu.VMEM((2, 4, 2, sub, cw), F32),
            pltpu.VMEM((2, 4, 2 * sub, cw), F32),
            pltpu.VMEM((2, 4, 2 * sub, cw), BF),
            pltpu.VMEM((4, 2 * sub, cw), BF),
            pltpu.VMEM((2, 4, sub, cw), F32),
            pltpu.VMEM((2, 4, sub, cw), F32),
            pltpu.VMEM((2, ctx_n, 4, bs, cw), BF),
            pltpu.VMEM((pair_n * block, vocab), BF),
            pltpu.VMEM((vocab, pair_n * block), BF),
            pltpu.VMEM((pair_n, block, cw), BF),
            pltpu.VMEM((dp_n, lr, cw), BF),
            pltpu.VMEM((dp_n, lr, cw), BF),
            pltpu.VMEM((vocab, cw), BF),
            pltpu.VMEM((dp_n, vr, cw), BF),
            dma((4,)),
            dma((pair_n,)), dma((pair_n,)),
            dma((dp_n,)), dma((dp_n,)),
            dma((pair_n,)), dma((pair_n,)),
            dma((pair_n,)), dma((pair_n,)),
            dma((dp_n,)), dma((dp_n,)),
            dma((dp_n,)), dma((dp_n,)),
        ],
        compiler_params=pltpu.CompilerParams(
            collective_id=0, has_side_effects=True, vmem_limit_bytes=56 * 1024 * 1024
        ),
        name="hyena",
    )(token_ids, perm, embedding, short_filter, long_filter, cotangent, fwd, inv)
    return pl.pallas_call(
        collect,
        out_shape=[jax.ShapeDtypeStruct(r.shape, r.dtype) for r in results],
        in_specs=[hbm] * 3,
        out_specs=[hbm] * 3,
        scratch_shapes=[dma((6,))],
        compiler_params=pltpu.CompilerParams(vmem_limit_bytes=56 * 1024 * 1024),
        name="collect",
    )(*results)


def solution(mesh):
    in_specs = (P("dp", "ctx"), P(), P(), P("dp", "ctx"), P("dp", "ctx", None))
    out_specs = (P("dp", "ctx", None), P("dp", "ctx"), P("dp", "ctx"))
    return jax.shard_map(body, mesh=mesh, in_specs=in_specs, out_specs=out_specs, check_vma=False)
```

```python
import functools
import math

import jax
import jax.numpy as jnp
import numpy as np
from jax import lax
from jax.experimental import pallas as pl
from jax.experimental.pallas import tpu as pltpu
from jax.sharding import PartitionSpec as P

BF = jnp.bfloat16
F32 = jnp.float32
MESH = pl.DeviceIdType.MESH
LANES = 128
KC = 16


def tables(length, block):
    sub = length // 4
    k = np.arange(sub)[None, :, None]
    t = 4 * np.arange(sub)[None, None, :] + np.arange(4)[:, None, None]
    angle = 2.0 * math.pi * (((4 * k + 1) * t) % (4 * length)) / (4 * length)
    fwd = np.concatenate([np.cos(angle), -np.sin(angle)], 1)
    inv = fwd.transpose(0, 2, 1) / length
    out = np.arange(block)
    perm = np.zeros((2, block, block))
    perm[0, out, 4 * (out % (block // 4)) + out // (block // 4)] = 1.0
    perm[1] = perm[0].T
    return jnp.asarray(fwd, BF), jnp.asarray(inv, BF), jnp.asarray(perm, BF)


def radix4(re, im, sign):
    a_re, a_im, b_re, b_im = re[0] + re[2], im[0] + im[2], re[0] - re[2], im[0] - im[2]
    c_re, c_im, d_re, d_im = re[1] + re[3], im[1] + im[3], re[1] - re[3], im[1] - im[3]
    if sign > 0:
        d_re, d_im = -d_re, -d_im
    return (
        [a_re + c_re, b_re + d_im, a_re - c_re, b_re - d_im],
        [a_im + c_im, b_im - d_re, a_im - c_im, b_im + d_re],
    )


def loop(count, step):
    def run(i, carry):
        step(i)
        return carry

    lax.fori_loop(0, count, run, 0)


def dot(a, b):
    return jnp.dot(a, b, preferred_element_type=F32)


def kernel(
    dims,
    ids_ref, perm, emb_hbm, taps_hbm, lf_hbm, cot_hbm, fwd_hbm, inv_hbm,
    mixed_hbm, ge_ref, gf_ref,
    ids_mine, ids_in, emb, taps, lf_in, cot_in, fwd, inv,
    x, uq, uk, uv, field, hfield, spec_h, spec_z, pbuf, wbuf, wf, conv, gq, gx,
    onehot, lookups, mixed_out, gf_out, gf_in, ge_out, ge_in,
    local_sem, ids_send, ids_recv, lf_send, lf_recv, cot_send, cot_recv,
    mix_send, mix_recv, gf_send, gf_recv, ge_send, ge_recv,
):
    dp_n, ctx_n, vocab, part, block = dims
    cw = part // 2
    sub = ctx_n * block // 4
    bs = block // 4
    pair_n = 2 * ctx_n
    per = dp_n // ctx_n
    lr = block // per
    vr = vocab // dp_n
    dp = lax.axis_index("dp")
    p_me = lax.axis_index("ctx")
    g = lax.div(dp, 2)
    c_me = lax.rem(dp, 2)
    pair_me = c_me * ctx_n + p_me
    first = pl.multiple_of(p_me * part + c_me * cw, cw)
    halves = [pl.ds(h * LANES, LANES) for h in range(cw // LANES)]

    def chunk(i, size):
        return pl.ds(pl.multiple_of(i * size, size), size)

    loads = [
        pltpu.make_async_copy(emb_hbm.at[:, pl.ds(first, cw)], emb, local_sem.at[0]),
        pltpu.make_async_copy(taps_hbm.at[:, :, pl.ds(first, cw)], taps, local_sem.at[1]),
        pltpu.make_async_copy(fwd_hbm, fwd, local_sem.at[2]),
        pltpu.make_async_copy(inv_hbm, inv, local_sem.at[3]),
    ]
    for load in loads:
        load.start()

    ids = jnp.broadcast_to(ids_ref[...].astype(F32), (8, block))
    high = jnp.where(ids >= 256.0, 1.0, 0.0)
    low = ids - 256.0 * high
    ids_mine[...] = dot(low.astype(BF), perm[1]) + 256.0 * dot(high.astype(BF), perm[1])

    barrier = pltpu.get_barrier_semaphore()

    def greet_pair(i):
        to = lax.rem(pair_me + 1 + i, pair_n)
        device = (2 * g + lax.div(to, ctx_n), lax.rem(to, ctx_n))
        pl.semaphore_signal(barrier, inc=1, device_id=device, device_id_type=MESH)

    def greet_dp(i):
        device = (lax.rem(dp + 1 + i, dp_n), p_me)
        pl.semaphore_signal(barrier, inc=1, device_id=device, device_id_type=MESH)

    loop(pair_n - 1, greet_pair)
    loop(dp_n - 1, greet_dp)
    pl.semaphore_wait(barrier, pair_n + dp_n - 2)

    def ids_copy(to):
        return pltpu.make_async_remote_copy(
            src_ref=ids_mine, dst_ref=ids_in.at[pair_me], send_sem=ids_send.at[to], recv_sem=ids_recv.at[pair_me],
            device_id=(2 * g + lax.div(to, ctx_n), lax.rem(to, ctx_n)), device_id_type=MESH,
        )

    def lf_copy(to):
        return pltpu.make_async_remote_copy(
            src_ref=lf_hbm.at[:, chunk(lax.rem(to, 2), cw)], dst_ref=lf_in.at[dp],
            send_sem=lf_send.at[to], recv_sem=lf_recv.at[dp], device_id=(to, p_me), device_id_type=MESH,
        )

    def cot_columns(to):
        return cot_hbm.at[0, :, chunk(2 * lax.rem(to, ctx_n) + lax.div(to, ctx_n), cw)]

    def cot_copy(to):
        return pltpu.make_async_remote_copy(
            src_ref=cot_columns(to), dst_ref=cot_in.at[pair_me], send_sem=cot_send.at[to], recv_sem=cot_recv.at[pair_me],
            device_id=(2 * g + lax.div(to, ctx_n), lax.rem(to, ctx_n)), device_id_type=MESH,
        )

    def mix_copy(to):
        return pltpu.make_async_remote_copy(
            src_ref=mixed_out.at[to], dst_ref=mixed_hbm.at[0, :, pl.ds(first, cw)],
            send_sem=mix_send.at[to], recv_sem=mix_recv.at[pair_me],
            device_id=(2 * g + lax.div(to, ctx_n), lax.rem(to, ctx_n)), device_id_type=MESH,
        )

    def gf_copy(to):
        return pltpu.make_async_remote_copy(
            src_ref=gf_out.at[to], dst_ref=gf_in.at[dp], send_sem=gf_send.at[to], recv_sem=gf_recv.at[dp],
            device_id=(to, p_me), device_id_type=MESH,
        )

    def ge_copy(to):
        return pltpu.make_async_remote_copy(
            src_ref=ge_out.at[chunk(to, vr)], dst_ref=ge_in.at[dp], send_sem=ge_send.at[to], recv_sem=ge_recv.at[dp],
            device_id=(to, p_me), device_id_type=MESH,
        )

    def others(count, me, step):
        loop(count - 1, lambda i: step(lax.rem(me + 1 + i, count)))

    def arrived(slot, sem):
        pltpu.make_async_copy(slot, slot, sem).wait()

    pltpu.make_async_copy(ids_mine, ids_in.at[pair_me], ids_recv.at[pair_me]).start()
    pltpu.make_async_copy(lf_hbm.at[:, chunk(c_me, cw)], lf_in.at[dp], lf_recv.at[dp]).start()
    pltpu.make_async_copy(cot_columns(pair_me), cot_in.at[pair_me], cot_recv.at[pair_me]).start()
    others(pair_n, pair_me, lambda to: ids_copy(to).start())
    others(dp_n, dp, lambda to: lf_copy(to).start())
    others(pair_n, pair_me, lambda to: cot_copy(to).start())

    loads[0].wait()
    loads[1].wait()
    vocab_lane = lax.broadcasted_iota(jnp.int32, (block, LANES), 1).astype(F32)

    def phase_lookup():
        def lookup(i):
            arrived(ids_in.at[i], ids_recv.at[i])
            column = jnp.transpose(jnp.broadcast_to(ids_in[i, 0:1, :], (block, block)))
            for q in range(vocab // LANES):
                onehot[chunk(i, block), q * LANES : (q + 1) * LANES] = (
                    (column == vocab_lane + float(q * LANES)).astype(F32).astype(BF)
                )

        loop(pair_n, lookup)

    def phase_embed():
        def embed(i):
            rows = dot(onehot[chunk(i, 4 * block), :], emb[...])
            for q in range(4):
                s, p = lax.div(4 * i + q, ctx_n), lax.rem(4 * i + q, ctx_n)
                for j in range(4):
                    x[s, j, chunk(p, bs), :] = rows[q * block + j * bs : q * block + (j + 1) * bs]

        loop(pair_n // 4, embed)

    phase_lookup()
    phase_embed()

    row16 = lax.broadcasted_iota(jnp.int32, (bs, LANES), 0)
    def phase_short():
        for h in halves:
            f = [[taps[r, i : i + 1, h] for i in range(3)] for r in range(3)]

            def short(s, h=h, f=f):
                def step(p, carry):
                    rows = chunk(p, bs)
                    xs = [x[s, j, rows, h] for j in range(4)]
                    turned = [pltpu.roll(xs[2], 1, 0), pltpu.roll(xs[3], 1, 0)]
                    late = [jnp.where(row16 == 0, carry[q], turned[q]) for q in range(2)]
                    line = late + xs
                    us = [
                        [f[r][0] * line[j + 2] + f[r][1] * line[j + 1] + f[r][2] * line[j] for j in range(4)]
                        for r in range(3)
                    ]
                    for j in range(4):
                        uq[s, j, rows, h] = us[0][j]
                        uk[s, j, rows, h] = us[1][j]
                        uv[s, j, rows, h] = us[2][j]
                        field[s, j, rows, h] = (us[1][j] * us[2][j]).astype(BF)
                    return tuple(turned)

                zero = jnp.zeros((bs, LANES), F32)
                lax.fori_loop(0, ctx_n, step, (zero, zero))

            loop(2, short)

    phase_short()

    loads[2].wait()

    def phase_taps():
        def gather_taps(i):
            for q in range(per):
                arrived(lf_in.at[i * per + q], lf_recv.at[i * per + q])
            rows = jnp.concatenate([lf_in[i * per + q] for q in range(per)], 0)
            rows = dot(perm[0], rows).astype(BF)
            for j in range(4):
                hfield[j, chunk(i, bs), :] = rows[j * bs : (j + 1) * bs]

        loop(ctx_n, gather_taps)

    phase_taps()

    def filter_dft(j):
        pbuf[0, j] = dot(fwd[j], hfield[j])

    def phase_filter_dft():
        loop(4, filter_dft)

    phase_filter_dft()

    def butterfly(s, i, h):
        re = [pbuf[s, j, chunk(i, KC), h] for j in range(4)]
        im = [pbuf[s, j, pl.ds(pl.multiple_of(sub + i * KC, KC), KC), h] for j in range(4)]
        return radix4(re, im, -1)

    def filter_mix(i):
        for h in halves:
            re, im = butterfly(0, i, h)
            for m in range(4):
                spec_h[m, 0, chunk(i, KC), h] = re[m]
                spec_h[m, 1, chunk(i, KC), h] = im[m]

    def phase_filter_mix():
        loop(sub // KC, filter_mix)

    phase_filter_mix()

    def field_dft(i):
        s, j = lax.div(i, 4), lax.rem(i, 4)
        pbuf[s, j] = dot(fwd[j], field[s, j])

    def put(ref, i, h, re, im):
        re, im = radix4(re, im, 1)
        for j in range(4):
            ref[j, chunk(i, KC), h] = re[j].astype(BF)
            ref[j, pl.ds(pl.multiple_of(sub + i * KC, KC), KC), h] = im[j].astype(BF)

    def phase_field_dft():
        loop(8, field_dft)

    phase_field_dft()
    loads[3].wait()

    for s in range(2):

        def conv_mix(i, s=s):
            for h in halves:
                re, im = butterfly(s, i, h)
                out_re, out_im = [], []
                for m in range(4):
                    spec_z[s, m, 0, chunk(i, KC), h] = re[m]
                    spec_z[s, m, 1, chunk(i, KC), h] = im[m]
                    h_re, h_im = spec_h[m, 0, chunk(i, KC), h], spec_h[m, 1, chunk(i, KC), h]
                    out_re.append(re[m] * h_re - im[m] * h_im)
                    out_im.append(re[m] * h_im + im[m] * h_re)
                put(wbuf.at[s], i, h, out_re, out_im)

        def phase_conv_mix():
            loop(sub // KC, conv_mix)

        phase_conv_mix()

        def conv_idft(j, s=s):
            conv[s, j] = dot(inv[j], wbuf[s, j]).astype(BF).astype(F32)

        def phase_conv_idft():
            loop(4, conv_idft)

        phase_conv_idft()

        def mix(i, s=s):
            p = lax.rem(p_me + 1 + i, ctx_n)
            rows = chunk(p, bs)
            out = jnp.concatenate([(uq[s, j, rows, :] * conv[s, j, rows, :]).astype(BF) for j in range(4)], 0)
            to = s * ctx_n + p
            mixed_out[to] = dot(perm[1], out).astype(BF)

            @pl.when(to != pair_me)
            def _():
                mix_copy(to).start()

            @pl.when(to == pair_me)
            def _():
                pltpu.make_async_copy(
                    mixed_out.at[to], mixed_hbm.at[0, :, pl.ds(first, cw)], mix_recv.at[pair_me]
                ).start()

        def phase_mix():
            loop(ctx_n, mix)

        phase_mix()

    vocab_row = lax.broadcasted_iota(jnp.int32, (vocab, block), 0).astype(F32)

    def phase_lookup_rows():
        def lookup(i):
            lookups[:, chunk(i, block)] = (vocab_row == ids_in[i, 0:1, :]).astype(F32).astype(BF)

        loop(pair_n, lookup)

    def take(i):
        s, p = lax.div(i, ctx_n), lax.rem(i, ctx_n)
        arrived(cot_in.at[i], cot_recv.at[i])
        out = dot(perm[0], cot_in[i])
        rows = chunk(p, bs)
        for j in range(4):
            piece = out[j * bs : (j + 1) * bs]
            field[s, j, rows, :] = (piece * uq[s, j, rows, :]).astype(BF)
            gq[s, j, rows, :] = piece * conv[s, j, rows, :]

    def phase_take():
        loop(pair_n, take)

    phase_lookup_rows()
    phase_take()
    phase_field_dft()

    def back_mix(i):
        for h in halves:
            sum_re, sum_im = None, None
            for s in range(2):
                re, im = butterfly(s, i, h)
                out_re, out_im, f_re, f_im = [], [], [], []
                for m in range(4):
                    h_re, h_im = spec_h[m, 0, chunk(i, KC), h], spec_h[m, 1, chunk(i, KC), h]
                    z_re, z_im = spec_z[s, m, 0, chunk(i, KC), h], spec_z[s, m, 1, chunk(i, KC), h]
                    out_re.append(re[m] * h_re + im[m] * h_im)
                    out_im.append(im[m] * h_re - re[m] * h_im)
                    f_re.append(re[m] * z_re + im[m] * z_im)
                    f_im.append(im[m] * z_re - re[m] * z_im)
                put(wbuf.at[s], i, h, out_re, out_im)
                if s == 0:
                    sum_re, sum_im = f_re, f_im
                else:
                    sum_re = [a + b for a, b in zip(sum_re, f_re)]
                    sum_im = [a + b for a, b in zip(sum_im, f_im)]
            put(wf, i, h, sum_re, sum_im)

    def phase_back_mix():
        loop(sub // KC, back_mix)

    phase_back_mix()

    def filter_idft(j):
        hfield[j] = dot(inv[j], wf[j]).astype(BF)

    def phase_filter_idft():
        loop(4, filter_idft)

    phase_filter_idft()

    def filter_rows(i):
        rows = jnp.concatenate([hfield[j, chunk(i, bs), :] for j in range(4)], 0)
        rows = dot(perm[1], rows).astype(BF)
        for q in range(per):
            gf_out[i * per + q] = rows[q * lr : (q + 1) * lr]

    def phase_filter_rows():
        loop(ctx_n, filter_rows)

    phase_filter_rows()
    others(dp_n, dp, lambda to: gf_copy(to).start())
    pltpu.make_async_copy(gf_out.at[dp], gf_in.at[dp], gf_recv.at[dp]).start()

    def gz_idft(i):
        s, j = lax.div(i, 4), lax.rem(i, 4)
        conv[s, j] = dot(inv[j], wbuf[s, j])

    def phase_gz_idft():
        loop(8, gz_idft)

    phase_gz_idft()

    def phase_grad():
        for h in halves:
            f = [[taps[r, i : i + 1, h] for i in range(3)] for r in range(3)]

            def grad(s, h=h, f=f):
                def step(i, carry):
                    p = ctx_n - 1 - i
                    rows = chunk(p, bs)
                    lines = [[], [], []]
                    for j in range(4):
                        gz = conv[s, j, rows, h].astype(BF).astype(F32)
                        gs = [gq[s, j, rows, h], gz * uv[s, j, rows, h], gz * uk[s, j, rows, h]]
                        for tap in range(3):
                            lines[tap].append(f[0][tap] * gs[0] + f[1][tap] * gs[1] + f[2][tap] * gs[2])
                    turned = [pltpu.roll(v, bs - 1, 0) for v in (lines[1][0], lines[2][0], lines[2][1])]
                    early = [jnp.where(row16 == bs - 1, carry[q], turned[q]) for q in range(3)]
                    once = lines[1][1:] + [early[0]]
                    twice = lines[2][2:] + [early[1], early[2]]
                    for j in range(4):
                        gx[s, p, j, :, h] = (lines[0][j] + once[j] + twice[j]).astype(BF)
                    return tuple(turned)

                zero = jnp.zeros((bs, LANES), F32)
                lax.fori_loop(0, ctx_n, step, (zero, zero, zero))

            loop(2, grad)

    phase_grad()

    def phase_scatter():
        ge_out[...] = dot(lookups[...], gx[...].reshape(pair_n * block, cw)).astype(BF)

    phase_scatter()
    others(dp_n, dp, lambda to: ge_copy(to).start())
    pltpu.make_async_copy(ge_out.at[chunk(dp, vr)], ge_in.at[dp], ge_recv.at[dp]).start()

    loop(dp_n, lambda i: arrived(gf_in.at[i], gf_recv.at[i]))
    for q in range(2):
        total = gf_in[q].astype(F32)
        for i in range(1, dp_n // 2):
            total = total + gf_in[2 * i + q].astype(F32)
        gf_ref[:, q * cw : (q + 1) * cw] = total
    loop(dp_n, lambda i: arrived(ge_in.at[i], ge_recv.at[i]))
    for q in range(2):
        total = ge_in[q].astype(F32)
        for i in range(1, dp_n // 2):
            total = total + ge_in[2 * i + q].astype(F32)
        ge_ref[:, q * cw : (q + 1) * cw] = total

    def mixed_arrived(i):
        s, p = lax.div(i, ctx_n), lax.rem(i, ctx_n)
        arrived(mixed_hbm.at[0, :, chunk(2 * p + s, cw)], mix_recv.at[i])

    loop(pair_n, mixed_arrived)

    def pair_sent(to):
        ids_copy(to).wait_send()
        cot_copy(to).wait_send()
        mix_copy(to).wait_send()

    def dp_sent(to):
        lf_copy(to).wait_send()
        gf_copy(to).wait_send()
        ge_copy(to).wait_send()

    others(pair_n, pair_me, pair_sent)
    others(dp_n, dp, dp_sent)


def collect(mixed_raw, ge_raw, gf_raw, mixed, ge, gf, mixed_vmem, ge_vmem, gf_vmem, in_sem, out_sem):
    rows = mixed.shape[1] // 4
    moves = [[ref.at[:, pl.ds(i * rows, rows)] for ref in (mixed_raw, mixed_vmem, mixed)] for i in range(4)]
    moves += [[ge_raw, ge_vmem, ge], [gf_raw, gf_vmem, gf]]
    ins = [pltpu.make_async_copy(a, b, in_sem.at[i]) for i, (a, b, _) in enumerate(moves)]
    outs = [pltpu.make_async_copy(b, c, out_sem.at[i]) for i, (_, b, c) in enumerate(moves)]
    for load in ins:
        load.start()
    for load, store in zip(ins, outs):
        load.wait()
        store.start()
    for store in outs:
        store.wait()


def body(token_ids, embedding, short_filter, long_filter, cotangent):
    vocab, width = embedding.shape
    dp_n, ctx_n = lax.axis_size("dp"), lax.axis_size("ctx")
    part = width // ctx_n
    block = token_ids.shape[1]
    length = block * ctx_n
    cw, sub, bs, pair_n = part // 2, length // 4, block // 4, 2 * ctx_n
    lr, vr = length // dp_n, vocab // dp_n
    fwd, inv, perm = tables(length, block)
    hbm = pl.BlockSpec(memory_space=pl.ANY)
    vmem = pl.BlockSpec(memory_space=pltpu.VMEM)
    dma = pltpu.SemaphoreType.DMA
    results = pl.pallas_call(
        functools.partial(kernel, (dp_n, ctx_n, vocab, part, block)),
        out_shape=[
            jax.ShapeDtypeStruct((1, block, width), BF),
            jax.ShapeDtypeStruct((vr, part), F32),
            jax.ShapeDtypeStruct((lr, part), F32),
        ],
        in_specs=[vmem, vmem, hbm, hbm, hbm, hbm, hbm, hbm],
        out_specs=[hbm, vmem, vmem],
        scratch_shapes=[
            pltpu.VMEM((8, block), F32),
            pltpu.VMEM((pair_n, 8, block), F32),
            pltpu.VMEM((vocab, cw), BF),
            pltpu.VMEM((3, 3, cw), F32),
            pltpu.VMEM((dp_n, lr, cw), BF),
            pltpu.VMEM((pair_n, block, cw), BF),
            pltpu.VMEM(fwd.shape, BF),
            pltpu.VMEM(inv.shape, BF),
            pltpu.VMEM((2, 4, sub, cw), F32),
            pltpu.VMEM((2, 4, sub, cw), F32),
            pltpu.VMEM((2, 4, sub, cw), F32),
            pltpu.VMEM((2, 4, sub, cw), F32),
            pltpu.VMEM((2, 4, sub, cw), BF),
            pltpu.VMEM((4, sub, cw), BF),
            pltpu.VMEM((4, 2, sub, cw), F32),
            pltpu.VMEM((2, 4, 2, sub, cw), F32),
            pltpu.VMEM((2, 4, 2 * sub, cw), F32),
            pltpu.VMEM((2, 4, 2 * sub, cw), BF),
            pltpu.VMEM((4, 2 * sub, cw), BF),
            pltpu.VMEM((2, 4, sub, cw), F32),
            pltpu.VMEM((2, 4, sub, cw), F32),
            pltpu.VMEM((2, ctx_n, 4, bs, cw), BF),
            pltpu.VMEM((pair_n * block, vocab), BF),
            pltpu.VMEM((vocab, pair_n * block), BF),
            pltpu.VMEM((pair_n, block, cw), BF),
            pltpu.VMEM((dp_n, lr, cw), BF),
            pltpu.VMEM((dp_n, lr, cw), BF),
            pltpu.VMEM((vocab, cw), BF),
            pltpu.VMEM((dp_n, vr, cw), BF),
            dma((4,)),
            dma((pair_n,)), dma((pair_n,)),
            dma((dp_n,)), dma((dp_n,)),
            dma((pair_n,)), dma((pair_n,)),
            dma((pair_n,)), dma((pair_n,)),
            dma((dp_n,)), dma((dp_n,)),
            dma((dp_n,)), dma((dp_n,)),
        ],
        compiler_params=pltpu.CompilerParams(
            collective_id=0, has_side_effects=True, vmem_limit_bytes=56 * 1024 * 1024
        ),
        name="hyena",
    )(token_ids, perm, embedding, short_filter, long_filter, cotangent, fwd, inv)
    return pl.pallas_call(
        collect,
        out_shape=[jax.ShapeDtypeStruct(r.shape, r.dtype) for r in results],
        in_specs=[hbm] * 3,
        out_specs=[hbm] * 3,
        scratch_shapes=[pltpu.VMEM(r.shape, r.dtype) for r in results] + [dma((6,)), dma((6,))],
        compiler_params=pltpu.CompilerParams(vmem_limit_bytes=56 * 1024 * 1024),
        name="collect",
    )(*results)


def solution(mesh):
    in_specs = (P("dp", "ctx"), P(), P(), P("dp", "ctx"), P("dp", "ctx", None))
    out_specs = (P("dp", "ctx", None), P("dp", "ctx"), P("dp", "ctx"))
    return jax.shard_map(body, mesh=mesh, in_specs=in_specs, out_specs=out_specs, check_vma=False)
```

```python
import functools
import math

import jax
import jax.numpy as jnp
import numpy as np
from jax import lax
from jax.experimental import pallas as pl
from jax.experimental.pallas import tpu as pltpu
from jax.sharding import PartitionSpec as P

BF = jnp.bfloat16
F32 = jnp.float32
MESH = pl.DeviceIdType.MESH
LANES = 128
KC = 16


def tables(length, block):
    sub = length // 4
    k = np.arange(sub)[None, :, None]
    t = 4 * np.arange(sub)[None, None, :] + np.arange(4)[:, None, None]
    angle = 2.0 * math.pi * (((4 * k + 1) * t) % (4 * length)) / (4 * length)
    fwd = np.concatenate([np.cos(angle), -np.sin(angle)], 1)
    inv = fwd.transpose(0, 2, 1) / length
    out = np.arange(block)
    perm = np.zeros((2, block, block))
    perm[0, out, 4 * (out % (block // 4)) + out // (block // 4)] = 1.0
    perm[1] = perm[0].T
    return jnp.asarray(fwd, BF), jnp.asarray(inv, BF), jnp.asarray(perm, BF)


def radix4(re, im, sign):
    a_re, a_im, b_re, b_im = re[0] + re[2], im[0] + im[2], re[0] - re[2], im[0] - im[2]
    c_re, c_im, d_re, d_im = re[1] + re[3], im[1] + im[3], re[1] - re[3], im[1] - im[3]
    if sign > 0:
        d_re, d_im = -d_re, -d_im
    return (
        [a_re + c_re, b_re + d_im, a_re - c_re, b_re - d_im],
        [a_im + c_im, b_im - d_re, a_im - c_im, b_im + d_re],
    )


def loop(count, step, unroll=1):
    def run(i, carry):
        for q in range(unroll):
            step(i * unroll + q)
        return carry

    lax.fori_loop(0, count // unroll, run, 0)


def dot(a, b):
    return jnp.dot(a, b, preferred_element_type=F32)


def kernel(
    dims,
    ids_ref, perm, emb_hbm, taps_hbm, lf_hbm, cot_hbm, fwd_hbm, inv_hbm,
    mixed_hbm, ge_ref, gf_ref,
    ids_mine, ids_in, emb, taps, lf_in, cot_in, fwd, inv,
    x, uq, uk, uv, field, hfield, spec_h, spec_z, pbuf, wbuf, wf, conv, gq, gx,
    onehot, lookups, mixed_out, gf_out, gf_in, gf_mid, gf_end, ge_out, ge_in, ge_mid, ge_end,
    local_sem, ids_send, ids_recv, cot_send, cot_recv, mix_send, mix_recv, quad_send, quad_recv, ring_send, ring_recv,
):
    dp_n, ctx_n, vocab, part, block = dims
    cw = part // 2
    sub = ctx_n * block // 4
    bs = block // 4
    pair_n = 2 * ctx_n
    per = dp_n // ctx_n
    lr = block // per
    vr = vocab // dp_n
    dp = lax.axis_index("dp")
    p_me = lax.axis_index("ctx")
    g = lax.div(dp, 2)
    c_me = lax.rem(dp, 2)
    ring_n = dp_n // 4
    y_me, z_me = lax.div(g, ring_n), lax.rem(g, ring_n)
    quad_me = 2 * y_me + c_me
    pair_me = c_me * ctx_n + p_me
    first = pl.multiple_of(p_me * part + c_me * cw, cw)
    halves = [pl.ds(h * LANES, LANES) for h in range(cw // LANES)]

    def chunk(i, size):
        return pl.ds(pl.multiple_of(i * size, size), size)

    loads = [
        pltpu.make_async_copy(emb_hbm.at[:, pl.ds(first, cw)], emb, local_sem.at[0]),
        pltpu.make_async_copy(taps_hbm.at[:, :, pl.ds(first, cw)], taps, local_sem.at[1]),
        pltpu.make_async_copy(fwd_hbm, fwd, local_sem.at[2]),
        pltpu.make_async_copy(inv_hbm, inv, local_sem.at[3]),
    ]
    for load in loads:
        load.start()

    ids = jnp.broadcast_to(ids_ref[...].astype(F32), (8, block))
    high = jnp.where(ids >= 256.0, 1.0, 0.0)
    low = ids - 256.0 * high
    ids_mine[...] = dot(low.astype(BF), perm[1]) + 256.0 * dot(high.astype(BF), perm[1])

    barrier = pltpu.get_barrier_semaphore()

    def greet_pair(i):
        to = lax.rem(pair_me + 1 + i, pair_n)
        device = (2 * g + lax.div(to, ctx_n), lax.rem(to, ctx_n))
        pl.semaphore_signal(barrier, inc=1, device_id=device, device_id_type=MESH)

    def quad_device(to):
        return ((lax.div(to, 2) * ring_n + z_me) * 2 + lax.rem(to, 2), p_me)

    def ring_device(to):
        return ((y_me * ring_n + to) * 2 + c_me, p_me)

    def greet_quad(i):
        device = quad_device(lax.rem(quad_me + 1 + i, 4))
        pl.semaphore_signal(barrier, inc=1, device_id=device, device_id_type=MESH)

    def greet_ring(i):
        device = ring_device(lax.rem(z_me + 1 + i, ring_n))
        pl.semaphore_signal(barrier, inc=1, device_id=device, device_id_type=MESH)

    loop(pair_n - 1, greet_pair)
    loop(3, greet_quad)
    loop(ring_n - 1, greet_ring)
    pl.semaphore_wait(barrier, pair_n - 1 + 3 + ring_n - 1)

    def ids_copy(to):
        return pltpu.make_async_remote_copy(
            src_ref=ids_mine, dst_ref=ids_in.at[pair_me], send_sem=ids_send.at[to], recv_sem=ids_recv.at[pair_me],
            device_id=(2 * g + lax.div(to, ctx_n), lax.rem(to, ctx_n)), device_id_type=MESH,
        )

    def quad_copy(kind, to):
        src = (lf_hbm.at[:, chunk(lax.rem(to, 2), cw)], gf_mid.at[to], ge_mid.at[to])[kind]
        dst = (lf_in.at[y_me, z_me, c_me], gf_end.at[quad_me], ge_end.at[quad_me])[kind]
        return pltpu.make_async_remote_copy(
            src_ref=src, dst_ref=dst, send_sem=quad_send.at[kind, to], recv_sem=quad_recv.at[kind, quad_me],
            device_id=quad_device(to), device_id_type=MESH,
        )

    def ring_copy(kind, to):
        src = (lf_in.at[:, z_me], gf_out.at[:, to], ge_out.at[:, to])[kind]
        dst = (lf_in.at[:, z_me], gf_in.at[z_me], ge_in.at[z_me])[kind]
        return pltpu.make_async_remote_copy(
            src_ref=src, dst_ref=dst, send_sem=ring_send.at[kind, to], recv_sem=ring_recv.at[kind, z_me],
            device_id=ring_device(to), device_id_type=MESH,
        )

    def cot_columns(to):
        return cot_hbm.at[0, :, chunk(2 * lax.rem(to, ctx_n) + lax.div(to, ctx_n), cw)]

    def cot_copy(to):
        return pltpu.make_async_remote_copy(
            src_ref=cot_columns(to), dst_ref=cot_in.at[pair_me], send_sem=cot_send.at[to], recv_sem=cot_recv.at[pair_me],
            device_id=(2 * g + lax.div(to, ctx_n), lax.rem(to, ctx_n)), device_id_type=MESH,
        )

    def mix_copy(to):
        return pltpu.make_async_remote_copy(
            src_ref=mixed_out.at[to], dst_ref=mixed_hbm.at[0, :, pl.ds(first, cw)],
            send_sem=mix_send.at[to], recv_sem=mix_recv.at[pair_me],
            device_id=(2 * g + lax.div(to, ctx_n), lax.rem(to, ctx_n)), device_id_type=MESH,
        )

    def others(count, me, step):
        loop(count - 1, lambda i: step(lax.rem(me + 1 + i, count)))

    def arrived(slot, sem):
        pltpu.make_async_copy(slot, slot, sem).wait()

    pltpu.make_async_copy(ids_mine, ids_in.at[pair_me], ids_recv.at[pair_me]).start()
    pltpu.make_async_copy(lf_hbm.at[:, chunk(c_me, cw)], lf_in.at[y_me, z_me, c_me], quad_recv.at[0, quad_me]).start()
    pltpu.make_async_copy(cot_columns(pair_me), cot_in.at[pair_me], cot_recv.at[pair_me]).start()
    others(pair_n, pair_me, lambda to: ids_copy(to).start())
    others(4, quad_me, lambda to: quad_copy(0, to).start())
    loop(4, lambda i: arrived(lf_in.at[lax.div(i, 2), z_me, lax.rem(i, 2)], quad_recv.at[0, i]))
    others(ring_n, z_me, lambda to: ring_copy(0, to).start())
    others(pair_n, pair_me, lambda to: cot_copy(to).start())

    loads[0].wait()
    loads[1].wait()
    vocab_lane = lax.broadcasted_iota(jnp.int32, (block, LANES), 1).astype(F32)

    def phase_lookup():
        def lookup(i):
            for k in range(4):
                arrived(ids_in.at[4 * i + k], ids_recv.at[4 * i + k])
            rows = [jnp.broadcast_to(ids_in[4 * i + k, 0:1, :], (block, block)) for k in range(4)]
            columns = [jnp.transpose(row) for row in rows]
            for k in range(4):
                for q in range(vocab // LANES):
                    onehot[chunk(4 * i + k, block), q * LANES : (q + 1) * LANES] = (
                        (columns[k] == vocab_lane + float(q * LANES)).astype(F32).astype(BF)
                    )

        loop(pair_n // 4, lookup)

    def phase_embed():
        def embed(i):
            rows = dot(onehot[chunk(i, 4 * block), :], emb[...])
            for q in range(4):
                s, p = lax.div(4 * i + q, ctx_n), lax.rem(4 * i + q, ctx_n)
                for j in range(4):
                    x[s, j, chunk(p, bs), :] = rows[q * block + j * bs : q * block + (j + 1) * bs]

        loop(pair_n // 4, embed)

    phase_lookup()
    phase_embed()

    row16 = lax.broadcasted_iota(jnp.int32, (bs, LANES), 0)
    def phase_short():
        for h in halves:
            f = [[taps[r, i : i + 1, h] for i in range(3)] for r in range(3)]

            def short(s, h=h, f=f):
                def step(p, carry):
                    rows = chunk(p, bs)
                    xs = [x[s, j, rows, h] for j in range(4)]
                    turned = [pltpu.roll(xs[2], 1, 0), pltpu.roll(xs[3], 1, 0)]
                    late = [jnp.where(row16 == 0, carry[q], turned[q]) for q in range(2)]
                    line = late + xs
                    us = [
                        [f[r][0] * line[j + 2] + f[r][1] * line[j + 1] + f[r][2] * line[j] for j in range(4)]
                        for r in range(3)
                    ]
                    for j in range(4):
                        uq[s, j, rows, h] = us[0][j]
                        uk[s, j, rows, h] = us[1][j]
                        uv[s, j, rows, h] = us[2][j]
                        field[s, j, rows, h] = (us[1][j] * us[2][j]).astype(BF)
                    return tuple(turned)

                zero = jnp.zeros((bs, LANES), F32)
                lax.fori_loop(0, ctx_n, step, (zero, zero))

            loop(2, short)

    phase_short()

    loads[2].wait()

    def phase_taps():
        def gather_taps(i):
            outs = []
            for k in range(2):
                pieces = [(2 * i + k) * per + q for q in range(per)]
                rows = [lf_in[lax.div(d, 2 * ring_n), lax.rem(lax.div(d, 2), ring_n), lax.rem(d, 2)] for d in pieces]
                outs.append(dot(perm[0], jnp.concatenate(rows, 0)).astype(BF))
            for k in range(2):
                for j in range(4):
                    hfield[j, chunk(2 * i + k, bs), :] = outs[k][j * bs : (j + 1) * bs]

        others(ring_n, z_me, lambda i: arrived(lf_in.at[:, i], ring_recv.at[0, i]))
        loop(ctx_n // 2, gather_taps)

    phase_taps()

    def filter_dft(j):
        pbuf[0, j] = dot(fwd[j], hfield[j])

    def phase_filter_dft():
        loop(4, filter_dft, 4)

    phase_filter_dft()

    def butterfly(s, i, h):
        re = [pbuf[s, j, chunk(i, KC), h] for j in range(4)]
        im = [pbuf[s, j, pl.ds(pl.multiple_of(sub + i * KC, KC), KC), h] for j in range(4)]
        return radix4(re, im, -1)

    def filter_mix(i):
        for h in halves:
            re, im = butterfly(0, i, h)
            for m in range(4):
                spec_h[m, 0, chunk(i, KC), h] = re[m]
                spec_h[m, 1, chunk(i, KC), h] = im[m]

    def phase_filter_mix():
        loop(sub // KC, filter_mix)

    phase_filter_mix()

    def field_dft(i):
        s, j = lax.div(i, 4), lax.rem(i, 4)
        pbuf[s, j] = dot(fwd[j], field[s, j])

    def put(ref, i, h, re, im):
        re, im = radix4(re, im, 1)
        for j in range(4):
            ref[j, chunk(i, KC), h] = re[j].astype(BF)
            ref[j, pl.ds(pl.multiple_of(sub + i * KC, KC), KC), h] = im[j].astype(BF)

    def phase_field_dft():
        loop(8, field_dft, 4)

    phase_field_dft()
    loads[3].wait()

    for s in range(2):

        def conv_mix(i, s=s):
            for h in halves:
                re, im = butterfly(s, i, h)
                out_re, out_im = [], []
                for m in range(4):
                    spec_z[s, m, 0, chunk(i, KC), h] = re[m]
                    spec_z[s, m, 1, chunk(i, KC), h] = im[m]
                    h_re, h_im = spec_h[m, 0, chunk(i, KC), h], spec_h[m, 1, chunk(i, KC), h]
                    out_re.append(re[m] * h_re - im[m] * h_im)
                    out_im.append(re[m] * h_im + im[m] * h_re)
                put(wbuf.at[s], i, h, out_re, out_im)

        def phase_conv_mix():
            loop(sub // KC, conv_mix)

        phase_conv_mix()

        def conv_idft(j, s=s):
            conv[s, j] = dot(inv[j], wbuf[s, j]).astype(BF).astype(F32)

        def phase_conv_idft():
            loop(4, conv_idft, 4)

        phase_conv_idft()

        def mix(i, s=s):
            outs = []
            for k in range(2):
                p = lax.rem(p_me + 1 + 2 * i + k, ctx_n)
                rows = chunk(p, bs)
                out = jnp.concatenate([(uq[s, j, rows, :] * conv[s, j, rows, :]).astype(BF) for j in range(4)], 0)
                outs.append((s * ctx_n + p, dot(perm[1], out).astype(BF)))
            for to, out in outs:
                mixed_out[to] = out
            for to, _ in outs:

                @pl.when(to != pair_me)
                def _():
                    mix_copy(to).start()

                @pl.when(to == pair_me)
                def _():
                    pltpu.make_async_copy(
                        mixed_out.at[to], mixed_hbm.at[0, :, pl.ds(first, cw)], mix_recv.at[pair_me]
                    ).start()

        def phase_mix():
            loop(ctx_n // 2, mix)

        phase_mix()

    vocab_row = lax.broadcasted_iota(jnp.int32, (vocab, block), 0).astype(F32)

    def phase_lookup_rows():
        def lookup(i):
            lookups[:, chunk(i, block)] = (vocab_row == ids_in[i, 0:1, :]).astype(F32).astype(BF)

        loop(pair_n, lookup)

    def take(i):
        for k in range(4):
            arrived(cot_in.at[4 * i + k], cot_recv.at[4 * i + k])
        outs = [dot(perm[0], cot_in[4 * i + k]) for k in range(4)]
        for k in range(4):
            s, p = lax.div(4 * i + k, ctx_n), lax.rem(4 * i + k, ctx_n)
            rows = chunk(p, bs)
            for j in range(4):
                piece = outs[k][j * bs : (j + 1) * bs]
                field[s, j, rows, :] = (piece * uq[s, j, rows, :]).astype(BF)
                gq[s, j, rows, :] = piece * conv[s, j, rows, :]

    def phase_take():
        loop(pair_n // 4, take)

    phase_lookup_rows()
    phase_take()
    phase_field_dft()

    def back_mix(i):
        for h in halves:
            sum_re, sum_im = None, None
            for s in range(2):
                re, im = butterfly(s, i, h)
                out_re, out_im, f_re, f_im = [], [], [], []
                for m in range(4):
                    h_re, h_im = spec_h[m, 0, chunk(i, KC), h], spec_h[m, 1, chunk(i, KC), h]
                    z_re, z_im = spec_z[s, m, 0, chunk(i, KC), h], spec_z[s, m, 1, chunk(i, KC), h]
                    out_re.append(re[m] * h_re + im[m] * h_im)
                    out_im.append(im[m] * h_re - re[m] * h_im)
                    f_re.append(re[m] * z_re + im[m] * z_im)
                    f_im.append(im[m] * z_re - re[m] * z_im)
                put(wbuf.at[s], i, h, out_re, out_im)
                if s == 0:
                    sum_re, sum_im = f_re, f_im
                else:
                    sum_re = [a + b for a, b in zip(sum_re, f_re)]
                    sum_im = [a + b for a, b in zip(sum_im, f_im)]
            put(wf, i, h, sum_re, sum_im)

    def phase_back_mix():
        loop(sub // KC, back_mix)

    phase_back_mix()

    def filter_idft(j):
        hfield[j] = dot(inv[j], wf[j]).astype(BF)

    def phase_filter_idft():
        loop(4, filter_idft, 4)

    phase_filter_idft()

    def filter_rows(i):
        outs = []
        for k in range(2):
            rows = jnp.concatenate([hfield[j, chunk(2 * i + k, bs), :] for j in range(4)], 0)
            outs.append(dot(perm[1], rows).astype(BF))
        for k in range(2):
            for q in range(per):
                d = (2 * i + k) * per + q
                gf_out[lax.div(d, 2 * ring_n), lax.rem(lax.div(d, 2), ring_n), lax.rem(d, 2)] = outs[k][q * lr : (q + 1) * lr]

    def phase_filter_rows():
        loop(ctx_n // 2, filter_rows)

    phase_filter_rows()
    others(ring_n, z_me, lambda to: ring_copy(1, to).start())

    def ring_sum(kind, out, arrivals, mid, end):
        others(ring_n, z_me, lambda i: arrived(arrivals.at[i], ring_recv.at[kind, i]))
        for q in range(4):
            total = out[q // 2, z_me, q % 2].astype(F32)
            for i in range(1, ring_n):
                total = total + arrivals[lax.rem(z_me + i, ring_n), q // 2, q % 2].astype(F32)
            mid[q] = total.astype(BF)
        end[quad_me] = mid[quad_me]
        others(4, quad_me, lambda to: quad_copy(kind, to).start())

    def quad_sum(kind, end, result):
        others(4, quad_me, lambda i: arrived(end.at[i], quad_recv.at[kind, i]))
        for c in range(2):
            result[:, c * cw : (c + 1) * cw] = end[c].astype(F32) + end[2 + c].astype(F32)

    def gz_idft(i):
        s, j = lax.div(i, 4), lax.rem(i, 4)
        conv[s, j] = dot(inv[j], wbuf[s, j])

    def phase_gz_idft():
        loop(8, gz_idft, 4)

    phase_gz_idft()

    def phase_grad():
        for h in halves:
            f = [[taps[r, i : i + 1, h] for i in range(3)] for r in range(3)]

            def grad(s, h=h, f=f):
                def step(i, carry):
                    p = ctx_n - 1 - i
                    rows = chunk(p, bs)
                    lines = [[], [], []]
                    for j in range(4):
                        gz = conv[s, j, rows, h].astype(BF).astype(F32)
                        gs = [gq[s, j, rows, h], gz * uv[s, j, rows, h], gz * uk[s, j, rows, h]]
                        for tap in range(3):
                            lines[tap].append(f[0][tap] * gs[0] + f[1][tap] * gs[1] + f[2][tap] * gs[2])
                    turned = [pltpu.roll(v, bs - 1, 0) for v in (lines[1][0], lines[2][0], lines[2][1])]
                    early = [jnp.where(row16 == bs - 1, carry[q], turned[q]) for q in range(3)]
                    once = lines[1][1:] + [early[0]]
                    twice = lines[2][2:] + [early[1], early[2]]
                    for j in range(4):
                        gx[s, p, j, :, h] = (lines[0][j] + once[j] + twice[j]).astype(BF)
                    return tuple(turned)

                zero = jnp.zeros((bs, LANES), F32)
                lax.fori_loop(0, ctx_n, step, (zero, zero, zero))

            loop(2, grad)

    phase_grad()

    ring_sum(1, gf_out, gf_in, gf_mid, gf_end)

    def phase_scatter():
        ge_out[...] = dot(lookups[...], gx[...].reshape(pair_n * block, cw)).astype(BF).reshape(ge_out.shape)

    phase_scatter()
    others(ring_n, z_me, lambda to: ring_copy(2, to).start())

    quad_sum(1, gf_end, gf_ref)
    ring_sum(2, ge_out, ge_in, ge_mid, ge_end)
    quad_sum(2, ge_end, ge_ref)

    def mixed_arrived(i):
        s, p = lax.div(i, ctx_n), lax.rem(i, ctx_n)
        arrived(mixed_hbm.at[0, :, chunk(2 * p + s, cw)], mix_recv.at[i])

    loop(pair_n, mixed_arrived)

    def pair_sent(to):
        ids_copy(to).wait_send()
        cot_copy(to).wait_send()
        mix_copy(to).wait_send()

    def quad_sent(to):
        for kind in range(3):
            quad_copy(kind, to).wait_send()

    def ring_sent(to):
        for kind in range(3):
            ring_copy(kind, to).wait_send()

    others(pair_n, pair_me, pair_sent)
    others(4, quad_me, quad_sent)
    others(ring_n, z_me, ring_sent)


def collect(mixed_raw, ge_raw, gf_raw, mixed, ge, gf, mixed_vmem, ge_vmem, gf_vmem, in_sem, out_sem):
    rows = mixed.shape[1] // 4
    moves = [[ref.at[:, pl.ds(i * rows, rows)] for ref in (mixed_raw, mixed_vmem, mixed)] for i in range(4)]
    moves += [[ge_raw, ge_vmem, ge], [gf_raw, gf_vmem, gf]]
    ins = [pltpu.make_async_copy(a, b, in_sem.at[i]) for i, (a, b, _) in enumerate(moves)]
    outs = [pltpu.make_async_copy(b, c, out_sem.at[i]) for i, (_, b, c) in enumerate(moves)]
    for load in ins:
        load.start()
    for load, store in zip(ins, outs):
        load.wait()
        store.start()
    for store in outs:
        store.wait()


def body(token_ids, embedding, short_filter, long_filter, cotangent):
    vocab, width = embedding.shape
    dp_n, ctx_n = lax.axis_size("dp"), lax.axis_size("ctx")
    part = width // ctx_n
    block = token_ids.shape[1]
    length = block * ctx_n
    cw, sub, bs, pair_n = part // 2, length // 4, block // 4, 2 * ctx_n
    lr, vr, ring_n = length // dp_n, vocab // dp_n, dp_n // 4
    fwd, inv, perm = tables(length, block)
    hbm = pl.BlockSpec(memory_space=pl.ANY)
    vmem = pl.BlockSpec(memory_space=pltpu.VMEM)
    dma = pltpu.SemaphoreType.DMA
    results = pl.pallas_call(
        functools.partial(kernel, (dp_n, ctx_n, vocab, part, block)),
        out_shape=[
            jax.ShapeDtypeStruct((1, block, width), BF),
            jax.ShapeDtypeStruct((vr, part), F32),
            jax.ShapeDtypeStruct((lr, part), F32),
        ],
        in_specs=[vmem, vmem, hbm, hbm, hbm, hbm, hbm, hbm],
        out_specs=[hbm, vmem, vmem],
        scratch_shapes=[
            pltpu.VMEM((8, block), F32),
            pltpu.VMEM((pair_n, 8, block), F32),
            pltpu.VMEM((vocab, cw), BF),
            pltpu.VMEM((3, 3, cw), F32),
            pltpu.VMEM((2, ring_n, 2, lr, cw), BF),
            pltpu.VMEM((pair_n, block, cw), BF),
            pltpu.VMEM(fwd.shape, BF),
            pltpu.VMEM(inv.shape, BF),
            pltpu.VMEM((2, 4, sub, cw), F32),
            pltpu.VMEM((2, 4, sub, cw), F32),
            pltpu.VMEM((2, 4, sub, cw), F32),
            pltpu.VMEM((2, 4, sub, cw), F32),
            pltpu.VMEM((2, 4, sub, cw), BF),
            pltpu.VMEM((4, sub, cw), BF),
            pltpu.VMEM((4, 2, sub, cw), F32),
            pltpu.VMEM((2, 4, 2, sub, cw), F32),
            pltpu.VMEM((2, 4, 2 * sub, cw), F32),
            pltpu.VMEM((2, 4, 2 * sub, cw), BF),
            pltpu.VMEM((4, 2 * sub, cw), BF),
            pltpu.VMEM((2, 4, sub, cw), F32),
            pltpu.VMEM((2, 4, sub, cw), F32),
            pltpu.VMEM((2, ctx_n, 4, bs, cw), BF),
            pltpu.VMEM((pair_n * block, vocab), BF),
            pltpu.VMEM((vocab, pair_n * block), BF),
            pltpu.VMEM((pair_n, block, cw), BF),
            pltpu.VMEM((2, ring_n, 2, lr, cw), BF),
            pltpu.VMEM((ring_n, 2, 2, lr, cw), BF),
            pltpu.VMEM((4, lr, cw), BF),
            pltpu.VMEM((4, lr, cw), BF),
            pltpu.VMEM((2, ring_n, 2, vr, cw), BF),
            pltpu.VMEM((ring_n, 2, 2, vr, cw), BF),
            pltpu.VMEM((4, vr, cw), BF),
            pltpu.VMEM((4, vr, cw), BF),
            dma((4,)),
            dma((pair_n,)), dma((pair_n,)),
            dma((pair_n,)), dma((pair_n,)),
            dma((pair_n,)), dma((pair_n,)),
            dma((3, 4)), dma((3, 4)),
            dma((3, ring_n)), dma((3, ring_n)),
        ],
        compiler_params=pltpu.CompilerParams(
            collective_id=0, has_side_effects=True, vmem_limit_bytes=56 * 1024 * 1024
        ),
        name="hyena",
    )(token_ids, perm, embedding, short_filter, long_filter, cotangent, fwd, inv)
    return pl.pallas_call(
        collect,
        out_shape=[jax.ShapeDtypeStruct(r.shape, r.dtype) for r in results],
        in_specs=[hbm] * 3,
        out_specs=[hbm] * 3,
        scratch_shapes=[pltpu.VMEM(r.shape, r.dtype) for r in results] + [dma((6,)), dma((6,))],
        compiler_params=pltpu.CompilerParams(vmem_limit_bytes=56 * 1024 * 1024),
        name="collect",
    )(*results)


def solution(mesh):
    in_specs = (P("dp", "ctx"), P(), P(), P("dp", "ctx"), P("dp", "ctx", None))
    out_specs = (P("dp", "ctx", None), P("dp", "ctx"), P("dp", "ctx"))
    return jax.shard_map(body, mesh=mesh, in_specs=in_specs, out_specs=out_specs, check_vma=False)
```

```python
import functools
import math

import jax
import jax.numpy as jnp
import numpy as np
from jax import lax
from jax.experimental import pallas as pl
from jax.experimental.pallas import tpu as pltpu
from jax.sharding import PartitionSpec as P

BF = jnp.bfloat16
F32 = jnp.float32
MESH = pl.DeviceIdType.MESH
LANES = 128
KC = 16


def tables(length):
    sub = length // 4
    k = np.arange(sub)[None, :, None]
    t = 4 * np.arange(sub)[None, None, :] + np.arange(4)[:, None, None]
    angle = 2.0 * math.pi * (((4 * k + 1) * t) % (4 * length)) / (4 * length)
    fwd = np.concatenate([np.cos(angle), -np.sin(angle)], 1)
    inv = fwd.transpose(0, 2, 1) / length
    return jnp.asarray(fwd, BF), jnp.asarray(inv, BF)


def radix4(re, im, sign):
    a_re, a_im, b_re, b_im = re[0] + re[2], im[0] + im[2], re[0] - re[2], im[0] - im[2]
    c_re, c_im, d_re, d_im = re[1] + re[3], im[1] + im[3], re[1] - re[3], im[1] - im[3]
    if sign > 0:
        d_re, d_im = -d_re, -d_im
    return (
        [a_re + c_re, b_re + d_im, a_re - c_re, b_re - d_im],
        [a_im + c_im, b_im - d_re, a_im - c_im, b_im + d_re],
    )


def loop(count, step, unroll=1):
    def run(i, carry):
        for q in range(unroll):
            step(i * unroll + q)
        return carry

    lax.fori_loop(0, count // unroll, run, 0)


def dot(a, b):
    return jnp.dot(a, b, preferred_element_type=F32)


def kernel(
    dims,
    ids_hbm, emb_hbm, taps_hbm, lf_hbm, cot_hbm, fwd_hbm, inv_hbm,
    mixed_hbm, ge_ref, gf_ref,
    ids_raw, ids_mine, ids_in, perm, emb, taps, lf_in, cot_in, fwd, inv,
    x, uq, uk, uv, field, hfield, spec_h, spec_z, hbuf, pbuf, wbuf, wf, conv, gq, gx,
    onehot, lookups, mixed_out, gf_out, gf_in, gf_mid, gf_end, ge_out, ge_in,
    local_sem, ids_send, ids_recv, cot_send, cot_recv, mix_send, mix_recv, quad_send, quad_recv, ring_send, ring_recv,
    ge_send, ge_recv,
):
    dp_n, ctx_n, vocab, part, block = dims
    cw = part // 2
    sub = ctx_n * block // 4
    bs = block // 4
    pair_n = 2 * ctx_n
    per = dp_n // ctx_n
    lr = block // per
    vr = vocab // dp_n
    dp = lax.axis_index("dp")
    p_me = lax.axis_index("ctx")
    g = lax.div(dp, 2)
    c_me = lax.rem(dp, 2)
    ring_n = dp_n // 4
    y_me, z_me = lax.div(g, ring_n), lax.rem(g, ring_n)
    quad_me = 2 * y_me + c_me
    pair_me = c_me * ctx_n + p_me
    first = pl.multiple_of(p_me * part + c_me * cw, cw)
    halves = [pl.ds(h * LANES, LANES) for h in range(cw // LANES)]

    def chunk(i, size):
        return pl.ds(pl.multiple_of(i * size, size), size)

    loads = [
        pltpu.make_async_copy(emb_hbm.at[:, pl.ds(first, cw)], emb, local_sem.at[0]),
        pltpu.make_async_copy(taps_hbm.at[:, :, pl.ds(first, cw)], taps, local_sem.at[1]),
        pltpu.make_async_copy(fwd_hbm, fwd, local_sem.at[2]),
        pltpu.make_async_copy(inv_hbm, inv, local_sem.at[3]),
    ]
    load_ids = pltpu.make_async_copy(ids_hbm, ids_raw, local_sem.at[4])
    load_ids.start()
    for load in loads:
        load.start()

    barrier = pltpu.get_barrier_semaphore()

    def greet_pair(i):
        to = lax.rem(pair_me + 1 + i, pair_n)
        device = (2 * g + lax.div(to, ctx_n), lax.rem(to, ctx_n))
        pl.semaphore_signal(barrier, inc=1, device_id=device, device_id_type=MESH)

    def quad_device(to):
        return ((lax.div(to, 2) * ring_n + z_me) * 2 + lax.rem(to, 2), p_me)

    def ring_device(to):
        return ((y_me * ring_n + to) * 2 + c_me, p_me)

    def greet_dp(i):
        device = (lax.rem(dp + 1 + i, dp_n), p_me)
        pl.semaphore_signal(barrier, inc=1, device_id=device, device_id_type=MESH)

    loop(pair_n - 1, greet_pair)
    loop(dp_n - 1, greet_dp)
    def natural(axis):
        place = lax.broadcasted_iota(jnp.int32, (block, block), axis)
        return 4 * lax.rem(place, bs) + lax.div(place, bs)

    perm[0] = (natural(0) == lax.broadcasted_iota(jnp.int32, (block, block), 1)).astype(F32).astype(BF)
    perm[1] = (natural(1) == lax.broadcasted_iota(jnp.int32, (block, block), 0)).astype(F32).astype(BF)

    load_ids.wait()
    ids = jnp.broadcast_to(ids_raw[...].astype(F32), (8, block))
    high = jnp.where(ids >= 256.0, 1.0, 0.0)
    low = ids - 256.0 * high
    ids_mine[...] = dot(low.astype(BF), perm[1]) + 256.0 * dot(high.astype(BF), perm[1])
    pl.semaphore_wait(barrier, pair_n - 1 + dp_n - 1)

    def ids_copy(to):
        return pltpu.make_async_remote_copy(
            src_ref=ids_mine, dst_ref=ids_in.at[pair_me], send_sem=ids_send.at[to], recv_sem=ids_recv.at[pair_me],
            device_id=(2 * g + lax.div(to, ctx_n), lax.rem(to, ctx_n)), device_id_type=MESH,
        )

    def quad_copy(kind, to):
        src = (lf_hbm.at[:, chunk(lax.rem(to, 2), cw)], gf_mid.at[to])[kind]
        dst = (lf_in.at[y_me, z_me, c_me], gf_end.at[quad_me])[kind]
        return pltpu.make_async_remote_copy(
            src_ref=src, dst_ref=dst, send_sem=quad_send.at[kind, to], recv_sem=quad_recv.at[kind, quad_me],
            device_id=quad_device(to), device_id_type=MESH,
        )

    def ring_copy(kind, to):
        src = (lf_in.at[:, z_me], gf_out.at[:, to])[kind]
        dst = (lf_in.at[:, z_me], gf_in.at[z_me])[kind]
        return pltpu.make_async_remote_copy(
            src_ref=src, dst_ref=dst, send_sem=ring_send.at[kind, to], recv_sem=ring_recv.at[kind, z_me],
            device_id=ring_device(to), device_id_type=MESH,
        )

    def cot_columns(to):
        return cot_hbm.at[0, :, chunk(2 * lax.rem(to, ctx_n) + lax.div(to, ctx_n), cw)]

    def cot_copy(to):
        return pltpu.make_async_remote_copy(
            src_ref=cot_columns(to), dst_ref=cot_in.at[pair_me], send_sem=cot_send.at[to], recv_sem=cot_recv.at[pair_me],
            device_id=(2 * g + lax.div(to, ctx_n), lax.rem(to, ctx_n)), device_id_type=MESH,
        )

    def mix_copy(to):
        return pltpu.make_async_remote_copy(
            src_ref=mixed_out.at[to], dst_ref=mixed_hbm.at[0, :, pl.ds(first, cw)],
            send_sem=mix_send.at[to], recv_sem=mix_recv.at[pair_me],
            device_id=(2 * g + lax.div(to, ctx_n), lax.rem(to, ctx_n)), device_id_type=MESH,
        )

    def ge_copy(to):
        return pltpu.make_async_remote_copy(
            src_ref=ge_out.at[to], dst_ref=ge_in.at[dp], send_sem=ge_send.at[to], recv_sem=ge_recv.at[dp],
            device_id=(to, p_me), device_id_type=MESH,
        )

    def others(count, me, step):
        loop(count - 1, lambda i: step(lax.rem(me + 1 + i, count)))

    def arrived(slot, sem):
        pltpu.make_async_copy(slot, slot, sem).wait()

    pltpu.make_async_copy(ids_mine, ids_in.at[pair_me], ids_recv.at[pair_me]).start()
    pltpu.make_async_copy(lf_hbm.at[:, chunk(c_me, cw)], lf_in.at[y_me, z_me, c_me], quad_recv.at[0, quad_me]).start()
    pltpu.make_async_copy(cot_columns(pair_me), cot_in.at[pair_me], cot_recv.at[pair_me]).start()
    others(4, quad_me, lambda to: quad_copy(0, to).start())
    others(pair_n, pair_me, lambda to: ids_copy(to).start())
    loop(4, lambda i: arrived(lf_in.at[lax.div(i, 2), z_me, lax.rem(i, 2)], quad_recv.at[0, i]))
    others(ring_n, z_me, lambda to: ring_copy(0, to).start())
    others(pair_n, pair_me, lambda to: cot_copy(to).start())

    loads[0].wait()
    loads[1].wait()
    vocab_lane = lax.broadcasted_iota(jnp.int32, (block, LANES), 1).astype(F32)

    def phase_lookup():
        def lookup(i):
            for k in range(4):
                arrived(ids_in.at[4 * i + k], ids_recv.at[4 * i + k])
            rows = [jnp.broadcast_to(ids_in[4 * i + k, 0:1, :], (block, block)) for k in range(4)]
            columns = [jnp.transpose(row) for row in rows]
            for k in range(4):
                for q in range(vocab // LANES):
                    onehot[chunk(4 * i + k, block), q * LANES : (q + 1) * LANES] = (
                        (columns[k] == vocab_lane + float(q * LANES)).astype(F32).astype(BF)
                    )

        loop(pair_n // 4, lookup)

    def phase_embed():
        def embed(i):
            rows = dot(onehot[chunk(i, 4 * block), :], emb[...])
            for q in range(4):
                s, p = lax.div(4 * i + q, ctx_n), lax.rem(4 * i + q, ctx_n)
                for j in range(4):
                    x[s, j, chunk(p, bs), :] = rows[q * block + j * bs : q * block + (j + 1) * bs]

        loop(pair_n // 4, embed)

    phase_lookup()
    phase_embed()

    row16 = lax.broadcasted_iota(jnp.int32, (bs, LANES), 0)
    def phase_short():
        for h in halves:
            f = [[taps[r, i : i + 1, h] for i in range(3)] for r in range(3)]

            def short(s, h=h, f=f):
                def step(p, carry):
                    rows = chunk(p, bs)
                    xs = [x[s, j, rows, h] for j in range(4)]
                    turned = [pltpu.roll(xs[2], 1, 0), pltpu.roll(xs[3], 1, 0)]
                    late = [jnp.where(row16 == 0, carry[q], turned[q]) for q in range(2)]
                    line = late + xs
                    us = [
                        [f[r][0] * line[j + 2] + f[r][1] * line[j + 1] + f[r][2] * line[j] for j in range(4)]
                        for r in range(3)
                    ]
                    for j in range(4):
                        uq[s, j, rows, h] = us[0][j]
                        uk[s, j, rows, h] = us[1][j]
                        uv[s, j, rows, h] = us[2][j]
                        field[s, j, rows, h] = (us[1][j] * us[2][j]).astype(BF)
                    return tuple(turned)

                zero = jnp.zeros((bs, LANES), F32)
                lax.fori_loop(0, ctx_n, step, (zero, zero))

            loop(2, short)

    phase_short()

    loads[2].wait()

    def field_dft(i):
        s, j = lax.div(i, 4), lax.rem(i, 4)
        pbuf[s, j] = dot(fwd[j], field[s, j])

    def phase_field_dft():
        loop(8, field_dft, 4)

    phase_field_dft()

    vocab_row = lax.broadcasted_iota(jnp.int32, (vocab, block), 0).astype(F32)

    def phase_lookup_rows():
        def lookup(i):
            lookups[:, chunk(i, block)] = (vocab_row == ids_in[i, 0:1, :]).astype(F32).astype(BF)

        loop(pair_n, lookup)

    phase_lookup_rows()


    def phase_taps():
        def gather_taps(i):
            outs = []
            for k in range(2):
                pieces = [(2 * i + k) * per + q for q in range(per)]
                rows = [lf_in[lax.div(d, 2 * ring_n), lax.rem(lax.div(d, 2), ring_n), lax.rem(d, 2)] for d in pieces]
                outs.append(dot(perm[0], jnp.concatenate(rows, 0)).astype(BF))
            for k in range(2):
                for j in range(4):
                    hfield[j, chunk(2 * i + k, bs), :] = outs[k][j * bs : (j + 1) * bs]

        others(ring_n, z_me, lambda i: arrived(lf_in.at[:, i], ring_recv.at[0, i]))
        loop(ctx_n // 2, gather_taps)

    phase_taps()

    def filter_dft(j):
        hbuf[j] = dot(fwd[j], hfield[j])

    def phase_filter_dft():
        loop(4, filter_dft, 4)

    phase_filter_dft()

    def butterfly(ref, i, h):
        re = [ref[j, chunk(i, KC), h] for j in range(4)]
        im = [ref[j, pl.ds(pl.multiple_of(sub + i * KC, KC), KC), h] for j in range(4)]
        return radix4(re, im, -1)

    def filter_mix(i):
        for h in halves:
            re, im = butterfly(hbuf, i, h)
            for m in range(4):
                spec_h[m, 0, chunk(i, KC), h] = re[m]
                spec_h[m, 1, chunk(i, KC), h] = im[m]

    def phase_filter_mix():
        loop(sub // KC, filter_mix)

    phase_filter_mix()

    def put(ref, i, h, re, im):
        re, im = radix4(re, im, 1)
        for j in range(4):
            ref[j, chunk(i, KC), h] = re[j].astype(BF)
            ref[j, pl.ds(pl.multiple_of(sub + i * KC, KC), KC), h] = im[j].astype(BF)


    loads[3].wait()

    for s in range(2):

        def conv_mix(i, s=s):
            for h in halves:
                re, im = butterfly(pbuf.at[s], i, h)
                out_re, out_im = [], []
                for m in range(4):
                    spec_z[s, m, 0, chunk(i, KC), h] = re[m]
                    spec_z[s, m, 1, chunk(i, KC), h] = im[m]
                    h_re, h_im = spec_h[m, 0, chunk(i, KC), h], spec_h[m, 1, chunk(i, KC), h]
                    out_re.append(re[m] * h_re - im[m] * h_im)
                    out_im.append(re[m] * h_im + im[m] * h_re)
                put(wbuf.at[s], i, h, out_re, out_im)

        def phase_conv_mix():
            loop(sub // KC, conv_mix)

        phase_conv_mix()

        def conv_idft(j, s=s):
            conv[s, j] = dot(inv[j], wbuf[s, j]).astype(BF).astype(F32)

        def phase_conv_idft():
            loop(4, conv_idft, 4)

        phase_conv_idft()

        def mix(i, s=s):
            outs = []
            for k in range(2):
                p = lax.rem(p_me + 1 + 2 * i + k, ctx_n)
                rows = chunk(p, bs)
                out = jnp.concatenate([(uq[s, j, rows, :] * conv[s, j, rows, :]).astype(BF) for j in range(4)], 0)
                outs.append((s * ctx_n + p, dot(perm[1], out).astype(BF)))
            for to, out in outs:
                mixed_out[to] = out
            for to, _ in outs:

                @pl.when(to != pair_me)
                def _():
                    mix_copy(to).start()

                @pl.when(to == pair_me)
                def _():
                    pltpu.make_async_copy(
                        mixed_out.at[to], mixed_hbm.at[0, :, pl.ds(first, cw)], mix_recv.at[pair_me]
                    ).start()

        def phase_mix():
            loop(ctx_n // 2, mix)

        phase_mix()

    def take(i):
        for k in range(4):
            arrived(cot_in.at[4 * i + k], cot_recv.at[4 * i + k])
        outs = [dot(perm[0], cot_in[4 * i + k]) for k in range(4)]
        for k in range(4):
            s, p = lax.div(4 * i + k, ctx_n), lax.rem(4 * i + k, ctx_n)
            rows = chunk(p, bs)
            for j in range(4):
                piece = outs[k][j * bs : (j + 1) * bs]
                field[s, j, rows, :] = (piece * uq[s, j, rows, :]).astype(BF)
                gq[s, j, rows, :] = piece * conv[s, j, rows, :]

    def phase_take():
        loop(pair_n // 4, take)

    phase_take()
    phase_field_dft()

    def back_mix(i):
        for h in halves:
            sum_re, sum_im = None, None
            for s in range(2):
                re, im = butterfly(pbuf.at[s], i, h)
                out_re, out_im, f_re, f_im = [], [], [], []
                for m in range(4):
                    h_re, h_im = spec_h[m, 0, chunk(i, KC), h], spec_h[m, 1, chunk(i, KC), h]
                    z_re, z_im = spec_z[s, m, 0, chunk(i, KC), h], spec_z[s, m, 1, chunk(i, KC), h]
                    out_re.append(re[m] * h_re + im[m] * h_im)
                    out_im.append(im[m] * h_re - re[m] * h_im)
                    f_re.append(re[m] * z_re + im[m] * z_im)
                    f_im.append(im[m] * z_re - re[m] * z_im)
                put(wbuf.at[s], i, h, out_re, out_im)
                if s == 0:
                    sum_re, sum_im = f_re, f_im
                else:
                    sum_re = [a + b for a, b in zip(sum_re, f_re)]
                    sum_im = [a + b for a, b in zip(sum_im, f_im)]
            put(wf, i, h, sum_re, sum_im)

    def phase_back_mix():
        loop(sub // KC, back_mix)

    phase_back_mix()

    def filter_idft(j):
        hfield[j] = dot(inv[j], wf[j]).astype(BF)

    def phase_filter_idft():
        loop(4, filter_idft, 4)

    phase_filter_idft()

    def filter_rows(i):
        outs = []
        for k in range(2):
            rows = jnp.concatenate([hfield[j, chunk(2 * i + k, bs), :] for j in range(4)], 0)
            outs.append(dot(perm[1], rows).astype(BF))
        for k in range(2):
            for q in range(per):
                d = (2 * i + k) * per + q
                gf_out[lax.div(d, 2 * ring_n), lax.rem(lax.div(d, 2), ring_n), lax.rem(d, 2)] = outs[k][q * lr : (q + 1) * lr]

    def phase_filter_rows():
        loop(ctx_n // 2, filter_rows)

    phase_filter_rows()
    others(ring_n, z_me, lambda to: ring_copy(1, to).start())

    def ring_sum(kind, out, arrivals, mid, end):
        others(ring_n, z_me, lambda i: arrived(arrivals.at[i], ring_recv.at[kind, i]))
        for q in range(4):
            total = out[q // 2, z_me, q % 2].astype(F32)
            for i in range(1, ring_n):
                total = total + arrivals[lax.rem(z_me + i, ring_n), q // 2, q % 2].astype(F32)
            mid[q] = total.astype(BF)
        end[quad_me] = mid[quad_me]
        others(4, quad_me, lambda to: quad_copy(kind, to).start())

    def quad_sum(kind, end, result):
        others(4, quad_me, lambda i: arrived(end.at[i], quad_recv.at[kind, i]))
        for c in range(2):
            result[:, c * cw : (c + 1) * cw] = end[c].astype(F32) + end[2 + c].astype(F32)

    def gz_idft(i):
        s, j = lax.div(i, 4), lax.rem(i, 4)
        conv[s, j] = dot(inv[j], wbuf[s, j])

    def phase_gz_idft():
        loop(8, gz_idft, 4)

    phase_gz_idft()

    def phase_grad():
        for h in halves:
            f = [[taps[r, i : i + 1, h] for i in range(3)] for r in range(3)]

            def grad(s, h=h, f=f):
                def step(i, carry):
                    p = ctx_n - 1 - i
                    rows = chunk(p, bs)
                    lines = [[], [], []]
                    for j in range(4):
                        gz = conv[s, j, rows, h].astype(BF).astype(F32)
                        gs = [gq[s, j, rows, h], gz * uv[s, j, rows, h], gz * uk[s, j, rows, h]]
                        for tap in range(3):
                            lines[tap].append(f[0][tap] * gs[0] + f[1][tap] * gs[1] + f[2][tap] * gs[2])
                    turned = [pltpu.roll(v, bs - 1, 0) for v in (lines[1][0], lines[2][0], lines[2][1])]
                    early = [jnp.where(row16 == bs - 1, carry[q], turned[q]) for q in range(3)]
                    once = lines[1][1:] + [early[0]]
                    twice = lines[2][2:] + [early[1], early[2]]
                    for j in range(4):
                        gx[s, p, j, :, h] = (lines[0][j] + once[j] + twice[j]).astype(BF)
                    return tuple(turned)

                zero = jnp.zeros((bs, LANES), F32)
                lax.fori_loop(0, ctx_n, step, (zero, zero, zero))

            loop(2, grad)

    phase_grad()

    def phase_scatter():
        ge_out[...] = dot(lookups[...], gx[...].reshape(pair_n * block, cw)).astype(BF).reshape(ge_out.shape)

    phase_scatter()
    others(dp_n, dp, lambda to: ge_copy(to).start())

    ring_sum(1, gf_out, gf_in, gf_mid, gf_end)
    quad_sum(1, gf_end, gf_ref)
    others(dp_n, dp, lambda i: arrived(ge_in.at[i], ge_recv.at[i]))
    ge_in[dp] = ge_out[dp]
    for c in range(2):
        total = ge_in[c].astype(F32)
        for i in range(1, dp_n // 2):
            total = total + ge_in[2 * i + c].astype(F32)
        ge_ref[:, c * cw : (c + 1) * cw] = total

    def mixed_arrived(i):
        s, p = lax.div(i, ctx_n), lax.rem(i, ctx_n)
        arrived(mixed_hbm.at[0, :, chunk(2 * p + s, cw)], mix_recv.at[i])

    loop(pair_n, mixed_arrived)

    def pair_sent(to):
        ids_copy(to).wait_send()
        cot_copy(to).wait_send()
        mix_copy(to).wait_send()

    def quad_sent(to):
        for kind in range(2):
            quad_copy(kind, to).wait_send()

    def ring_sent(to):
        for kind in range(2):
            ring_copy(kind, to).wait_send()

    others(pair_n, pair_me, pair_sent)
    others(4, quad_me, quad_sent)
    others(dp_n, dp, lambda to: ge_copy(to).wait_send())
    others(ring_n, z_me, ring_sent)


def collect(mixed_raw, ge_raw, gf_raw, mixed, ge, gf, mixed_vmem, ge_vmem, gf_vmem, in_sem, out_sem):
    rows = mixed.shape[1] // 4
    moves = [[ref.at[:, pl.ds(i * rows, rows)] for ref in (mixed_raw, mixed_vmem, mixed)] for i in range(4)]
    moves += [[ge_raw, ge_vmem, ge], [gf_raw, gf_vmem, gf]]
    ins = [pltpu.make_async_copy(a, b, in_sem.at[i]) for i, (a, b, _) in enumerate(moves)]
    outs = [pltpu.make_async_copy(b, c, out_sem.at[i]) for i, (_, b, c) in enumerate(moves)]
    for load in ins:
        load.start()
    for load, store in zip(ins, outs):
        load.wait()
        store.start()
    for store in outs:
        store.wait()


def body(token_ids, embedding, short_filter, long_filter, cotangent):
    vocab, width = embedding.shape
    dp_n, ctx_n = lax.axis_size("dp"), lax.axis_size("ctx")
    part = width // ctx_n
    block = token_ids.shape[1]
    length = block * ctx_n
    cw, sub, bs, pair_n = part // 2, length // 4, block // 4, 2 * ctx_n
    lr, vr, ring_n = length // dp_n, vocab // dp_n, dp_n // 4
    fwd, inv = tables(length)
    hbm = pl.BlockSpec(memory_space=pl.ANY)
    vmem = pl.BlockSpec(memory_space=pltpu.VMEM)
    dma = pltpu.SemaphoreType.DMA
    results = pl.pallas_call(
        functools.partial(kernel, (dp_n, ctx_n, vocab, part, block)),
        out_shape=[
            jax.ShapeDtypeStruct((1, block, width), BF),
            jax.ShapeDtypeStruct((vr, part), F32),
            jax.ShapeDtypeStruct((lr, part), F32),
        ],
        in_specs=[hbm, hbm, hbm, hbm, hbm, hbm, hbm],
        out_specs=[hbm, vmem, vmem],
        scratch_shapes=[
            pltpu.VMEM((1, block), jnp.int32),
            pltpu.VMEM((8, block), F32),
            pltpu.VMEM((pair_n, 8, block), F32),
            pltpu.VMEM((2, block, block), BF),
            pltpu.VMEM((vocab, cw), BF),
            pltpu.VMEM((3, 3, cw), F32),
            pltpu.VMEM((2, ring_n, 2, lr, cw), BF),
            pltpu.VMEM((pair_n, block, cw), BF),
            pltpu.VMEM(fwd.shape, BF),
            pltpu.VMEM(inv.shape, BF),
            pltpu.VMEM((2, 4, sub, cw), F32),
            pltpu.VMEM((2, 4, sub, cw), F32),
            pltpu.VMEM((2, 4, sub, cw), F32),
            pltpu.VMEM((2, 4, sub, cw), F32),
            pltpu.VMEM((2, 4, sub, cw), BF),
            pltpu.VMEM((4, sub, cw), BF),
            pltpu.VMEM((4, 2, sub, cw), F32),
            pltpu.VMEM((2, 4, 2, sub, cw), F32),
            pltpu.VMEM((4, 2 * sub, cw), F32),
            pltpu.VMEM((2, 4, 2 * sub, cw), F32),
            pltpu.VMEM((2, 4, 2 * sub, cw), BF),
            pltpu.VMEM((4, 2 * sub, cw), BF),
            pltpu.VMEM((2, 4, sub, cw), F32),
            pltpu.VMEM((2, 4, sub, cw), F32),
            pltpu.VMEM((2, ctx_n, 4, bs, cw), BF),
            pltpu.VMEM((pair_n * block, vocab), BF),
            pltpu.VMEM((vocab, pair_n * block), BF),
            pltpu.VMEM((pair_n, block, cw), BF),
            pltpu.VMEM((2, ring_n, 2, lr, cw), BF),
            pltpu.VMEM((ring_n, 2, 2, lr, cw), BF),
            pltpu.VMEM((4, lr, cw), BF),
            pltpu.VMEM((4, lr, cw), BF),
            pltpu.VMEM((dp_n, vr, cw), BF),
            pltpu.VMEM((dp_n, vr, cw), BF),
            dma((5,)),
            dma((pair_n,)), dma((pair_n,)),
            dma((pair_n,)), dma((pair_n,)),
            dma((pair_n,)), dma((pair_n,)),
            dma((2, 4)), dma((2, 4)),
            dma((2, ring_n)), dma((2, ring_n)),
            dma((dp_n,)), dma((dp_n,)),
        ],
        compiler_params=pltpu.CompilerParams(
            collective_id=0, has_side_effects=True, vmem_limit_bytes=56 * 1024 * 1024
        ),
        name="hyena",
    )(token_ids, embedding, short_filter, long_filter, cotangent, fwd, inv)
    return pl.pallas_call(
        collect,
        out_shape=[jax.ShapeDtypeStruct(r.shape, r.dtype) for r in results],
        in_specs=[hbm] * 3,
        out_specs=[hbm] * 3,
        scratch_shapes=[pltpu.VMEM(r.shape, r.dtype) for r in results] + [dma((6,)), dma((6,))],
        compiler_params=pltpu.CompilerParams(vmem_limit_bytes=56 * 1024 * 1024),
        name="collect",
    )(*results)


def solution(mesh):
    in_specs = (P("dp", "ctx"), P(), P(), P("dp", "ctx"), P("dp", "ctx", None))
    out_specs = (P("dp", "ctx", None), P("dp", "ctx"), P("dp", "ctx"))
    return jax.shard_map(body, mesh=mesh, in_specs=in_specs, out_specs=out_specs, check_vma=False)
```

```python
import functools
import math

import jax
import jax.numpy as jnp
import numpy as np
from jax import lax
from jax.experimental import pallas as pl
from jax.experimental.pallas import tpu as pltpu
from jax.sharding import PartitionSpec as P

BF = jnp.bfloat16
F32 = jnp.float32
MESH = pl.DeviceIdType.MESH
LANES = 128
KC = 16


def tables(length):
    sub = length // 4
    k = np.arange(sub)[None, :, None]
    t = 4 * np.arange(sub)[None, None, :] + np.arange(4)[:, None, None]
    angle = 2.0 * math.pi * (((4 * k + 1) * t) % (4 * length)) / (4 * length)
    fwd = np.concatenate([np.cos(angle), -np.sin(angle)], 1)
    inv = fwd.transpose(0, 2, 1) / length
    return jnp.asarray(fwd, BF), jnp.asarray(inv, BF)


def radix4(re, im, sign):
    a_re, a_im, b_re, b_im = re[0] + re[2], im[0] + im[2], re[0] - re[2], im[0] - im[2]
    c_re, c_im, d_re, d_im = re[1] + re[3], im[1] + im[3], re[1] - re[3], im[1] - im[3]
    if sign > 0:
        d_re, d_im = -d_re, -d_im
    return (
        [a_re + c_re, b_re + d_im, a_re - c_re, b_re - d_im],
        [a_im + c_im, b_im - d_re, a_im - c_im, b_im + d_re],
    )


def loop(count, step, unroll=1):
    def run(i, carry):
        for q in range(unroll):
            step(i * unroll + q)
        return carry

    lax.fori_loop(0, count // unroll, run, 0)


def dot(a, b):
    return jnp.dot(a, b, preferred_element_type=F32)


def kernel(
    dims,
    ids_hbm, emb_hbm, taps_hbm, lf_hbm, cot_hbm, fwd_hbm, inv_hbm,
    mixed_hbm, ge_ref, gf_ref,
    ids_raw, ids_mine, ids_in, perm, emb, taps, lf_in, cot_in, fwd, inv,
    x, uq, uk, uv, field, hfield, spec_h, spec_z, hbuf, pbuf, wbuf, wf, conv, gq, gx,
    onehot, lookups, mixed_out, gf_out, gf_in, ge_out, ge_in, lf_raw, cot_raw,
    local_sem, ids_send, ids_recv, cot_send, cot_recv, mix_send, mix_recv, half_send, half_recv,
    cross_send, cross_recv, relay_send, relay_recv, gf_send, gf_recv, ge_send, ge_recv,
):
    dp_n, ctx_n, vocab, part, block = dims
    cw = part // 2
    sub = ctx_n * block // 4
    bs = block // 4
    pair_n = 2 * ctx_n
    per = dp_n // ctx_n
    lr = block // per
    vr = vocab // dp_n
    dp = lax.axis_index("dp")
    p_me = lax.axis_index("ctx")
    g = lax.div(dp, 2)
    c_me = lax.rem(dp, 2)
    ring_n = dp_n // 4
    y_me, z_me = lax.div(g, ring_n), lax.rem(g, ring_n)
    half_n, half_me = 2 * ring_n, 2 * z_me + c_me
    pair_me = c_me * ctx_n + p_me
    first = pl.multiple_of(p_me * part + c_me * cw, cw)
    halves = [pl.ds(h * LANES, LANES) for h in range(cw // LANES)]

    def chunk(i, size):
        return pl.ds(pl.multiple_of(i * size, size), size)

    loads = [
        pltpu.make_async_copy(emb_hbm.at[:, pl.ds(first, cw)], emb, local_sem.at[0]),
        pltpu.make_async_copy(taps_hbm.at[:, :, pl.ds(first, cw)], taps, local_sem.at[1]),
        pltpu.make_async_copy(fwd_hbm, fwd, local_sem.at[2]),
        pltpu.make_async_copy(inv_hbm, inv, local_sem.at[3]),
    ]
    load_ids = pltpu.make_async_copy(ids_hbm, ids_raw, local_sem.at[4])
    load_ids.start()
    load_lf = pltpu.make_async_copy(lf_hbm, lf_raw, local_sem.at[5])
    load_lf.start()
    load_cot = pltpu.make_async_copy(cot_hbm.at[0], cot_raw, local_sem.at[6])
    load_cot.start()
    for load in loads:
        load.start()

    barrier = pltpu.get_barrier_semaphore()

    def greet_pair(i):
        to = lax.rem(pair_me + 1 + i, pair_n)
        device = (2 * g + lax.div(to, ctx_n), lax.rem(to, ctx_n))
        pl.semaphore_signal(barrier, inc=1, device_id=device, device_id_type=MESH)

    def greet_dp(i):
        device = (lax.rem(dp + 1 + i, dp_n), p_me)
        pl.semaphore_signal(barrier, inc=1, device_id=device, device_id_type=MESH)

    loop(pair_n - 1, greet_pair)
    loop(dp_n - 1, greet_dp)
    def natural(axis):
        place = lax.broadcasted_iota(jnp.int32, (block, block), axis)
        return 4 * (place & (bs - 1)) + (place >> (bs.bit_length() - 1))

    perm[0] = (natural(0) == lax.broadcasted_iota(jnp.int32, (block, block), 1)).astype(F32).astype(BF)
    perm[1] = (natural(1) == lax.broadcasted_iota(jnp.int32, (block, block), 0)).astype(F32).astype(BF)

    load_ids.wait()
    ids = jnp.broadcast_to(ids_raw[...].astype(F32), (8, block))
    high = jnp.where(ids >= 256.0, 1.0, 0.0)
    low = ids - 256.0 * high
    ids_mine[...] = dot(low.astype(BF), perm[1]) + 256.0 * dot(high.astype(BF), perm[1])
    pl.semaphore_wait(barrier, pair_n - 1 + dp_n - 1)

    def ids_copy(to):
        return pltpu.make_async_remote_copy(
            src_ref=ids_mine, dst_ref=ids_in.at[pair_me], send_sem=ids_send.at[to], recv_sem=ids_recv.at[pair_me],
            device_id=(2 * g + lax.div(to, ctx_n), lax.rem(to, ctx_n)), device_id_type=MESH,
        )

    def half_copy(to):
        return pltpu.make_async_remote_copy(
            src_ref=lf_raw.at[:, chunk(lax.rem(to, 2), cw)], dst_ref=lf_in.at[y_me, z_me, c_me],
            send_sem=half_send.at[to], recv_sem=half_recv.at[half_me],
            device_id=(y_me * half_n + to, p_me), device_id_type=MESH,
        )

    def cross_copy(to):
        return pltpu.make_async_remote_copy(
            src_ref=lf_raw.at[:, to * cw : (to + 1) * cw], dst_ref=lf_in.at[y_me, z_me, c_me],
            send_sem=cross_send.at[to], recv_sem=cross_recv.at[c_me],
            device_id=((1 - y_me) * half_n + 2 * z_me + to, p_me), device_id_type=MESH,
        )

    def relay_copy(to):
        return pltpu.make_async_remote_copy(
            src_ref=lf_in.at[1 - y_me, z_me], dst_ref=lf_in.at[1 - y_me, z_me],
            send_sem=relay_send.at[to], recv_sem=relay_recv.at[z_me],
            device_id=(y_me * half_n + 2 * to + c_me, p_me), device_id_type=MESH,
        )

    def cot_columns(to):
        return cot_raw.at[:, chunk(2 * lax.rem(to, ctx_n) + lax.div(to, ctx_n), cw)]

    def cot_copy(to):
        return pltpu.make_async_remote_copy(
            src_ref=cot_columns(to), dst_ref=cot_in.at[pair_me], send_sem=cot_send.at[to], recv_sem=cot_recv.at[pair_me],
            device_id=(2 * g + lax.div(to, ctx_n), lax.rem(to, ctx_n)), device_id_type=MESH,
        )

    def mix_copy(to):
        return pltpu.make_async_remote_copy(
            src_ref=mixed_out.at[to], dst_ref=mixed_hbm.at[0, :, pl.ds(first, cw)],
            send_sem=mix_send.at[to], recv_sem=mix_recv.at[pair_me],
            device_id=(2 * g + lax.div(to, ctx_n), lax.rem(to, ctx_n)), device_id_type=MESH,
        )

    def gf_copy(to):
        return pltpu.make_async_remote_copy(
            src_ref=gf_out.at[to], dst_ref=gf_in.at[dp], send_sem=gf_send.at[to], recv_sem=gf_recv.at[dp],
            device_id=(to, p_me), device_id_type=MESH,
        )

    def ge_copy(to):
        return pltpu.make_async_remote_copy(
            src_ref=ge_out.at[to], dst_ref=ge_in.at[dp], send_sem=ge_send.at[to], recv_sem=ge_recv.at[dp],
            device_id=(to, p_me), device_id_type=MESH,
        )

    def others(count, me, step):
        loop(count - 1, lambda i: step(lax.rem(me + 1 + i, count)))

    def arrived(slot, sem):
        pltpu.make_async_copy(slot, slot, sem).wait()

    load_lf.wait()
    for to in range(2):
        cross_copy(to).start()
    others(half_n, half_me, lambda to: half_copy(to).start())
    others(pair_n, pair_me, lambda to: ids_copy(to).start())
    pltpu.make_async_copy(ids_mine, ids_in.at[pair_me], ids_recv.at[pair_me]).start()
    pltpu.make_async_copy(lf_raw.at[:, chunk(c_me, cw)], lf_in.at[y_me, z_me, c_me], half_recv.at[half_me]).start()
    load_cot.wait()
    pltpu.make_async_copy(cot_columns(pair_me), cot_in.at[pair_me], cot_recv.at[pair_me]).start()
    for c in range(2):
        arrived(lf_in.at[1 - y_me, z_me, c], cross_recv.at[c])
    others(ring_n, z_me, lambda to: relay_copy(to).start())
    others(pair_n, pair_me, lambda to: cot_copy(to).start())

    loads[0].wait()
    loads[1].wait()
    vocab_lane = lax.broadcasted_iota(jnp.int32, (block, LANES), 1).astype(F32)

    def phase_lookup():
        def lookup(i):
            for k in range(4):
                arrived(ids_in.at[4 * i + k], ids_recv.at[4 * i + k])
            rows = [jnp.broadcast_to(ids_in[4 * i + k, 0:1, :], (block, block)) for k in range(4)]
            columns = [jnp.transpose(row) for row in rows]
            for k in range(4):
                for q in range(vocab // LANES):
                    onehot[chunk(4 * i + k, block), q * LANES : (q + 1) * LANES] = (
                        (columns[k] == vocab_lane + float(q * LANES)).astype(F32).astype(BF)
                    )

        loop(pair_n // 4, lookup)

    def phase_embed():
        def embed(i):
            rows = dot(onehot[chunk(i, 4 * block), :], emb[...])
            for q in range(4):
                s, p = lax.div(4 * i + q, ctx_n), lax.rem(4 * i + q, ctx_n)
                for j in range(4):
                    x[s, j, chunk(p, bs), :] = rows[q * block + j * bs : q * block + (j + 1) * bs]

        loop(pair_n // 4, embed)

    phase_lookup()
    phase_embed()

    row16 = lax.broadcasted_iota(jnp.int32, (bs, LANES), 0)
    def phase_short():
        for h in halves:
            f = [[taps[r, i : i + 1, h] for i in range(3)] for r in range(3)]

            def short(s, h=h, f=f):
                def step(p, carry):
                    rows = chunk(p, bs)
                    xs = [x[s, j, rows, h] for j in range(4)]
                    turned = [pltpu.roll(xs[2], 1, 0), pltpu.roll(xs[3], 1, 0)]
                    late = [jnp.where(row16 == 0, carry[q], turned[q]) for q in range(2)]
                    line = late + xs
                    us = [
                        [f[r][0] * line[j + 2] + f[r][1] * line[j + 1] + f[r][2] * line[j] for j in range(4)]
                        for r in range(3)
                    ]
                    for j in range(4):
                        uq[s, j, rows, h] = us[0][j]
                        uk[s, j, rows, h] = us[1][j]
                        uv[s, j, rows, h] = us[2][j]
                        field[s, j, rows, h] = (us[1][j] * us[2][j]).astype(BF)
                    return tuple(turned)

                zero = jnp.zeros((bs, LANES), F32)
                lax.fori_loop(0, ctx_n, step, (zero, zero))

            loop(2, short)

    phase_short()

    loads[2].wait()

    def field_dft(i):
        s, j = lax.div(i, 4), lax.rem(i, 4)
        pbuf[s, j] = dot(fwd[j], field[s, j])

    def phase_field_dft():
        loop(8, field_dft, 4)

    phase_field_dft()

    vocab_row = lax.broadcasted_iota(jnp.int32, (vocab, block), 0).astype(F32)

    def phase_lookup_rows():
        def lookup(i):
            lookups[:, chunk(i, block)] = (vocab_row == ids_in[i, 0:1, :]).astype(F32).astype(BF)

        loop(pair_n, lookup)

    phase_lookup_rows()


    def phase_taps():
        def gather_taps(i):
            outs = []
            for k in range(2):
                pieces = [(2 * i + k) * per + q for q in range(per)]
                rows = [lf_in[lax.div(d, 2 * ring_n), lax.rem(lax.div(d, 2), ring_n), lax.rem(d, 2)] for d in pieces]
                outs.append(dot(perm[0], jnp.concatenate(rows, 0)).astype(BF))
            for k in range(2):
                for j in range(4):
                    hfield[j, chunk(2 * i + k, bs), :] = outs[k][j * bs : (j + 1) * bs]

        loop(half_n, lambda i: arrived(lf_in.at[y_me, lax.div(i, 2), lax.rem(i, 2)], half_recv.at[i]))
        others(ring_n, z_me, lambda i: arrived(lf_in.at[1 - y_me, i], relay_recv.at[i]))
        loop(ctx_n // 2, gather_taps)

    phase_taps()

    def filter_dft(j):
        hbuf[j] = dot(fwd[j], hfield[j])

    def phase_filter_dft():
        loop(4, filter_dft, 4)

    phase_filter_dft()

    def butterfly(ref, i, h):
        re = [ref[j, chunk(i, KC), h] for j in range(4)]
        im = [ref[j, pl.ds(pl.multiple_of(sub + i * KC, KC), KC), h] for j in range(4)]
        return radix4(re, im, -1)

    def filter_mix(i):
        for h in halves:
            re, im = butterfly(hbuf, i, h)
            for m in range(4):
                spec_h[m, 0, chunk(i, KC), h] = re[m]
                spec_h[m, 1, chunk(i, KC), h] = im[m]

    def phase_filter_mix():
        loop(sub // KC, filter_mix)

    phase_filter_mix()

    def put(ref, i, h, re, im):
        re, im = radix4(re, im, 1)
        for j in range(4):
            ref[j, chunk(i, KC), h] = re[j].astype(BF)
            ref[j, pl.ds(pl.multiple_of(sub + i * KC, KC), KC), h] = im[j].astype(BF)


    loads[3].wait()

    for s in range(2):

        def conv_mix(i, s=s):
            for h in halves:
                re, im = butterfly(pbuf.at[s], i, h)
                out_re, out_im = [], []
                for m in range(4):
                    spec_z[s, m, 0, chunk(i, KC), h] = re[m]
                    spec_z[s, m, 1, chunk(i, KC), h] = im[m]
                    h_re, h_im = spec_h[m, 0, chunk(i, KC), h], spec_h[m, 1, chunk(i, KC), h]
                    out_re.append(re[m] * h_re - im[m] * h_im)
                    out_im.append(re[m] * h_im + im[m] * h_re)
                put(wbuf.at[s], i, h, out_re, out_im)

        def phase_conv_mix():
            loop(sub // KC, conv_mix)

        phase_conv_mix()

        def conv_idft(j, s=s):
            conv[s, j] = dot(inv[j], wbuf[s, j]).astype(BF).astype(F32)

        def phase_conv_idft():
            loop(4, conv_idft, 4)

        phase_conv_idft()

        def mix(i, s=s):
            outs = []
            for k in range(2):
                p = lax.rem(p_me + 1 + 2 * i + k, ctx_n)
                rows = chunk(p, bs)
                out = jnp.concatenate([(uq[s, j, rows, :] * conv[s, j, rows, :]).astype(BF) for j in range(4)], 0)
                outs.append((s * ctx_n + p, dot(perm[1], out).astype(BF)))
            for to, out in outs:
                mixed_out[to] = out
            for to, _ in outs:

                @pl.when(to != pair_me)
                def _():
                    mix_copy(to).start()

                @pl.when(to == pair_me)
                def _():
                    pltpu.make_async_copy(
                        mixed_out.at[to], mixed_hbm.at[0, :, pl.ds(first, cw)], mix_recv.at[pair_me]
                    ).start()

        def phase_mix():
            loop(ctx_n // 2, mix)

        phase_mix()

    def take(i):
        for k in range(4):
            arrived(cot_in.at[4 * i + k], cot_recv.at[4 * i + k])
        outs = [dot(perm[0], cot_in[4 * i + k]) for k in range(4)]
        for k in range(4):
            s, p = lax.div(4 * i + k, ctx_n), lax.rem(4 * i + k, ctx_n)
            rows = chunk(p, bs)
            for j in range(4):
                piece = outs[k][j * bs : (j + 1) * bs]
                field[s, j, rows, :] = (piece * uq[s, j, rows, :]).astype(BF)
                gq[s, j, rows, :] = piece * conv[s, j, rows, :]

    def phase_take():
        loop(pair_n // 4, take)

    phase_take()
    phase_field_dft()

    def back_mix(i):
        for h in halves:
            sum_re, sum_im = None, None
            for s in range(2):
                re, im = butterfly(pbuf.at[s], i, h)
                out_re, out_im, f_re, f_im = [], [], [], []
                for m in range(4):
                    h_re, h_im = spec_h[m, 0, chunk(i, KC), h], spec_h[m, 1, chunk(i, KC), h]
                    z_re, z_im = spec_z[s, m, 0, chunk(i, KC), h], spec_z[s, m, 1, chunk(i, KC), h]
                    out_re.append(re[m] * h_re + im[m] * h_im)
                    out_im.append(im[m] * h_re - re[m] * h_im)
                    f_re.append(re[m] * z_re + im[m] * z_im)
                    f_im.append(im[m] * z_re - re[m] * z_im)
                put(wbuf.at[s], i, h, out_re, out_im)
                if s == 0:
                    sum_re, sum_im = f_re, f_im
                else:
                    sum_re = [a + b for a, b in zip(sum_re, f_re)]
                    sum_im = [a + b for a, b in zip(sum_im, f_im)]
            put(wf, i, h, sum_re, sum_im)

    def phase_back_mix():
        loop(sub // KC, back_mix)

    phase_back_mix()

    def filter_idft(j):
        hfield[j] = dot(inv[j], wf[j]).astype(BF)

    def phase_filter_idft():
        loop(4, filter_idft, 4)

    phase_filter_idft()

    def filter_rows(i):
        outs = []
        for k in range(2):
            rows = jnp.concatenate([hfield[j, chunk(2 * i + k, bs), :] for j in range(4)], 0)
            outs.append(dot(perm[1], rows).astype(BF))
        for k in range(2):
            for q in range(per):
                d = (2 * i + k) * per + q
                gf_out[d] = outs[k][q * lr : (q + 1) * lr]

    def phase_filter_rows():
        loop(ctx_n // 2, filter_rows)

    phase_filter_rows()
    others(dp_n, dp, lambda to: gf_copy(to).start())

    def owner_sum(out, arrivals, sems, result):
        others(dp_n, dp, lambda i: arrived(arrivals.at[i], sems.at[i]))
        arrivals[dp] = out[dp]
        for c in range(2):
            total = arrivals[c].astype(F32)
            for i in range(1, dp_n // 2):
                total = total + arrivals[2 * i + c].astype(F32)
            result[:, c * cw : (c + 1) * cw] = total

    def gz_idft(i):
        s, j = lax.div(i, 4), lax.rem(i, 4)
        conv[s, j] = dot(inv[j], wbuf[s, j])

    def phase_gz_idft():
        loop(8, gz_idft, 4)

    phase_gz_idft()

    def phase_grad():
        for h in halves:
            f = [[taps[r, i : i + 1, h] for i in range(3)] for r in range(3)]

            def grad(s, h=h, f=f):
                def step(i, carry):
                    p = ctx_n - 1 - i
                    rows = chunk(p, bs)
                    lines = [[], [], []]
                    for j in range(4):
                        gz = conv[s, j, rows, h].astype(BF).astype(F32)
                        gs = [gq[s, j, rows, h], gz * uv[s, j, rows, h], gz * uk[s, j, rows, h]]
                        for tap in range(3):
                            lines[tap].append(f[0][tap] * gs[0] + f[1][tap] * gs[1] + f[2][tap] * gs[2])
                    turned = [pltpu.roll(v, bs - 1, 0) for v in (lines[1][0], lines[2][0], lines[2][1])]
                    early = [jnp.where(row16 == bs - 1, carry[q], turned[q]) for q in range(3)]
                    once = lines[1][1:] + [early[0]]
                    twice = lines[2][2:] + [early[1], early[2]]
                    for j in range(4):
                        gx[s, p, j, :, h] = (lines[0][j] + once[j] + twice[j]).astype(BF)
                    return tuple(turned)

                zero = jnp.zeros((bs, LANES), F32)
                lax.fori_loop(0, ctx_n, step, (zero, zero, zero))

            loop(2, grad)

    phase_grad()

    def phase_scatter():
        ge_out[...] = dot(lookups[...], gx[...].reshape(pair_n * block, cw)).astype(BF).reshape(ge_out.shape)

    phase_scatter()
    others(dp_n, dp, lambda to: ge_copy(to).start())

    owner_sum(gf_out, gf_in, gf_recv, gf_ref)
    owner_sum(ge_out, ge_in, ge_recv, ge_ref)

    def mixed_arrived(i):
        s, p = lax.div(i, ctx_n), lax.rem(i, ctx_n)
        arrived(mixed_hbm.at[0, :, chunk(2 * p + s, cw)], mix_recv.at[i])

    loop(pair_n, mixed_arrived)

    def pair_sent(to):
        ids_copy(to).wait_send()
        cot_copy(to).wait_send()
        mix_copy(to).wait_send()

    def dp_sent(to):
        gf_copy(to).wait_send()
        ge_copy(to).wait_send()

    others(pair_n, pair_me, pair_sent)
    others(dp_n, dp, dp_sent)
    others(half_n, half_me, lambda to: half_copy(to).wait_send())
    others(ring_n, z_me, lambda to: relay_copy(to).wait_send())
    for to in range(2):
        cross_copy(to).wait_send()


def collect(mixed_raw, ge_raw, gf_raw, mixed, ge, gf, mixed_vmem, ge_vmem, gf_vmem, in_sem, out_sem):
    rows = mixed.shape[1] // 4
    moves = [[ref.at[:, pl.ds(i * rows, rows)] for ref in (mixed_raw, mixed_vmem, mixed)] for i in range(4)]
    moves += [[ge_raw, ge_vmem, ge], [gf_raw, gf_vmem, gf]]
    ins = [pltpu.make_async_copy(a, b, in_sem.at[i]) for i, (a, b, _) in enumerate(moves)]
    outs = [pltpu.make_async_copy(b, c, out_sem.at[i]) for i, (_, b, c) in enumerate(moves)]
    for load in ins:
        load.start()
    for load, store in zip(ins, outs):
        load.wait()
        store.start()
    for store in outs:
        store.wait()


def body(token_ids, embedding, short_filter, long_filter, cotangent):
    vocab, width = embedding.shape
    dp_n, ctx_n = lax.axis_size("dp"), lax.axis_size("ctx")
    part = width // ctx_n
    block = token_ids.shape[1]
    length = block * ctx_n
    cw, sub, bs, pair_n = part // 2, length // 4, block // 4, 2 * ctx_n
    lr, vr, ring_n = length // dp_n, vocab // dp_n, dp_n // 4
    fwd, inv = tables(length)
    hbm = pl.BlockSpec(memory_space=pl.ANY)
    vmem = pl.BlockSpec(memory_space=pltpu.VMEM)
    dma = pltpu.SemaphoreType.DMA
    results = pl.pallas_call(
        functools.partial(kernel, (dp_n, ctx_n, vocab, part, block)),
        out_shape=[
            jax.ShapeDtypeStruct((1, block, width), BF),
            jax.ShapeDtypeStruct((vr, part), F32),
            jax.ShapeDtypeStruct((lr, part), F32),
        ],
        in_specs=[hbm, hbm, hbm, hbm, hbm, hbm, hbm],
        out_specs=[hbm, vmem, vmem],
        scratch_shapes=[
            pltpu.VMEM((1, block), jnp.int32),
            pltpu.VMEM((8, block), F32),
            pltpu.VMEM((pair_n, 8, block), F32),
            pltpu.VMEM((2, block, block), BF),
            pltpu.VMEM((vocab, cw), BF),
            pltpu.VMEM((3, 3, cw), F32),
            pltpu.VMEM((2, ring_n, 2, lr, cw), BF),
            pltpu.VMEM((pair_n, block, cw), BF),
            pltpu.VMEM(fwd.shape, BF),
            pltpu.VMEM(inv.shape, BF),
            pltpu.VMEM((2, 4, sub, cw), F32),
            pltpu.VMEM((2, 4, sub, cw), F32),
            pltpu.VMEM((2, 4, sub, cw), F32),
            pltpu.VMEM((2, 4, sub, cw), F32),
            pltpu.VMEM((2, 4, sub, cw), BF),
            pltpu.VMEM((4, sub, cw), BF),
            pltpu.VMEM((4, 2, sub, cw), F32),
            pltpu.VMEM((2, 4, 2, sub, cw), F32),
            pltpu.VMEM((4, 2 * sub, cw), F32),
            pltpu.VMEM((2, 4, 2 * sub, cw), F32),
            pltpu.VMEM((2, 4, 2 * sub, cw), BF),
            pltpu.VMEM((4, 2 * sub, cw), BF),
            pltpu.VMEM((2, 4, sub, cw), F32),
            pltpu.VMEM((2, 4, sub, cw), F32),
            pltpu.VMEM((2, ctx_n, 4, bs, cw), BF),
            pltpu.VMEM((pair_n * block, vocab), BF),
            pltpu.VMEM((vocab, pair_n * block), BF),
            pltpu.VMEM((pair_n, block, cw), BF),
            pltpu.VMEM((dp_n, lr, cw), BF),
            pltpu.VMEM((dp_n, lr, cw), BF),
            pltpu.VMEM((dp_n, vr, cw), BF),
            pltpu.VMEM((dp_n, vr, cw), BF),
            pltpu.VMEM((lr, part), BF),
            pltpu.VMEM((block, width), BF),
            dma((7,)),
            dma((pair_n,)), dma((pair_n,)),
            dma((pair_n,)), dma((pair_n,)),
            dma((pair_n,)), dma((pair_n,)),
            dma((2 * ring_n,)), dma((2 * ring_n,)),
            dma((2,)), dma((2,)),
            dma((ring_n,)), dma((ring_n,)),
            dma((dp_n,)), dma((dp_n,)),
            dma((dp_n,)), dma((dp_n,)),
        ],
        compiler_params=pltpu.CompilerParams(
            collective_id=0, has_side_effects=True, vmem_limit_bytes=56 * 1024 * 1024
        ),
        name="hyena",
    )(token_ids, embedding, short_filter, long_filter, cotangent, fwd, inv)
    return pl.pallas_call(
        collect,
        out_shape=[jax.ShapeDtypeStruct(r.shape, r.dtype) for r in results],
        in_specs=[hbm] * 3,
        out_specs=[hbm] * 3,
        scratch_shapes=[pltpu.VMEM(r.shape, r.dtype) for r in results] + [dma((6,)), dma((6,))],
        compiler_params=pltpu.CompilerParams(vmem_limit_bytes=56 * 1024 * 1024),
        name="collect",
    )(*results)


def solution(mesh):
    in_specs = (P("dp", "ctx"), P(), P(), P("dp", "ctx"), P("dp", "ctx", None))
    out_specs = (P("dp", "ctx", None), P("dp", "ctx"), P("dp", "ctx"))
    return jax.shard_map(body, mesh=mesh, in_specs=in_specs, out_specs=out_specs, check_vma=False)
```

```python
import functools
import math

import jax
import jax.numpy as jnp
import numpy as np
from jax import lax
from jax.experimental import pallas as pl
from jax.experimental.pallas import tpu as pltpu
from jax.sharding import PartitionSpec as P

BF = jnp.bfloat16
F32 = jnp.float32
MESH = pl.DeviceIdType.MESH
LANES = 128
KC = 16


def tables(length):
    sub = length // 4
    k = np.arange(sub)[None, :, None]
    t = 4 * np.arange(sub)[None, None, :] + np.arange(4)[:, None, None]
    angle = 2.0 * math.pi * (((4 * k + 1) * t) % (4 * length)) / (4 * length)
    fwd = np.concatenate([np.cos(angle), -np.sin(angle)], 1)
    inv = fwd.transpose(0, 2, 1) / length
    return jnp.asarray(fwd, BF), jnp.asarray(inv, BF)


def radix4(re, im, sign):
    a_re, a_im, b_re, b_im = re[0] + re[2], im[0] + im[2], re[0] - re[2], im[0] - im[2]
    c_re, c_im, d_re, d_im = re[1] + re[3], im[1] + im[3], re[1] - re[3], im[1] - im[3]
    if sign > 0:
        d_re, d_im = -d_re, -d_im
    return (
        [a_re + c_re, b_re + d_im, a_re - c_re, b_re - d_im],
        [a_im + c_im, b_im - d_re, a_im - c_im, b_im + d_re],
    )


def loop(count, step, unroll=1):
    def run(i, carry):
        for q in range(unroll):
            step(i * unroll + q)
        return carry

    lax.fori_loop(0, count // unroll, run, 0)


def dot(a, b):
    return jnp.dot(a, b, preferred_element_type=F32)


def kernel(
    dims,
    ids_hbm, emb_hbm, taps_hbm, lf_hbm, cot_hbm, fwd_hbm, inv_hbm,
    mixed_hbm, ge_ref, gf_ref,
    ids_raw, ids_mine, ids_in, perm, emb, taps, lf_in, cot_in, fwd, inv,
    x, uq, uk, uv, field, hfield, spec_h, spec_z, hbuf, pbuf, wbuf, wf, conv, gq, gx,
    onehot, lookups, mixed_out, gf_out, gf_in, ge_out, ge_in, lf_raw, cot_raw,
    local_sem, ids_send, ids_recv, cot_send, cot_recv, mix_send, mix_recv, half_send, half_recv,
    cross_send, cross_recv, relay_send, relay_recv, gf_send, gf_recv, ge_send, ge_recv,
):
    dp_n, ctx_n, vocab, part, block = dims
    cw = part // 2
    sub = ctx_n * block // 4
    bs = block // 4
    pair_n = 2 * ctx_n
    per = dp_n // ctx_n
    lr = block // per
    vr = vocab // dp_n
    dp = lax.axis_index("dp")
    p_me = lax.axis_index("ctx")
    g = lax.div(dp, 2)
    c_me = lax.rem(dp, 2)
    ring_n = dp_n // 4
    y_me, z_me = lax.div(g, ring_n), lax.rem(g, ring_n)
    half_n, half_me = 2 * ring_n, 2 * z_me + c_me
    pair_me = c_me * ctx_n + p_me
    first = pl.multiple_of(p_me * part + c_me * cw, cw)
    halves = [pl.ds(h * LANES, LANES) for h in range(cw // LANES)]

    unroll_n = 4 if ctx_n % 4 == 0 else 2

    def chunk(i, size):
        return pl.ds(pl.multiple_of(i * size, size), size)

    loads = [
        pltpu.make_async_copy(emb_hbm.at[:, pl.ds(first, cw)], emb, local_sem.at[0]),
        pltpu.make_async_copy(taps_hbm.at[:, :, pl.ds(first, cw)], taps, local_sem.at[1]),
        pltpu.make_async_copy(fwd_hbm, fwd, local_sem.at[2]),
        pltpu.make_async_copy(inv_hbm, inv, local_sem.at[3]),
    ]
    load_ids = pltpu.make_async_copy(ids_hbm, ids_raw, local_sem.at[4])
    load_ids.start()
    load_lf = pltpu.make_async_copy(lf_hbm, lf_raw, local_sem.at[5])
    load_lf.start()
    load_cot = pltpu.make_async_copy(cot_hbm.at[0], cot_raw, local_sem.at[6])
    load_cot.start()
    for load in loads:
        load.start()

    barrier = pltpu.get_barrier_semaphore()

    def greet_pair(i):
        to = lax.rem(pair_me + 1 + i, pair_n)
        device = (2 * g + lax.div(to, ctx_n), lax.rem(to, ctx_n))
        pl.semaphore_signal(barrier, inc=1, device_id=device, device_id_type=MESH)

    def greet_dp(i):
        device = (lax.rem(dp + 1 + i, dp_n), p_me)
        pl.semaphore_signal(barrier, inc=1, device_id=device, device_id_type=MESH)

    loop(pair_n - 1, greet_pair)
    loop(dp_n - 1, greet_dp)
    def natural(axis):
        place = lax.broadcasted_iota(jnp.int32, (block, block), axis)
        return 4 * (place & (bs - 1)) + (place >> (bs.bit_length() - 1))

    perm[0] = (natural(0) == lax.broadcasted_iota(jnp.int32, (block, block), 1)).astype(F32).astype(BF)
    perm[1] = (natural(1) == lax.broadcasted_iota(jnp.int32, (block, block), 0)).astype(F32).astype(BF)

    load_ids.wait()
    ids = jnp.broadcast_to(ids_raw[...].astype(F32), (8, block))
    high = jnp.where(ids >= 256.0, 1.0, 0.0)
    low = ids - 256.0 * high
    ids_mine[...] = dot(low.astype(BF), perm[1]) + 256.0 * dot(high.astype(BF), perm[1])
    pl.semaphore_wait(barrier, pair_n - 1 + dp_n - 1)

    def ids_copy(to):
        return pltpu.make_async_remote_copy(
            src_ref=ids_mine, dst_ref=ids_in.at[pair_me], send_sem=ids_send.at[to], recv_sem=ids_recv.at[pair_me],
            device_id=(2 * g + lax.div(to, ctx_n), lax.rem(to, ctx_n)), device_id_type=MESH,
        )

    def half_copy(to):
        return pltpu.make_async_remote_copy(
            src_ref=lf_raw.at[:, chunk(lax.rem(to, 2), cw)], dst_ref=lf_in.at[y_me, z_me, c_me],
            send_sem=half_send.at[to], recv_sem=half_recv.at[half_me],
            device_id=(y_me * half_n + to, p_me), device_id_type=MESH,
        )

    def cross_copy(to):
        return pltpu.make_async_remote_copy(
            src_ref=lf_raw.at[:, to * cw : (to + 1) * cw], dst_ref=lf_in.at[y_me, z_me, c_me],
            send_sem=cross_send.at[to], recv_sem=cross_recv.at[c_me],
            device_id=((1 - y_me) * half_n + 2 * z_me + to, p_me), device_id_type=MESH,
        )

    def relay_copy(to):
        return pltpu.make_async_remote_copy(
            src_ref=lf_in.at[1 - y_me, z_me], dst_ref=lf_in.at[1 - y_me, z_me],
            send_sem=relay_send.at[to], recv_sem=relay_recv.at[z_me],
            device_id=(y_me * half_n + 2 * to + c_me, p_me), device_id_type=MESH,
        )

    def cot_columns(to):
        return cot_raw.at[:, chunk(2 * lax.rem(to, ctx_n) + lax.div(to, ctx_n), cw)]

    def cot_copy(to):
        return pltpu.make_async_remote_copy(
            src_ref=cot_columns(to), dst_ref=cot_in.at[pair_me], send_sem=cot_send.at[to], recv_sem=cot_recv.at[pair_me],
            device_id=(2 * g + lax.div(to, ctx_n), lax.rem(to, ctx_n)), device_id_type=MESH,
        )

    def mix_copy(to):
        return pltpu.make_async_remote_copy(
            src_ref=mixed_out.at[to], dst_ref=mixed_hbm.at[0, :, pl.ds(first, cw)],
            send_sem=mix_send.at[to], recv_sem=mix_recv.at[pair_me],
            device_id=(2 * g + lax.div(to, ctx_n), lax.rem(to, ctx_n)), device_id_type=MESH,
        )

    def gf_copy(to):
        return pltpu.make_async_remote_copy(
            src_ref=gf_out.at[to], dst_ref=gf_in.at[dp], send_sem=gf_send.at[to], recv_sem=gf_recv.at[dp],
            device_id=(to, p_me), device_id_type=MESH,
        )

    def ge_copy(to):
        return pltpu.make_async_remote_copy(
            src_ref=ge_out.at[to], dst_ref=ge_in.at[dp], send_sem=ge_send.at[to], recv_sem=ge_recv.at[dp],
            device_id=(to, p_me), device_id_type=MESH,
        )

    def others(count, me, step):
        loop(count - 1, lambda i: step(lax.rem(me + 1 + i, count)))

    def arrived(slot, sem):
        pltpu.make_async_copy(slot, slot, sem).wait()

    load_lf.wait()
    for to in range(2):
        cross_copy(to).start()
    others(half_n, half_me, lambda to: half_copy(to).start())
    others(pair_n, pair_me, lambda to: ids_copy(to).start())
    pltpu.make_async_copy(ids_mine, ids_in.at[pair_me], ids_recv.at[pair_me]).start()
    pltpu.make_async_copy(lf_raw.at[:, chunk(c_me, cw)], lf_in.at[y_me, z_me, c_me], half_recv.at[half_me]).start()
    load_cot.wait()
    pltpu.make_async_copy(cot_columns(pair_me), cot_in.at[pair_me], cot_recv.at[pair_me]).start()
    for c in range(2):
        arrived(lf_in.at[1 - y_me, z_me, c], cross_recv.at[c])
    others(ring_n, z_me, lambda to: relay_copy(to).start())
    others(pair_n, pair_me, lambda to: cot_copy(to).start())

    loads[0].wait()
    loads[1].wait()
    vocab_lane = lax.broadcasted_iota(jnp.int32, (block, LANES), 1).astype(F32)

    def phase_lookup():
        def lookup(i):
            for k in range(4):
                arrived(ids_in.at[4 * i + k], ids_recv.at[4 * i + k])
            rows = [jnp.broadcast_to(ids_in[4 * i + k, 0:1, :], (block, block)) for k in range(4)]
            columns = [jnp.transpose(row) for row in rows]
            for k in range(4):
                for q in range(vocab // LANES):
                    onehot[chunk(4 * i + k, block), q * LANES : (q + 1) * LANES] = (
                        (columns[k] == vocab_lane + float(q * LANES)).astype(F32).astype(BF)
                    )

        loop(pair_n // 4, lookup)

    def phase_embed():
        def embed(i):
            rows = dot(onehot[chunk(i, 4 * block), :], emb[...]).astype(BF)
            for q in range(4):
                s, p = lax.div(4 * i + q, ctx_n), lax.rem(4 * i + q, ctx_n)
                for j in range(4):
                    x[s, j, chunk(p, bs), :] = rows[q * block + j * bs : q * block + (j + 1) * bs]

        loop(pair_n // 4, embed)

    phase_lookup()
    phase_embed()

    row16 = lax.broadcasted_iota(jnp.int32, (bs, LANES), 0)
    def phase_short():
        for h in halves:
            f = [[taps[r, i : i + 1, h] for i in range(3)] for r in range(3)]

            def short(s, h=h, f=f):
                def step(p, carry):
                    rows = chunk(p, bs)
                    xs = [x[s, j, rows, h].astype(F32) for j in range(4)]
                    turned = [pltpu.roll(xs[2], 1, 0), pltpu.roll(xs[3], 1, 0)]
                    late = [jnp.where(row16 == 0, carry[q], turned[q]) for q in range(2)]
                    line = late + xs
                    us = [
                        [f[r][0] * line[j + 2] + f[r][1] * line[j + 1] + f[r][2] * line[j] for j in range(4)]
                        for r in range(3)
                    ]
                    for j in range(4):
                        uq[s, j, rows, h] = us[0][j].astype(BF)
                        uk[s, j, rows, h] = us[1][j].astype(BF)
                        uv[s, j, rows, h] = us[2][j].astype(BF)
                        field[s, j, rows, h] = (us[1][j] * us[2][j]).astype(BF)
                    return tuple(turned)

                zero = jnp.zeros((bs, LANES), F32)
                lax.fori_loop(0, ctx_n, step, (zero, zero))

            loop(2, short)

    phase_short()

    loads[2].wait()

    def field_dft(i):
        s, j = lax.div(i, 4), lax.rem(i, 4)
        pbuf[s, j] = dot(fwd[j], field[s, j]).astype(BF)

    def phase_field_dft():
        loop(8, field_dft, 4)

    phase_field_dft()

    vocab_row = lax.broadcasted_iota(jnp.int32, (vocab, block), 0).astype(F32)

    def phase_lookup_rows():
        def lookup(i):
            lookups[:, chunk(i, block)] = (vocab_row == ids_in[i, 0:1, :]).astype(F32).astype(BF)

        loop(pair_n, lookup)

    phase_lookup_rows()


    def phase_taps():
        def gather_taps(i):
            outs = []
            for k in range(unroll_n):
                pieces = [(unroll_n * i + k) * per + q for q in range(per)]
                rows = [lf_in[lax.div(d, 2 * ring_n), lax.rem(lax.div(d, 2), ring_n), lax.rem(d, 2)] for d in pieces]
                outs.append(dot(perm[0], jnp.concatenate(rows, 0)).astype(BF))
            for k in range(unroll_n):
                for j in range(4):
                    hfield[j, chunk(unroll_n * i + k, bs), :] = outs[k][j * bs : (j + 1) * bs]

        loop(half_n, lambda i: arrived(lf_in.at[y_me, lax.div(i, 2), lax.rem(i, 2)], half_recv.at[i]))
        others(ring_n, z_me, lambda i: arrived(lf_in.at[1 - y_me, i], relay_recv.at[i]))
        loop(ctx_n // unroll_n, gather_taps)

    phase_taps()

    def filter_dft(j):
        hbuf[j] = dot(fwd[j], hfield[j]).astype(BF)

    def phase_filter_dft():
        loop(4, filter_dft, 4)

    phase_filter_dft()

    def butterfly(ref, i, h):
        re = [ref[j, chunk(i, KC), h].astype(F32) for j in range(4)]
        im = [ref[j, pl.ds(pl.multiple_of(sub + i * KC, KC), KC), h].astype(F32) for j in range(4)]
        return radix4(re, im, -1)

    def filter_mix(i):
        for h in halves:
            re, im = butterfly(hbuf, i, h)
            for m in range(4):
                spec_h[m, 0, chunk(i, KC), h] = re[m].astype(BF)
                spec_h[m, 1, chunk(i, KC), h] = im[m].astype(BF)

    def phase_filter_mix():
        loop(sub // KC, filter_mix)

    phase_filter_mix()

    def put(ref, i, h, re, im):
        re, im = radix4(re, im, 1)
        for j in range(4):
            ref[j, chunk(i, KC), h] = re[j].astype(BF)
            ref[j, pl.ds(pl.multiple_of(sub + i * KC, KC), KC), h] = im[j].astype(BF)


    loads[3].wait()

    for s in range(2):

        def conv_mix(i, s=s):
            for h in halves:
                re, im = butterfly(pbuf.at[s], i, h)
                out_re, out_im = [], []
                for m in range(4):
                    spec_z[s, m, 0, chunk(i, KC), h] = re[m].astype(BF)
                    spec_z[s, m, 1, chunk(i, KC), h] = im[m].astype(BF)
                    h_re, h_im = spec_h[m, 0, chunk(i, KC), h].astype(F32), spec_h[m, 1, chunk(i, KC), h].astype(F32)
                    out_re.append(re[m] * h_re - im[m] * h_im)
                    out_im.append(re[m] * h_im + im[m] * h_re)
                put(wbuf.at[s], i, h, out_re, out_im)

        def phase_conv_mix():
            loop(sub // KC, conv_mix)

        phase_conv_mix()

        def conv_idft(j, s=s):
            conv[s, j] = dot(inv[j], wbuf[s, j]).astype(BF)

        def phase_conv_idft():
            loop(4, conv_idft, 4)

        phase_conv_idft()

        def mix(i, s=s):
            outs = []
            for k in range(unroll_n):
                rows = chunk(unroll_n * i + k, bs)
                pieces = [
                    (uq[s, j, rows, :].astype(F32) * conv[s, j, rows, :].astype(F32)).astype(BF) for j in range(4)
                ]
                outs.append(dot(perm[1], jnp.concatenate(pieces, 0)).astype(BF))
            for k in range(unroll_n):
                mixed_out[s * ctx_n + unroll_n * i + k] = outs[k]

        def phase_mix():
            loop(ctx_n // unroll_n, mix)

        phase_mix()

    others(pair_n, pair_me, lambda to: mix_copy(to).start())
    pltpu.make_async_copy(mixed_out.at[pair_me], mixed_hbm.at[0, :, pl.ds(first, cw)], mix_recv.at[pair_me]).start()

    def take(i):
        for k in range(4):
            arrived(cot_in.at[4 * i + k], cot_recv.at[4 * i + k])
        outs = [dot(perm[0], cot_in[4 * i + k]) for k in range(4)]
        for k in range(4):
            s, p = lax.div(4 * i + k, ctx_n), lax.rem(4 * i + k, ctx_n)
            rows = chunk(p, bs)
            for j in range(4):
                piece = outs[k][j * bs : (j + 1) * bs]
                field[s, j, rows, :] = (piece * uq[s, j, rows, :].astype(F32)).astype(BF)
                gq[s, j, rows, :] = (piece * conv[s, j, rows, :].astype(F32)).astype(BF)

    def phase_take():
        loop(pair_n // 4, take)

    phase_take()
    phase_field_dft()

    def back_mix(i):
        for h in halves:
            sum_re, sum_im = None, None
            for s in range(2):
                re, im = butterfly(pbuf.at[s], i, h)
                out_re, out_im, f_re, f_im = [], [], [], []
                for m in range(4):
                    h_re, h_im = spec_h[m, 0, chunk(i, KC), h].astype(F32), spec_h[m, 1, chunk(i, KC), h].astype(F32)
                    z_re, z_im = spec_z[s, m, 0, chunk(i, KC), h].astype(F32), spec_z[s, m, 1, chunk(i, KC), h].astype(F32)
                    out_re.append(re[m] * h_re + im[m] * h_im)
                    out_im.append(im[m] * h_re - re[m] * h_im)
                    f_re.append(re[m] * z_re + im[m] * z_im)
                    f_im.append(im[m] * z_re - re[m] * z_im)
                put(wbuf.at[s], i, h, out_re, out_im)
                if s == 0:
                    sum_re, sum_im = f_re, f_im
                else:
                    sum_re = [a + b for a, b in zip(sum_re, f_re)]
                    sum_im = [a + b for a, b in zip(sum_im, f_im)]
            put(wf, i, h, sum_re, sum_im)

    def phase_back_mix():
        loop(sub // KC, back_mix)

    phase_back_mix()

    def filter_idft(j):
        hfield[j] = dot(inv[j], wf[j]).astype(BF)

    def phase_filter_idft():
        loop(4, filter_idft, 4)

    phase_filter_idft()

    def filter_rows(i):
        outs = []
        for k in range(unroll_n):
            rows = jnp.concatenate([hfield[j, chunk(unroll_n * i + k, bs), :] for j in range(4)], 0)
            outs.append(dot(perm[1], rows).astype(BF))
        for k in range(unroll_n):
            for q in range(per):
                d = (unroll_n * i + k) * per + q
                gf_out[d] = outs[k][q * lr : (q + 1) * lr]

    def phase_filter_rows():
        loop(ctx_n // unroll_n, filter_rows)

    phase_filter_rows()
    others(dp_n, dp, lambda to: gf_copy(to).start())

    def owner_sum(out, arrivals, sems, result):
        others(dp_n, dp, lambda i: arrived(arrivals.at[i], sems.at[i]))
        arrivals[dp] = out[dp]
        for c in range(2):
            total = arrivals[c].astype(F32)
            for i in range(1, dp_n // 2):
                total = total + arrivals[2 * i + c].astype(F32)
            result[:, c * cw : (c + 1) * cw] = total

    def gz_idft(i):
        s, j = lax.div(i, 4), lax.rem(i, 4)
        conv[s, j] = dot(inv[j], wbuf[s, j]).astype(BF)

    def phase_gz_idft():
        loop(8, gz_idft, 4)

    phase_gz_idft()

    def phase_grad():
        for h in halves:
            f = [[taps[r, i : i + 1, h] for i in range(3)] for r in range(3)]

            def grad(s, h=h, f=f):
                def step(i, carry):
                    p = ctx_n - 1 - i
                    rows = chunk(p, bs)
                    lines = [[], [], []]
                    for j in range(4):
                        gz = conv[s, j, rows, h].astype(F32)
                        gs = [
                        gq[s, j, rows, h].astype(F32),
                        gz * uv[s, j, rows, h].astype(F32),
                        gz * uk[s, j, rows, h].astype(F32),
                    ]
                        for tap in range(3):
                            lines[tap].append(f[0][tap] * gs[0] + f[1][tap] * gs[1] + f[2][tap] * gs[2])
                    turned = [pltpu.roll(v, bs - 1, 0) for v in (lines[1][0], lines[2][0], lines[2][1])]
                    early = [jnp.where(row16 == bs - 1, carry[q], turned[q]) for q in range(3)]
                    once = lines[1][1:] + [early[0]]
                    twice = lines[2][2:] + [early[1], early[2]]
                    for j in range(4):
                        gx[s, p, j, :, h] = (lines[0][j] + once[j] + twice[j]).astype(BF)
                    return tuple(turned)

                zero = jnp.zeros((bs, LANES), F32)
                lax.fori_loop(0, ctx_n, step, (zero, zero, zero))

            loop(2, grad)

    phase_grad()

    def phase_scatter():
        ge_out[...] = dot(lookups[...], gx[...].reshape(pair_n * block, cw)).astype(BF).reshape(ge_out.shape)

    phase_scatter()
    others(dp_n, dp, lambda to: ge_copy(to).start())

    owner_sum(gf_out, gf_in, gf_recv, gf_ref)
    owner_sum(ge_out, ge_in, ge_recv, ge_ref)

    def mixed_arrived(i):
        s, p = lax.div(i, ctx_n), lax.rem(i, ctx_n)
        arrived(mixed_hbm.at[0, :, chunk(2 * p + s, cw)], mix_recv.at[i])

    loop(pair_n, mixed_arrived)

    def pair_sent(to):
        ids_copy(to).wait_send()
        cot_copy(to).wait_send()
        mix_copy(to).wait_send()

    def dp_sent(to):
        gf_copy(to).wait_send()
        ge_copy(to).wait_send()

    others(pair_n, pair_me, pair_sent)
    others(dp_n, dp, dp_sent)
    others(half_n, half_me, lambda to: half_copy(to).wait_send())
    others(ring_n, z_me, lambda to: relay_copy(to).wait_send())
    for to in range(2):
        cross_copy(to).wait_send()


def collect(mixed_raw, ge_raw, gf_raw, mixed, ge, gf, mixed_vmem, ge_vmem, gf_vmem, in_sem, out_sem):
    rows = mixed.shape[1] // 4
    moves = [[ref.at[:, pl.ds(i * rows, rows)] for ref in (mixed_raw, mixed_vmem, mixed)] for i in range(4)]
    moves += [[ge_raw, ge_vmem, ge], [gf_raw, gf_vmem, gf]]
    ins = [pltpu.make_async_copy(a, b, in_sem.at[i]) for i, (a, b, _) in enumerate(moves)]
    outs = [pltpu.make_async_copy(b, c, out_sem.at[i]) for i, (_, b, c) in enumerate(moves)]
    for load in ins:
        load.start()
    for load, store in zip(ins, outs):
        load.wait()
        store.start()
    for store in outs:
        store.wait()


def body(token_ids, embedding, short_filter, long_filter, cotangent):
    vocab, width = embedding.shape
    dp_n, ctx_n = lax.axis_size("dp"), lax.axis_size("ctx")
    part = width // ctx_n
    block = token_ids.shape[1]
    length = block * ctx_n
    cw, sub, bs, pair_n = part // 2, length // 4, block // 4, 2 * ctx_n
    lr, vr, ring_n = length // dp_n, vocab // dp_n, dp_n // 4
    fwd, inv = tables(length)
    hbm = pl.BlockSpec(memory_space=pl.ANY)
    vmem = pl.BlockSpec(memory_space=pltpu.VMEM)
    dma = pltpu.SemaphoreType.DMA
    results = pl.pallas_call(
        functools.partial(kernel, (dp_n, ctx_n, vocab, part, block)),
        out_shape=[
            jax.ShapeDtypeStruct((1, block, width), BF),
            jax.ShapeDtypeStruct((vr, part), F32),
            jax.ShapeDtypeStruct((lr, part), F32),
        ],
        in_specs=[hbm, hbm, hbm, hbm, hbm, hbm, hbm],
        out_specs=[hbm, vmem, vmem],
        scratch_shapes=[
            pltpu.VMEM((1, block), jnp.int32),
            pltpu.VMEM((8, block), F32),
            pltpu.VMEM((pair_n, 8, block), F32),
            pltpu.VMEM((2, block, block), BF),
            pltpu.VMEM((vocab, cw), BF),
            pltpu.VMEM((3, 3, cw), F32),
            pltpu.VMEM((2, ring_n, 2, lr, cw), BF),
            pltpu.VMEM((pair_n, block, cw), BF),
            pltpu.VMEM(fwd.shape, BF),
            pltpu.VMEM(inv.shape, BF),
            pltpu.VMEM((2, 4, sub, cw), BF),
            pltpu.VMEM((2, 4, sub, cw), BF),
            pltpu.VMEM((2, 4, sub, cw), BF),
            pltpu.VMEM((2, 4, sub, cw), BF),
            pltpu.VMEM((2, 4, sub, cw), BF),
            pltpu.VMEM((4, sub, cw), BF),
            pltpu.VMEM((4, 2, sub, cw), BF),
            pltpu.VMEM((2, 4, 2, sub, cw), BF),
            pltpu.VMEM((4, 2 * sub, cw), BF),
            pltpu.VMEM((2, 4, 2 * sub, cw), BF),
            pltpu.VMEM((2, 4, 2 * sub, cw), BF),
            pltpu.VMEM((4, 2 * sub, cw), BF),
            pltpu.VMEM((2, 4, sub, cw), BF),
            pltpu.VMEM((2, 4, sub, cw), BF),
            pltpu.VMEM((2, ctx_n, 4, bs, cw), BF),
            pltpu.VMEM((pair_n * block, vocab), BF),
            pltpu.VMEM((vocab, pair_n * block), BF),
            pltpu.VMEM((pair_n, block, cw), BF),
            pltpu.VMEM((dp_n, lr, cw), BF),
            pltpu.VMEM((dp_n, lr, cw), BF),
            pltpu.VMEM((dp_n, vr, cw), BF),
            pltpu.VMEM((dp_n, vr, cw), BF),
            pltpu.VMEM((lr, part), BF),
            pltpu.VMEM((block, width), BF),
            dma((7,)),
            dma((pair_n,)), dma((pair_n,)),
            dma((pair_n,)), dma((pair_n,)),
            dma((pair_n,)), dma((pair_n,)),
            dma((2 * ring_n,)), dma((2 * ring_n,)),
            dma((2,)), dma((2,)),
            dma((ring_n,)), dma((ring_n,)),
            dma((dp_n,)), dma((dp_n,)),
            dma((dp_n,)), dma((dp_n,)),
        ],
        compiler_params=pltpu.CompilerParams(
            collective_id=0, has_side_effects=True, vmem_limit_bytes=56 * 1024 * 1024
        ),
        name="hyena",
    )(token_ids, embedding, short_filter, long_filter, cotangent, fwd, inv)
    return pl.pallas_call(
        collect,
        out_shape=[jax.ShapeDtypeStruct(r.shape, r.dtype) for r in results],
        in_specs=[hbm] * 3,
        out_specs=[hbm] * 3,
        scratch_shapes=[pltpu.VMEM(r.shape, r.dtype) for r in results] + [dma((6,)), dma((6,))],
        compiler_params=pltpu.CompilerParams(vmem_limit_bytes=56 * 1024 * 1024),
        name="collect",
    )(*results)


def solution(mesh):
    in_specs = (P("dp", "ctx"), P(), P(), P("dp", "ctx"), P("dp", "ctx", None))
    out_specs = (P("dp", "ctx", None), P("dp", "ctx"), P("dp", "ctx"))
    return jax.shard_map(body, mesh=mesh, in_specs=in_specs, out_specs=out_specs, check_vma=False)
```

```python
import functools
import math

import jax
import jax.numpy as jnp
import numpy as np
from jax import lax
from jax.experimental import pallas as pl
from jax.experimental.pallas import tpu as pltpu
from jax.sharding import PartitionSpec as P

BF = jnp.bfloat16
F32 = jnp.float32
MESH = pl.DeviceIdType.MESH
LANES = 128
KC = 16


def tables(length):
    sub = length // 4
    k = np.arange(sub)[None, :, None]
    t = 4 * np.arange(sub)[None, None, :] + np.arange(4)[:, None, None]
    angle = 2.0 * math.pi * (((4 * k + 1) * t) % (4 * length)) / (4 * length)
    fwd = np.concatenate([np.cos(angle), -np.sin(angle)], 1)
    inv = fwd.transpose(0, 2, 1) / length
    return jnp.asarray(fwd, BF), jnp.asarray(inv, BF)


def radix4(re, im, sign):
    a_re, a_im, b_re, b_im = re[0] + re[2], im[0] + im[2], re[0] - re[2], im[0] - im[2]
    c_re, c_im, d_re, d_im = re[1] + re[3], im[1] + im[3], re[1] - re[3], im[1] - im[3]
    if sign > 0:
        d_re, d_im = -d_re, -d_im
    return (
        [a_re + c_re, b_re + d_im, a_re - c_re, b_re - d_im],
        [a_im + c_im, b_im - d_re, a_im - c_im, b_im + d_re],
    )


def loop(count, step, unroll=1):
    def run(i, carry):
        for q in range(unroll):
            step(i * unroll + q)
        return carry

    lax.fori_loop(0, count // unroll, run, 0)


def dot(a, b):
    return jnp.dot(a, b, preferred_element_type=F32)


def kernel(
    dims,
    ids_hbm, emb_hbm, taps_hbm, lf_hbm, cot_hbm, fwd_hbm, inv_hbm,
    mixed_hbm, ge_ref, gf_ref,
    ids_raw, ids_mine, ids_in, perm, emb, taps, lf_in, cot_in, fwd, inv,
    x, uq, uk, uv, field, hfield, spec_h, spec_z, hbuf, pbuf, wbuf, wf, conv, gq, gx,
    onehot, lookups, mixed_out, gf_out, gf_in, ge_out, ge_in, lf_raw, cot_raw,
    local_sem, ids_send, ids_recv, cot_send, cot_recv, mix_send, mix_recv, half_send, half_recv,
    cross_send, cross_recv, relay_send, relay_recv, gf_send, gf_recv, ge_send, ge_recv,
):
    dp_n, ctx_n, vocab, part, block = dims
    cw = part // 2
    sub = ctx_n * block // 4
    bs = block // 4
    pair_n = 2 * ctx_n
    per = dp_n // ctx_n
    lr = block // per
    vr = vocab // dp_n
    dp = lax.axis_index("dp")
    p_me = lax.axis_index("ctx")
    g = lax.div(dp, 2)
    c_me = lax.rem(dp, 2)
    ring_n = dp_n // 4
    y_me, z_me = lax.div(g, ring_n), lax.rem(g, ring_n)
    half_n, half_me = 2 * ring_n, 2 * z_me + c_me
    pair_me = c_me * ctx_n + p_me
    first = pl.multiple_of(p_me * part + c_me * cw, cw)
    halves = [pl.ds(h * LANES, LANES) for h in range(cw // LANES)]

    unroll_n = 4 if ctx_n % 4 == 0 else 2

    def chunk(i, size):
        return pl.ds(pl.multiple_of(i * size, size), size)

    loads = [
        pltpu.make_async_copy(emb_hbm.at[:, pl.ds(first, cw)], emb, local_sem.at[0]),
        pltpu.make_async_copy(taps_hbm.at[:, :, pl.ds(first, cw)], taps, local_sem.at[1]),
        pltpu.make_async_copy(fwd_hbm, fwd, local_sem.at[2]),
        pltpu.make_async_copy(inv_hbm, inv, local_sem.at[3]),
    ]
    load_ids = pltpu.make_async_copy(ids_hbm, ids_raw, local_sem.at[4])
    load_ids.start()
    load_lf = pltpu.make_async_copy(lf_hbm, lf_raw, local_sem.at[5])
    load_lf.start()
    load_cot = pltpu.make_async_copy(cot_hbm.at[0], cot_raw, local_sem.at[6])
    load_cot.start()
    for load in loads:
        load.start()

    barrier = pltpu.get_barrier_semaphore()

    def greet_pair(i):
        to = lax.rem(pair_me + 1 + i, pair_n)
        device = (2 * g + lax.div(to, ctx_n), lax.rem(to, ctx_n))
        pl.semaphore_signal(barrier, inc=1, device_id=device, device_id_type=MESH)

    def greet_dp(i):
        device = (lax.rem(dp + 1 + i, dp_n), p_me)
        pl.semaphore_signal(barrier, inc=1, device_id=device, device_id_type=MESH)

    loop(pair_n - 1, greet_pair)
    loop(dp_n - 1, greet_dp)
    def natural(axis):
        place = lax.broadcasted_iota(jnp.int32, (block, block), axis)
        return 4 * (place & (bs - 1)) + (place >> (bs.bit_length() - 1))

    perm[0] = (natural(0) == lax.broadcasted_iota(jnp.int32, (block, block), 1)).astype(F32).astype(BF)
    perm[1] = (natural(1) == lax.broadcasted_iota(jnp.int32, (block, block), 0)).astype(F32).astype(BF)

    load_ids.wait()
    ids = jnp.broadcast_to(ids_raw[...].astype(F32), (8, block))
    high = jnp.where(ids >= 256.0, 1.0, 0.0)
    low = ids - 256.0 * high
    ids_mine[...] = dot(low.astype(BF), perm[1]) + 256.0 * dot(high.astype(BF), perm[1])
    pl.semaphore_wait(barrier, pair_n - 1 + dp_n - 1)

    def ids_copy(to):
        return pltpu.make_async_remote_copy(
            src_ref=ids_mine, dst_ref=ids_in.at[pair_me], send_sem=ids_send, recv_sem=ids_recv,
            device_id=(2 * g + lax.div(to, ctx_n), lax.rem(to, ctx_n)), device_id_type=MESH,
        )

    def half_copy(to):
        return pltpu.make_async_remote_copy(
            src_ref=lf_raw.at[:, chunk(lax.rem(to, 2), cw)], dst_ref=lf_in.at[y_me, z_me, c_me],
            send_sem=half_send, recv_sem=half_recv,
            device_id=(y_me * half_n + to, p_me), device_id_type=MESH,
        )

    def cross_copy(to):
        return pltpu.make_async_remote_copy(
            src_ref=lf_raw.at[:, to * cw : (to + 1) * cw], dst_ref=lf_in.at[y_me, z_me, c_me],
            send_sem=cross_send, recv_sem=cross_recv,
            device_id=((1 - y_me) * half_n + 2 * z_me + to, p_me), device_id_type=MESH,
        )

    def relay_copy(to):
        return pltpu.make_async_remote_copy(
            src_ref=lf_in.at[1 - y_me, z_me], dst_ref=lf_in.at[1 - y_me, z_me],
            send_sem=relay_send, recv_sem=relay_recv,
            device_id=(y_me * half_n + 2 * to + c_me, p_me), device_id_type=MESH,
        )

    def cot_columns(to):
        return cot_raw.at[:, chunk(2 * lax.rem(to, ctx_n) + lax.div(to, ctx_n), cw)]

    def cot_copy(to):
        return pltpu.make_async_remote_copy(
            src_ref=cot_columns(to), dst_ref=cot_in.at[pair_me], send_sem=cot_send, recv_sem=cot_recv,
            device_id=(2 * g + lax.div(to, ctx_n), lax.rem(to, ctx_n)), device_id_type=MESH,
        )

    def mix_copy(to):
        return pltpu.make_async_remote_copy(
            src_ref=mixed_out.at[to], dst_ref=mixed_hbm.at[0, :, pl.ds(first, cw)],
            send_sem=mix_send, recv_sem=mix_recv,
            device_id=(2 * g + lax.div(to, ctx_n), lax.rem(to, ctx_n)), device_id_type=MESH,
        )

    def gf_copy(to):
        return pltpu.make_async_remote_copy(
            src_ref=gf_out.at[to], dst_ref=gf_in.at[dp], send_sem=gf_send, recv_sem=gf_recv,
            device_id=(to, p_me), device_id_type=MESH,
        )

    def ge_copy(to):
        return pltpu.make_async_remote_copy(
            src_ref=ge_out.at[to], dst_ref=ge_in.at[dp], send_sem=ge_send, recv_sem=ge_recv,
            device_id=(to, p_me), device_id_type=MESH,
        )

    def others(count, me, step):
        loop(count - 1, lambda i: step(lax.rem(me + 1 + i, count)))

    def arrived(slot, sem):
        pltpu.make_async_copy(slot, slot, sem).wait()

    load_lf.wait()
    for to in range(2):
        cross_copy(to).start()
    others(half_n, half_me, lambda to: half_copy(to).start())
    others(pair_n, pair_me, lambda to: ids_copy(to).start())
    pltpu.make_async_copy(ids_mine, ids_in.at[pair_me], ids_recv).start()
    pltpu.make_async_copy(lf_raw.at[:, chunk(c_me, cw)], lf_in.at[y_me, z_me, c_me], half_recv).start()
    load_cot.wait()
    pltpu.make_async_copy(cot_columns(pair_me), cot_in.at[pair_me], cot_recv).start()
    arrived(lf_in.at[1 - y_me, z_me], cross_recv)
    others(ring_n, z_me, lambda to: relay_copy(to).start())
    others(pair_n, pair_me, lambda to: cot_copy(to).start())

    loads[0].wait()
    loads[1].wait()
    vocab_lane = lax.broadcasted_iota(jnp.int32, (block, LANES), 1).astype(F32)

    def phase_lookup():
        def lookup(i):
            rows = [jnp.broadcast_to(ids_in[4 * i + k, 0:1, :], (block, block)) for k in range(4)]
            columns = [jnp.transpose(row) for row in rows]
            for k in range(4):
                for q in range(vocab // LANES):
                    onehot[chunk(4 * i + k, block), q * LANES : (q + 1) * LANES] = (
                        (columns[k] == vocab_lane + float(q * LANES)).astype(F32).astype(BF)
                    )

        arrived(ids_in, ids_recv)
        loop(pair_n // 4, lookup)

    def phase_embed():
        def embed(i):
            rows = dot(onehot[chunk(i, 4 * block), :], emb[...])
            for q in range(4):
                s, p = lax.div(4 * i + q, ctx_n), lax.rem(4 * i + q, ctx_n)
                for j in range(4):
                    x[s, j, chunk(p, bs), :] = rows[q * block + j * bs : q * block + (j + 1) * bs]

        loop(pair_n // 4, embed)

    phase_lookup()
    phase_embed()

    row16 = lax.broadcasted_iota(jnp.int32, (bs, LANES), 0)
    def phase_short():
        for h in halves:
            f = [[taps[r, i : i + 1, h] for i in range(3)] for r in range(3)]

            def short(s, h=h, f=f):
                def step(p, carry):
                    rows = chunk(p, bs)
                    xs = [x[s, j, rows, h] for j in range(4)]
                    turned = [pltpu.roll(xs[2], 1, 0), pltpu.roll(xs[3], 1, 0)]
                    late = [jnp.where(row16 == 0, carry[q], turned[q]) for q in range(2)]
                    line = late + xs
                    us = [
                        [f[r][0] * line[j + 2] + f[r][1] * line[j + 1] + f[r][2] * line[j] for j in range(4)]
                        for r in range(3)
                    ]
                    for j in range(4):
                        uq[s, j, rows, h] = us[0][j]
                        uk[s, j, rows, h] = us[1][j]
                        uv[s, j, rows, h] = us[2][j]
                        field[s, j, rows, h] = (us[1][j] * us[2][j]).astype(BF)
                    return tuple(turned)

                zero = jnp.zeros((bs, LANES), F32)
                lax.fori_loop(0, ctx_n, step, (zero, zero))

            loop(2, short)

    phase_short()

    loads[2].wait()

    def field_dft(i):
        s, j = lax.div(i, 4), lax.rem(i, 4)
        pbuf[s, j] = dot(fwd[j], field[s, j])

    def phase_field_dft():
        loop(8, field_dft, 4)

    phase_field_dft()

    vocab_row = lax.broadcasted_iota(jnp.int32, (vocab, block), 0).astype(F32)

    def phase_lookup_rows():
        def lookup(i):
            lookups[:, chunk(i, block)] = (vocab_row == ids_in[i, 0:1, :]).astype(F32).astype(BF)

        loop(pair_n, lookup)

    phase_lookup_rows()


    def phase_taps():
        def gather_taps(i):
            outs = []
            for k in range(unroll_n):
                pieces = [(unroll_n * i + k) * per + q for q in range(per)]
                rows = [lf_in[lax.div(d, 2 * ring_n), lax.rem(lax.div(d, 2), ring_n), lax.rem(d, 2)] for d in pieces]
                outs.append(dot(perm[0], jnp.concatenate(rows, 0)).astype(BF))
            for k in range(unroll_n):
                for j in range(4):
                    hfield[j, chunk(unroll_n * i + k, bs), :] = outs[k][j * bs : (j + 1) * bs]

        arrived(lf_in.at[y_me], half_recv)
        arrived(lf_in.at[1 - y_me, pl.ds(0, ring_n - 1)], relay_recv)
        loop(ctx_n // unroll_n, gather_taps)

    phase_taps()

    def filter_dft(j):
        hbuf[j] = dot(fwd[j], hfield[j])

    def phase_filter_dft():
        loop(4, filter_dft, 4)

    phase_filter_dft()

    def butterfly(ref, i, h):
        re = [ref[j, chunk(i, KC), h] for j in range(4)]
        im = [ref[j, pl.ds(pl.multiple_of(sub + i * KC, KC), KC), h] for j in range(4)]
        return radix4(re, im, -1)

    def filter_mix(i):
        for h in halves:
            re, im = butterfly(hbuf, i, h)
            for m in range(4):
                spec_h[m, 0, chunk(i, KC), h] = re[m]
                spec_h[m, 1, chunk(i, KC), h] = im[m]

    def phase_filter_mix():
        loop(sub // KC, filter_mix)

    phase_filter_mix()

    def put(ref, i, h, re, im):
        re, im = radix4(re, im, 1)
        for j in range(4):
            ref[j, chunk(i, KC), h] = re[j].astype(BF)
            ref[j, pl.ds(pl.multiple_of(sub + i * KC, KC), KC), h] = im[j].astype(BF)


    loads[3].wait()

    for s in range(2):

        def conv_mix(i, s=s):
            for h in halves:
                re, im = butterfly(pbuf.at[s], i, h)
                out_re, out_im = [], []
                for m in range(4):
                    spec_z[s, m, 0, chunk(i, KC), h] = re[m]
                    spec_z[s, m, 1, chunk(i, KC), h] = im[m]
                    h_re, h_im = spec_h[m, 0, chunk(i, KC), h], spec_h[m, 1, chunk(i, KC), h]
                    out_re.append(re[m] * h_re - im[m] * h_im)
                    out_im.append(re[m] * h_im + im[m] * h_re)
                put(wbuf.at[s], i, h, out_re, out_im)

        def phase_conv_mix():
            loop(sub // KC, conv_mix)

        phase_conv_mix()

        def conv_idft(j, s=s):
            conv[s, j] = dot(inv[j], wbuf[s, j]).astype(BF).astype(F32)

        def phase_conv_idft():
            loop(4, conv_idft, 4)

        phase_conv_idft()

        def mix(i, s=s):
            outs = []
            for k in range(unroll_n):
                rows = chunk(unroll_n * i + k, bs)
                pieces = [
                    (uq[s, j, rows, :] * conv[s, j, rows, :]).astype(BF) for j in range(4)
                ]
                outs.append(dot(perm[1], jnp.concatenate(pieces, 0)).astype(BF))
            for k in range(unroll_n):
                mixed_out[s * ctx_n + unroll_n * i + k] = outs[k]

        def phase_mix():
            loop(ctx_n // unroll_n, mix)

        phase_mix()

    others(pair_n, pair_me, lambda to: mix_copy(to).start())
    pltpu.make_async_copy(mixed_out.at[pair_me], mixed_hbm.at[0, :, pl.ds(first, cw)], mix_recv).start()

    def take(i):
        outs = [dot(perm[0], cot_in[4 * i + k]) for k in range(4)]
        for k in range(4):
            s, p = lax.div(4 * i + k, ctx_n), lax.rem(4 * i + k, ctx_n)
            rows = chunk(p, bs)
            for j in range(4):
                piece = outs[k][j * bs : (j + 1) * bs]
                field[s, j, rows, :] = (piece * uq[s, j, rows, :]).astype(BF)
                gq[s, j, rows, :] = piece * conv[s, j, rows, :]

    def phase_take():
        arrived(cot_in, cot_recv)
        loop(pair_n // 4, take)

    phase_take()
    phase_field_dft()

    def back_mix(i):
        for h in halves:
            sum_re, sum_im = None, None
            for s in range(2):
                re, im = butterfly(pbuf.at[s], i, h)
                out_re, out_im, f_re, f_im = [], [], [], []
                for m in range(4):
                    h_re, h_im = spec_h[m, 0, chunk(i, KC), h], spec_h[m, 1, chunk(i, KC), h]
                    z_re, z_im = spec_z[s, m, 0, chunk(i, KC), h], spec_z[s, m, 1, chunk(i, KC), h]
                    out_re.append(re[m] * h_re + im[m] * h_im)
                    out_im.append(im[m] * h_re - re[m] * h_im)
                    f_re.append(re[m] * z_re + im[m] * z_im)
                    f_im.append(im[m] * z_re - re[m] * z_im)
                put(wbuf.at[s], i, h, out_re, out_im)
                if s == 0:
                    sum_re, sum_im = f_re, f_im
                else:
                    sum_re = [a + b for a, b in zip(sum_re, f_re)]
                    sum_im = [a + b for a, b in zip(sum_im, f_im)]
            put(wf, i, h, sum_re, sum_im)

    def phase_back_mix():
        loop(sub // KC, back_mix)

    phase_back_mix()

    def filter_idft(j):
        hfield[j] = dot(inv[j], wf[j]).astype(BF)

    def phase_filter_idft():
        loop(4, filter_idft, 4)

    phase_filter_idft()

    def filter_rows(i):
        outs = []
        for k in range(unroll_n):
            rows = jnp.concatenate([hfield[j, chunk(unroll_n * i + k, bs), :] for j in range(4)], 0)
            outs.append(dot(perm[1], rows).astype(BF))
        for k in range(unroll_n):
            for q in range(per):
                d = (unroll_n * i + k) * per + q
                gf_out[d] = outs[k][q * lr : (q + 1) * lr]

    def phase_filter_rows():
        loop(ctx_n // unroll_n, filter_rows)

    phase_filter_rows()
    others(dp_n, dp, lambda to: gf_copy(to).start())
    pltpu.make_async_copy(gf_out.at[dp], gf_in.at[dp], gf_recv).start()

    def owner_sum(arrivals, sems, result):
        arrived(arrivals, sems)
        for c in range(2):
            total = arrivals[c].astype(F32)
            for i in range(1, dp_n // 2):
                total = total + arrivals[2 * i + c].astype(F32)
            result[:, c * cw : (c + 1) * cw] = total

    def gz_idft(i):
        s, j = lax.div(i, 4), lax.rem(i, 4)
        conv[s, j] = dot(inv[j], wbuf[s, j])

    def phase_gz_idft():
        loop(8, gz_idft, 4)

    phase_gz_idft()

    def phase_grad():
        for h in halves:
            f = [[taps[r, i : i + 1, h] for i in range(3)] for r in range(3)]

            def grad(s, h=h, f=f):
                def step(i, carry):
                    p = ctx_n - 1 - i
                    rows = chunk(p, bs)
                    lines = [[], [], []]
                    for j in range(4):
                        gz = conv[s, j, rows, h].astype(BF).astype(F32)
                        gs = [
                        gq[s, j, rows, h],
                        gz * uv[s, j, rows, h],
                        gz * uk[s, j, rows, h],
                    ]
                        for tap in range(3):
                            lines[tap].append(f[0][tap] * gs[0] + f[1][tap] * gs[1] + f[2][tap] * gs[2])
                    turned = [pltpu.roll(v, bs - 1, 0) for v in (lines[1][0], lines[2][0], lines[2][1])]
                    early = [jnp.where(row16 == bs - 1, carry[q], turned[q]) for q in range(3)]
                    once = lines[1][1:] + [early[0]]
                    twice = lines[2][2:] + [early[1], early[2]]
                    for j in range(4):
                        gx[s, p, j, :, h] = (lines[0][j] + once[j] + twice[j]).astype(BF)
                    return tuple(turned)

                zero = jnp.zeros((bs, LANES), F32)
                lax.fori_loop(0, ctx_n, step, (zero, zero, zero))

            loop(2, grad)

    phase_grad()

    def phase_scatter():
        ge_out[...] = dot(lookups[...], gx[...].reshape(pair_n * block, cw)).astype(BF).reshape(ge_out.shape)

    phase_scatter()
    others(dp_n, dp, lambda to: ge_copy(to).start())
    pltpu.make_async_copy(ge_out.at[dp], ge_in.at[dp], ge_recv).start()

    owner_sum(gf_in, gf_recv, gf_ref)
    owner_sum(ge_in, ge_recv, ge_ref)

    def sent(ref, sem):
        pltpu.make_async_copy(ref, ref, sem).wait()

    sent(ids_in.at[pl.ds(0, pair_n - 1)], ids_send)
    sent(lf_in.at[:, 0, 0], cross_send)
    sent(gf_in.at[pl.ds(0, half_n - 1)], half_send)
    sent(lf_in.at[0, pl.ds(0, ring_n - 1)], relay_send)
    sent(cot_in.at[pl.ds(0, pair_n - 1)], cot_send)
    sent(gf_in.at[pl.ds(0, dp_n - 1)], gf_send)
    sent(ge_in.at[pl.ds(0, dp_n - 1)], ge_send)
    sent(mixed_out.at[pl.ds(0, pair_n - 1)], mix_send)
    arrived(mixed_hbm.at[0], mix_recv)


def collect(mixed_raw, ge_raw, gf_raw, mixed, ge, gf, mixed_vmem, ge_vmem, gf_vmem, in_sem, out_sem):
    rows = mixed.shape[1] // 4
    moves = [[ref.at[:, pl.ds(i * rows, rows)] for ref in (mixed_raw, mixed_vmem, mixed)] for i in range(4)]
    moves += [[ge_raw, ge_vmem, ge], [gf_raw, gf_vmem, gf]]
    ins = [pltpu.make_async_copy(a, b, in_sem.at[i]) for i, (a, b, _) in enumerate(moves)]
    outs = [pltpu.make_async_copy(b, c, out_sem.at[i]) for i, (_, b, c) in enumerate(moves)]
    for load in ins:
        load.start()
    for load, store in zip(ins, outs):
        load.wait()
        store.start()
    for store in outs:
        store.wait()


def body(token_ids, embedding, short_filter, long_filter, cotangent):
    vocab, width = embedding.shape
    dp_n, ctx_n = lax.axis_size("dp"), lax.axis_size("ctx")
    part = width // ctx_n
    block = token_ids.shape[1]
    length = block * ctx_n
    cw, sub, bs, pair_n = part // 2, length // 4, block // 4, 2 * ctx_n
    lr, vr, ring_n = length // dp_n, vocab // dp_n, dp_n // 4
    fwd, inv = tables(length)
    hbm = pl.BlockSpec(memory_space=pl.ANY)
    vmem = pl.BlockSpec(memory_space=pltpu.VMEM)
    dma = pltpu.SemaphoreType.DMA
    results = pl.pallas_call(
        functools.partial(kernel, (dp_n, ctx_n, vocab, part, block)),
        out_shape=[
            jax.ShapeDtypeStruct((1, block, width), BF),
            jax.ShapeDtypeStruct((vr, part), F32),
            jax.ShapeDtypeStruct((lr, part), F32),
        ],
        in_specs=[hbm, hbm, hbm, hbm, hbm, hbm, hbm],
        out_specs=[hbm, vmem, vmem],
        scratch_shapes=[
            pltpu.VMEM((1, block), jnp.int32),
            pltpu.VMEM((8, block), F32),
            pltpu.VMEM((pair_n, 8, block), F32),
            pltpu.VMEM((2, block, block), BF),
            pltpu.VMEM((vocab, cw), BF),
            pltpu.VMEM((3, 3, cw), F32),
            pltpu.VMEM((2, ring_n, 2, lr, cw), BF),
            pltpu.VMEM((pair_n, block, cw), BF),
            pltpu.VMEM(fwd.shape, BF),
            pltpu.VMEM(inv.shape, BF),
            pltpu.VMEM((2, 4, sub, cw), F32),
            pltpu.VMEM((2, 4, sub, cw), F32),
            pltpu.VMEM((2, 4, sub, cw), F32),
            pltpu.VMEM((2, 4, sub, cw), F32),
            pltpu.VMEM((2, 4, sub, cw), BF),
            pltpu.VMEM((4, sub, cw), BF),
            pltpu.VMEM((4, 2, sub, cw), F32),
            pltpu.VMEM((2, 4, 2, sub, cw), F32),
            pltpu.VMEM((4, 2 * sub, cw), F32),
            pltpu.VMEM((2, 4, 2 * sub, cw), F32),
            pltpu.VMEM((2, 4, 2 * sub, cw), BF),
            pltpu.VMEM((4, 2 * sub, cw), BF),
            pltpu.VMEM((2, 4, sub, cw), F32),
            pltpu.VMEM((2, 4, sub, cw), F32),
            pltpu.VMEM((2, ctx_n, 4, bs, cw), BF),
            pltpu.VMEM((pair_n * block, vocab), BF),
            pltpu.VMEM((vocab, pair_n * block), BF),
            pltpu.VMEM((pair_n, block, cw), BF),
            pltpu.VMEM((dp_n, lr, cw), BF),
            pltpu.VMEM((dp_n, lr, cw), BF),
            pltpu.VMEM((dp_n, vr, cw), BF),
            pltpu.VMEM((dp_n, vr, cw), BF),
            pltpu.VMEM((lr, part), BF),
            pltpu.VMEM((block, width), BF),
            dma((7,)),
        ] + [dma] * 16,
        compiler_params=pltpu.CompilerParams(
            collective_id=0, has_side_effects=True, vmem_limit_bytes=56 * 1024 * 1024
        ),
        name="hyena",
    )(token_ids, embedding, short_filter, long_filter, cotangent, fwd, inv)
    return pl.pallas_call(
        collect,
        out_shape=[jax.ShapeDtypeStruct(r.shape, r.dtype) for r in results],
        in_specs=[hbm] * 3,
        out_specs=[hbm] * 3,
        scratch_shapes=[pltpu.VMEM(r.shape, r.dtype) for r in results] + [dma((6,)), dma((6,))],
        compiler_params=pltpu.CompilerParams(vmem_limit_bytes=56 * 1024 * 1024),
        name="collect",
    )(*results)


def solution(mesh):
    in_specs = (P("dp", "ctx"), P(), P(), P("dp", "ctx"), P("dp", "ctx", None))
    out_specs = (P("dp", "ctx", None), P("dp", "ctx"), P("dp", "ctx"))
    return jax.shard_map(body, mesh=mesh, in_specs=in_specs, out_specs=out_specs, check_vma=False)
```

```python
import functools
import math

import jax
import jax.numpy as jnp
import numpy as np
from jax import lax
from jax.experimental import pallas as pl
from jax.experimental.pallas import tpu as pltpu
from jax.sharding import PartitionSpec as P

BF = jnp.bfloat16
F32 = jnp.float32
MESH = pl.DeviceIdType.MESH
LANES = 128
KC = 16


def tables(length):
    sub = length // 4
    k = np.arange(sub)[None, :, None]
    t = 4 * np.arange(sub)[None, None, :] + np.arange(4)[:, None, None]
    angle = 2.0 * math.pi * (((4 * k + 1) * t) % (4 * length)) / (4 * length)
    fwd = np.concatenate([np.cos(angle), -np.sin(angle)], 1)
    inv = fwd.transpose(0, 2, 1) / length
    return jnp.asarray(fwd, BF), jnp.asarray(inv, BF)


def radix4(re, im, sign):
    a_re, a_im, b_re, b_im = re[0] + re[2], im[0] + im[2], re[0] - re[2], im[0] - im[2]
    c_re, c_im, d_re, d_im = re[1] + re[3], im[1] + im[3], re[1] - re[3], im[1] - im[3]
    if sign > 0:
        d_re, d_im = -d_re, -d_im
    return (
        [a_re + c_re, b_re + d_im, a_re - c_re, b_re - d_im],
        [a_im + c_im, b_im - d_re, a_im - c_im, b_im + d_re],
    )


def loop(count, step, unroll=1):
    def run(i, carry):
        for q in range(unroll):
            step(i * unroll + q)
        return carry

    lax.fori_loop(0, count // unroll, run, 0)


def dot(a, b):
    return jnp.dot(a, b, preferred_element_type=F32)


def kernel(
    dims,
    ids_hbm, emb_hbm, taps_hbm, lf_hbm, cot_hbm, fwd_hbm, inv_hbm,
    mixed_hbm, ge_ref, gf_ref,
    ids_raw, ids_mine, ids_in, perm, emb, taps, lf_in, cot_in, fwd, inv,
    x, uq, uk, uv, field, hfield, spec_h, spec_z, hbuf, pbuf, wbuf, wf, conv, gq, gx,
    onehot, lookups, mixed_out, gf_out, gf_in, ge_out, ge_in, lf_raw, cot_raw,
    local_sem, ids_send, ids_recv, cot_send, cot_recv, mix_send, mix_recv, half_send, half_recv,
    cross_send, cross_recv, relay_send, relay_recv, gf_send, gf_recv, ge_send, ge_recv,
):
    dp_n, ctx_n, vocab, part, block = dims
    cw = part // 2
    sub = ctx_n * block // 4
    bs = block // 4
    pair_n = 2 * ctx_n
    per = dp_n // ctx_n
    lr = block // per
    vr = vocab // dp_n
    dp = lax.axis_index("dp")
    p_me = lax.axis_index("ctx")
    g = lax.div(dp, 2)
    c_me = lax.rem(dp, 2)
    ring_n = dp_n // 4
    y_me, z_me = lax.div(g, ring_n), lax.rem(g, ring_n)
    half_n, half_me = 2 * ring_n, 2 * z_me + c_me
    pair_me = c_me * ctx_n + p_me
    first = pl.multiple_of(p_me * part + c_me * cw, cw)
    halves = [pl.ds(h * LANES, LANES) for h in range(cw // LANES)]

    unroll_n = 4 if ctx_n % 4 == 0 else 2

    def chunk(i, size):
        return pl.ds(pl.multiple_of(i * size, size), size)

    loads = [
        pltpu.make_async_copy(emb_hbm.at[:, pl.ds(first, cw)], emb, local_sem.at[0]),
        pltpu.make_async_copy(taps_hbm.at[:, :, pl.ds(first, cw)], taps, local_sem.at[1]),
        pltpu.make_async_copy(fwd_hbm, fwd, local_sem.at[2]),
        pltpu.make_async_copy(inv_hbm, inv, local_sem.at[3]),
    ]
    load_ids = pltpu.make_async_copy(ids_hbm, ids_raw, local_sem.at[4])
    load_ids.start()
    load_lf = pltpu.make_async_copy(lf_hbm, lf_raw, local_sem.at[5])
    load_lf.start()
    load_cot = pltpu.make_async_copy(cot_hbm.at[0], cot_raw, local_sem.at[6])
    load_cot.start()
    for load in loads:
        load.start()

    barrier = pltpu.get_barrier_semaphore()

    def greet_pair(i):
        to = lax.rem(pair_me + 1 + i, pair_n)
        device = (2 * g + lax.div(to, ctx_n), lax.rem(to, ctx_n))
        pl.semaphore_signal(barrier, inc=1, device_id=device, device_id_type=MESH)

    def greet_dp(i):
        device = (lax.rem(dp + 1 + i, dp_n), p_me)
        pl.semaphore_signal(barrier, inc=1, device_id=device, device_id_type=MESH)

    loop(pair_n - 1, greet_pair)
    loop(dp_n - 1, greet_dp)
    def natural(axis):
        place = lax.broadcasted_iota(jnp.int32, (block, block), axis)
        return 4 * (place & (bs - 1)) + (place >> (bs.bit_length() - 1))

    perm[0] = (natural(0) == lax.broadcasted_iota(jnp.int32, (block, block), 1)).astype(F32).astype(BF)
    perm[1] = (natural(1) == lax.broadcasted_iota(jnp.int32, (block, block), 0)).astype(F32).astype(BF)

    load_ids.wait()
    ids = jnp.broadcast_to(ids_raw[...].astype(F32), (8, block))
    high = jnp.where(ids >= 256.0, 1.0, 0.0)
    low = ids - 256.0 * high
    ids_mine[...] = dot(low.astype(BF), perm[1]) + 256.0 * dot(high.astype(BF), perm[1])
    pl.semaphore_wait(barrier, pair_n - 1 + dp_n - 1)

    def ids_copy(to):
        return pltpu.make_async_remote_copy(
            src_ref=ids_mine, dst_ref=ids_in.at[pair_me], send_sem=ids_send, recv_sem=ids_recv,
            device_id=(2 * g + lax.div(to, ctx_n), lax.rem(to, ctx_n)), device_id_type=MESH,
        )

    def half_copy(to):
        return pltpu.make_async_remote_copy(
            src_ref=lf_raw.at[:, chunk(lax.rem(to, 2), cw)], dst_ref=lf_in.at[y_me, z_me, c_me],
            send_sem=half_send, recv_sem=half_recv,
            device_id=(y_me * half_n + to, p_me), device_id_type=MESH,
        )

    def cross_copy(to):
        return pltpu.make_async_remote_copy(
            src_ref=lf_raw.at[:, to * cw : (to + 1) * cw], dst_ref=lf_in.at[y_me, z_me, c_me],
            send_sem=cross_send, recv_sem=cross_recv,
            device_id=((1 - y_me) * half_n + 2 * z_me + to, p_me), device_id_type=MESH,
        )

    def relay_copy(to):
        return pltpu.make_async_remote_copy(
            src_ref=lf_in.at[1 - y_me, z_me], dst_ref=lf_in.at[1 - y_me, z_me],
            send_sem=relay_send, recv_sem=relay_recv,
            device_id=(y_me * half_n + 2 * to + c_me, p_me), device_id_type=MESH,
        )

    def cot_columns(to):
        return cot_raw.at[:, chunk(2 * lax.rem(to, ctx_n) + lax.div(to, ctx_n), cw)]

    def cot_copy(to):
        return pltpu.make_async_remote_copy(
            src_ref=cot_columns(to), dst_ref=cot_in.at[pair_me], send_sem=cot_send, recv_sem=cot_recv,
            device_id=(2 * g + lax.div(to, ctx_n), lax.rem(to, ctx_n)), device_id_type=MESH,
        )

    def mix_copy(to):
        return pltpu.make_async_remote_copy(
            src_ref=mixed_out.at[to], dst_ref=mixed_hbm.at[0, :, pl.ds(first, cw)],
            send_sem=mix_send, recv_sem=mix_recv,
            device_id=(2 * g + lax.div(to, ctx_n), lax.rem(to, ctx_n)), device_id_type=MESH,
        )

    def gf_copy(to):
        return pltpu.make_async_remote_copy(
            src_ref=gf_out.at[to], dst_ref=gf_in.at[dp], send_sem=gf_send, recv_sem=gf_recv,
            device_id=(to, p_me), device_id_type=MESH,
        )

    def ge_copy(to):
        return pltpu.make_async_remote_copy(
            src_ref=ge_out.at[to], dst_ref=ge_in.at[dp], send_sem=ge_send, recv_sem=ge_recv,
            device_id=(to, p_me), device_id_type=MESH,
        )

    def others(count, me, step):
        loop(count - 1, lambda i: step(lax.rem(me + 1 + i, count)))

    def arrived(slot, sem):
        pltpu.make_async_copy(slot, slot, sem).wait()

    load_lf.wait()
    for to in range(2):
        cross_copy(to).start()
    others(half_n, half_me, lambda to: half_copy(to).start())
    others(pair_n, pair_me, lambda to: ids_copy(to).start())
    pltpu.make_async_copy(ids_mine, ids_in.at[pair_me], ids_recv).start()
    pltpu.make_async_copy(lf_raw.at[:, chunk(c_me, cw)], lf_in.at[y_me, z_me, c_me], half_recv).start()
    load_cot.wait()
    pltpu.make_async_copy(cot_columns(pair_me), cot_in.at[pair_me], cot_recv).start()
    others(pair_n, pair_me, lambda to: cot_copy(to).start())
    arrived(lf_in.at[1 - y_me, z_me], cross_recv)
    others(ring_n, z_me, lambda to: relay_copy(to).start())

    loads[0].wait()
    loads[1].wait()
    vocab_lane = lax.broadcasted_iota(jnp.int32, (block, LANES), 1).astype(F32)

    def phase_lookup():
        def lookup(i):
            rows = [jnp.broadcast_to(ids_in[4 * i + k, 0:1, :], (block, block)) for k in range(4)]
            columns = [jnp.transpose(row) for row in rows]
            for k in range(4):
                for q in range(vocab // LANES):
                    onehot[chunk(4 * i + k, block), q * LANES : (q + 1) * LANES] = (
                        (columns[k] == vocab_lane + float(q * LANES)).astype(F32).astype(BF)
                    )

        arrived(ids_in, ids_recv)
        loop(pair_n // 4, lookup)

    def phase_embed():
        def embed(i):
            rows = dot(onehot[chunk(i, 4 * block), :], emb[...])
            for q in range(4):
                s, p = lax.div(4 * i + q, ctx_n), lax.rem(4 * i + q, ctx_n)
                for j in range(4):
                    x[s, j, chunk(p, bs), :] = rows[q * block + j * bs : q * block + (j + 1) * bs]

        loop(pair_n // 4, embed)

    phase_lookup()
    phase_embed()

    row16 = lax.broadcasted_iota(jnp.int32, (bs, LANES), 0)
    def phase_short():
        for h in halves:
            f = [[taps[r, i : i + 1, h] for i in range(3)] for r in range(3)]

            def short(s, h=h, f=f):
                def step(p, carry):
                    rows = chunk(p, bs)
                    xs = [x[s, j, rows, h] for j in range(4)]
                    turned = [pltpu.roll(xs[2], 1, 0), pltpu.roll(xs[3], 1, 0)]
                    late = [jnp.where(row16 == 0, carry[q], turned[q]) for q in range(2)]
                    line = late + xs
                    us = [
                        [f[r][0] * line[j + 2] + f[r][1] * line[j + 1] + f[r][2] * line[j] for j in range(4)]
                        for r in range(3)
                    ]
                    for j in range(4):
                        uq[s, j, rows, h] = us[0][j]
                        uk[s, j, rows, h] = us[1][j]
                        uv[s, j, rows, h] = us[2][j]
                        field[s, j, rows, h] = (us[1][j] * us[2][j]).astype(BF)
                    return tuple(turned)

                zero = jnp.zeros((bs, LANES), F32)
                lax.fori_loop(0, ctx_n, step, (zero, zero))

            loop(2, short)

    phase_short()

    loads[2].wait()

    def field_dft(i):
        s, j = lax.div(i, 4), lax.rem(i, 4)
        pbuf[s, j] = dot(fwd[j], field[s, j])

    def phase_field_dft():
        loop(8, field_dft, 4)

    phase_field_dft()

    vocab_row = lax.broadcasted_iota(jnp.int32, (vocab, block), 0).astype(F32)

    def phase_lookup_rows():
        def lookup(i):
            lookups[:, chunk(i, block)] = (vocab_row == ids_in[i, 0:1, :]).astype(F32).astype(BF)

        loop(pair_n, lookup)

    phase_lookup_rows()


    def phase_taps():
        def gather_taps(i):
            outs = []
            for k in range(unroll_n):
                pieces = [(unroll_n * i + k) * per + q for q in range(per)]
                rows = [lf_in[lax.div(d, 2 * ring_n), lax.rem(lax.div(d, 2), ring_n), lax.rem(d, 2)] for d in pieces]
                outs.append(dot(perm[0], jnp.concatenate(rows, 0)).astype(BF))
            for k in range(unroll_n):
                for j in range(4):
                    hfield[j, chunk(unroll_n * i + k, bs), :] = outs[k][j * bs : (j + 1) * bs]

        arrived(lf_in.at[y_me], half_recv)
        arrived(lf_in.at[1 - y_me, pl.ds(0, ring_n - 1)], relay_recv)
        loop(ctx_n // unroll_n, gather_taps)

    phase_taps()

    def filter_dft(j):
        hbuf[j] = dot(fwd[j], hfield[j])

    def phase_filter_dft():
        loop(4, filter_dft, 4)

    phase_filter_dft()

    def butterfly(ref, i, h):
        re = [ref[j, chunk(i, KC), h] for j in range(4)]
        im = [ref[j, pl.ds(pl.multiple_of(sub + i * KC, KC), KC), h] for j in range(4)]
        return radix4(re, im, -1)

    def filter_mix(i):
        for h in halves:
            re, im = butterfly(hbuf, i, h)
            for m in range(4):
                spec_h[m, 0, chunk(i, KC), h] = re[m]
                spec_h[m, 1, chunk(i, KC), h] = im[m]

    def phase_filter_mix():
        loop(sub // KC, filter_mix)

    phase_filter_mix()

    def put(ref, i, h, re, im):
        re, im = radix4(re, im, 1)
        for j in range(4):
            ref[j, chunk(i, KC), h] = re[j].astype(BF)
            ref[j, pl.ds(pl.multiple_of(sub + i * KC, KC), KC), h] = im[j].astype(BF)


    loads[3].wait()

    for s in range(2):

        def conv_mix(i, s=s):
            for h in halves:
                re, im = butterfly(pbuf.at[s], i, h)
                out_re, out_im = [], []
                for m in range(4):
                    spec_z[s, m, 0, chunk(i, KC), h] = re[m]
                    spec_z[s, m, 1, chunk(i, KC), h] = im[m]
                    h_re, h_im = spec_h[m, 0, chunk(i, KC), h], spec_h[m, 1, chunk(i, KC), h]
                    out_re.append(re[m] * h_re - im[m] * h_im)
                    out_im.append(re[m] * h_im + im[m] * h_re)
                put(wbuf.at[s], i, h, out_re, out_im)

        def phase_conv_mix():
            loop(sub // KC, conv_mix)

        phase_conv_mix()

        def conv_idft(j, s=s):
            conv[s, j] = dot(inv[j], wbuf[s, j]).astype(BF).astype(F32)

        def phase_conv_idft():
            loop(4, conv_idft, 4)

        phase_conv_idft()

        def mix(i, s=s):
            outs = []
            for k in range(unroll_n):
                rows = chunk(unroll_n * i + k, bs)
                pieces = [
                    (uq[s, j, rows, :] * conv[s, j, rows, :]).astype(BF) for j in range(4)
                ]
                outs.append(dot(perm[1], jnp.concatenate(pieces, 0)).astype(BF))
            for k in range(unroll_n):
                mixed_out[s * ctx_n + unroll_n * i + k] = outs[k]

        def phase_mix():
            loop(ctx_n // unroll_n, mix)

        phase_mix()

    others(pair_n, pair_me, lambda to: mix_copy(to).start())
    pltpu.make_async_copy(mixed_out.at[pair_me], mixed_hbm.at[0, :, pl.ds(first, cw)], mix_recv).start()

    def take(i):
        outs = [dot(perm[0], cot_in[4 * i + k]) for k in range(4)]
        for k in range(4):
            s, p = lax.div(4 * i + k, ctx_n), lax.rem(4 * i + k, ctx_n)
            rows = chunk(p, bs)
            for j in range(4):
                piece = outs[k][j * bs : (j + 1) * bs]
                field[s, j, rows, :] = (piece * uq[s, j, rows, :]).astype(BF)
                gq[s, j, rows, :] = piece * conv[s, j, rows, :]

    def phase_take():
        arrived(cot_in, cot_recv)
        loop(pair_n // 4, take)

    phase_take()
    phase_field_dft()

    def back_mix(i):
        for h in halves:
            sum_re, sum_im = None, None
            for s in range(2):
                re, im = butterfly(pbuf.at[s], i, h)
                out_re, out_im, f_re, f_im = [], [], [], []
                for m in range(4):
                    h_re, h_im = spec_h[m, 0, chunk(i, KC), h], spec_h[m, 1, chunk(i, KC), h]
                    z_re, z_im = spec_z[s, m, 0, chunk(i, KC), h], spec_z[s, m, 1, chunk(i, KC), h]
                    out_re.append(re[m] * h_re + im[m] * h_im)
                    out_im.append(im[m] * h_re - re[m] * h_im)
                    f_re.append(re[m] * z_re + im[m] * z_im)
                    f_im.append(im[m] * z_re - re[m] * z_im)
                put(wbuf.at[s], i, h, out_re, out_im)
                if s == 0:
                    sum_re, sum_im = f_re, f_im
                else:
                    sum_re = [a + b for a, b in zip(sum_re, f_re)]
                    sum_im = [a + b for a, b in zip(sum_im, f_im)]
            put(wf, i, h, sum_re, sum_im)

    def phase_back_mix():
        loop(sub // KC, back_mix)

    phase_back_mix()

    def filter_idft(j):
        hfield[j] = dot(inv[j], wf[j]).astype(BF)

    def phase_filter_idft():
        loop(4, filter_idft, 4)

    phase_filter_idft()

    def filter_rows(i):
        outs = []
        for k in range(unroll_n):
            rows = jnp.concatenate([hfield[j, chunk(unroll_n * i + k, bs), :] for j in range(4)], 0)
            outs.append(dot(perm[1], rows).astype(BF))
        for k in range(unroll_n):
            for q in range(per):
                d = (unroll_n * i + k) * per + q
                gf_out[d] = outs[k][q * lr : (q + 1) * lr]

    def phase_filter_rows():
        loop(ctx_n // unroll_n, filter_rows)

    phase_filter_rows()
    others(dp_n, dp, lambda to: gf_copy(to).start())
    pltpu.make_async_copy(gf_out.at[dp], gf_in.at[dp], gf_recv).start()

    def owner_sum(arrivals, sems, result):
        arrived(arrivals, sems)
        for c in range(2):
            total = arrivals[c].astype(F32)
            for i in range(1, dp_n // 2):
                total = total + arrivals[2 * i + c].astype(F32)
            result[:, c * cw : (c + 1) * cw] = total

    def gz_idft(i):
        s, j = lax.div(i, 4), lax.rem(i, 4)
        conv[s, j] = dot(inv[j], wbuf[s, j])

    def phase_gz_idft():
        loop(8, gz_idft, 4)

    phase_gz_idft()

    def phase_grad():
        for h in halves:
            f = [[taps[r, i : i + 1, h] for i in range(3)] for r in range(3)]

            def grad(s, h=h, f=f):
                def step(i, carry):
                    p = ctx_n - 1 - i
                    rows = chunk(p, bs)
                    lines = [[], [], []]
                    for j in range(4):
                        gz = conv[s, j, rows, h].astype(BF).astype(F32)
                        gs = [
                        gq[s, j, rows, h],
                        gz * uv[s, j, rows, h],
                        gz * uk[s, j, rows, h],
                    ]
                        for tap in range(3):
                            lines[tap].append(f[0][tap] * gs[0] + f[1][tap] * gs[1] + f[2][tap] * gs[2])
                    turned = [pltpu.roll(v, bs - 1, 0) for v in (lines[1][0], lines[2][0], lines[2][1])]
                    early = [jnp.where(row16 == bs - 1, carry[q], turned[q]) for q in range(3)]
                    once = lines[1][1:] + [early[0]]
                    twice = lines[2][2:] + [early[1], early[2]]
                    for j in range(4):
                        gx[s, p, j, :, h] = (lines[0][j] + once[j] + twice[j]).astype(BF)
                    return tuple(turned)

                zero = jnp.zeros((bs, LANES), F32)
                lax.fori_loop(0, ctx_n, step, (zero, zero, zero))

            loop(2, grad)

    phase_grad()

    def phase_scatter():
        ge_out[...] = dot(lookups[...], gx[...].reshape(pair_n * block, cw)).astype(BF).reshape(ge_out.shape)

    phase_scatter()
    others(dp_n, dp, lambda to: ge_copy(to).start())
    pltpu.make_async_copy(ge_out.at[dp], ge_in.at[dp], ge_recv).start()

    owner_sum(gf_in, gf_recv, gf_ref)
    owner_sum(ge_in, ge_recv, ge_ref)

    def sent(ref, sem):
        pltpu.make_async_copy(ref, ref, sem).wait()

    sent(ids_in.at[pl.ds(0, pair_n - 1)], ids_send)
    sent(lf_in.at[:, 0, 0], cross_send)
    sent(gf_in.at[pl.ds(0, half_n - 1)], half_send)
    sent(lf_in.at[0, pl.ds(0, ring_n - 1)], relay_send)
    sent(cot_in.at[pl.ds(0, pair_n - 1)], cot_send)
    sent(gf_in.at[pl.ds(0, dp_n - 1)], gf_send)
    sent(ge_in.at[pl.ds(0, dp_n - 1)], ge_send)
    sent(mixed_out.at[pl.ds(0, pair_n - 1)], mix_send)
    arrived(mixed_hbm.at[0], mix_recv)


def collect(mixed_raw, ge_raw, gf_raw, mixed, ge, gf, mixed_vmem, ge_vmem, gf_vmem, in_sem, out_sem):
    rows = mixed.shape[1] // 4
    moves = [[ref.at[:, pl.ds(i * rows, rows)] for ref in (mixed_raw, mixed_vmem, mixed)] for i in range(4)]
    moves += [[ge_raw, ge_vmem, ge], [gf_raw, gf_vmem, gf]]
    ins = [pltpu.make_async_copy(a, b, in_sem.at[i]) for i, (a, b, _) in enumerate(moves)]
    outs = [pltpu.make_async_copy(b, c, out_sem.at[i]) for i, (_, b, c) in enumerate(moves)]
    for load in ins:
        load.start()
    for load, store in zip(ins, outs):
        load.wait()
        store.start()
    for store in outs:
        store.wait()


def body(token_ids, embedding, short_filter, long_filter, cotangent):
    vocab, width = embedding.shape
    dp_n, ctx_n = lax.axis_size("dp"), lax.axis_size("ctx")
    part = width // ctx_n
    block = token_ids.shape[1]
    length = block * ctx_n
    cw, sub, bs, pair_n = part // 2, length // 4, block // 4, 2 * ctx_n
    lr, vr, ring_n = length // dp_n, vocab // dp_n, dp_n // 4
    fwd, inv = tables(length)
    hbm = pl.BlockSpec(memory_space=pl.ANY)
    vmem = pl.BlockSpec(memory_space=pltpu.VMEM)
    dma = pltpu.SemaphoreType.DMA
    results = pl.pallas_call(
        functools.partial(kernel, (dp_n, ctx_n, vocab, part, block)),
        out_shape=[
            jax.ShapeDtypeStruct((1, block, width), BF),
            jax.ShapeDtypeStruct((vr, part), F32),
            jax.ShapeDtypeStruct((lr, part), F32),
        ],
        in_specs=[hbm, hbm, hbm, hbm, hbm, hbm, hbm],
        out_specs=[hbm, vmem, vmem],
        scratch_shapes=[
            pltpu.VMEM((1, block), jnp.int32),
            pltpu.VMEM((8, block), F32),
            pltpu.VMEM((pair_n, 8, block), F32),
            pltpu.VMEM((2, block, block), BF),
            pltpu.VMEM((vocab, cw), BF),
            pltpu.VMEM((3, 3, cw), F32),
            pltpu.VMEM((2, ring_n, 2, lr, cw), BF),
            pltpu.VMEM((pair_n, block, cw), BF),
            pltpu.VMEM(fwd.shape, BF),
            pltpu.VMEM(inv.shape, BF),
            pltpu.VMEM((2, 4, sub, cw), F32),
            pltpu.VMEM((2, 4, sub, cw), F32),
            pltpu.VMEM((2, 4, sub, cw), F32),
            pltpu.VMEM((2, 4, sub, cw), F32),
            pltpu.VMEM((2, 4, sub, cw), BF),
            pltpu.VMEM((4, sub, cw), BF),
            pltpu.VMEM((4, 2, sub, cw), F32),
            pltpu.VMEM((2, 4, 2, sub, cw), F32),
            pltpu.VMEM((4, 2 * sub, cw), F32),
            pltpu.VMEM((2, 4, 2 * sub, cw), F32),
            pltpu.VMEM((2, 4, 2 * sub, cw), BF),
            pltpu.VMEM((4, 2 * sub, cw), BF),
            pltpu.VMEM((2, 4, sub, cw), F32),
            pltpu.VMEM((2, 4, sub, cw), F32),
            pltpu.VMEM((2, ctx_n, 4, bs, cw), BF),
            pltpu.VMEM((pair_n * block, vocab), BF),
            pltpu.VMEM((vocab, pair_n * block), BF),
            pltpu.VMEM((pair_n, block, cw), BF),
            pltpu.VMEM((dp_n, lr, cw), BF),
            pltpu.VMEM((dp_n, lr, cw), BF),
            pltpu.VMEM((dp_n, vr, cw), BF),
            pltpu.VMEM((dp_n, vr, cw), BF),
            pltpu.VMEM((lr, part), BF),
            pltpu.VMEM((block, width), BF),
            dma((7,)),
        ] + [dma] * 16,
        compiler_params=pltpu.CompilerParams(
            collective_id=0, has_side_effects=True, vmem_limit_bytes=56 * 1024 * 1024
        ),
        name="hyena",
    )(token_ids, embedding, short_filter, long_filter, cotangent, fwd, inv)
    return pl.pallas_call(
        collect,
        out_shape=[jax.ShapeDtypeStruct(r.shape, r.dtype) for r in results],
        in_specs=[hbm] * 3,
        out_specs=[hbm] * 3,
        scratch_shapes=[pltpu.VMEM(r.shape, r.dtype) for r in results] + [dma((6,)), dma((6,))],
        compiler_params=pltpu.CompilerParams(vmem_limit_bytes=56 * 1024 * 1024),
        name="collect",
    )(*results)


def solution(mesh):
    in_specs = (P("dp", "ctx"), P(), P(), P("dp", "ctx"), P("dp", "ctx", None))
    out_specs = (P("dp", "ctx", None), P("dp", "ctx"), P("dp", "ctx"))
    return jax.shard_map(body, mesh=mesh, in_specs=in_specs, out_specs=out_specs, check_vma=False)
```
